128 devices in a mesh: dp: 8 (over x, y_lo), shard: 16 (over y_hi, z, core).
Axes of the slice: x: 4, y: 4 (y_hi: 2, y_lo: 2; y = y_hi * 2 + y_lo), z: 4, core: 2. Of those that a mesh axis runs over, the one named last changes fastest.
Arguments:
- tokens: bfloat16 [2, 16, 1024, 1024], P(None, 'shard', 'dp'), may hold values from -6 to 6
- cotangent: bfloat16 [2, 16, 1024, 1024], P(None, 'shard', 'dp'), may hold values from -6 to 6
- seq_lengths: int32 [2, 16, 16], P(None, 'shard'), may hold values from 16 to 192, as said below
- block_offsets: int32 [2, 16, 16], P(None, 'shard'), may hold values from 0 to 240, as said below
- deal_order: int32 [2, 16, 16], P(None, 'shard'), may hold values from 0 to 15, as said below
- w_query: bfloat16 [1024, 1024], P(('dp', 'shard')), may hold values from -0.25 to 0.25
- w_key: bfloat16 [1024, 1024], P(('dp', 'shard')), may hold values from -0.25 to 0.25
- w_value: bfloat16 [1024, 1024], P(('dp', 'shard')), may hold values from -0.1875 to 0.1875
- w_output: bfloat16 [1024, 1024], P(('dp', 'shard')), may hold values from -0.5 to 0.5
- b_query: bfloat16 [1024], P(('dp', 'shard')), may hold values from -3 to 3
- b_value: bfloat16 [1024], P(('dp', 'shard')), may hold values from -3 to 3
- b_output: bfloat16 [1024], P(('dp', 'shard')), may hold values from -3 to 3
- gain_one: bfloat16 [1024], P(('dp', 'shard')), may hold values from 0.25 to 1.75
- shift_one: bfloat16 [1024], P(('dp', 'shard')), may hold values from -3 to 3
- w_inner: bfloat16 [1024, 4096], P(('dp', 'shard')), may hold values from -0.1875 to 0.1875
- b_inner: bfloat16 [4096], P(('dp', 'shard')), may hold values from -3 to 3
- w_outer: bfloat16 [4096, 1024], P(('dp', 'shard')), may hold values from -0.09375 to 0.09375
- b_outer: bfloat16 [1024], P(('dp', 'shard')), may hold values from -3 to 3
- gain_two: bfloat16 [1024], P(('dp', 'shard')), may hold values from 0.25 to 1.75
- shift_two: bfloat16 [1024], P(('dp', 'shard')), may hold values from -3 to 3
Outputs:
- output: bfloat16 [2, 16, 1024, 1024], P(None, 'shard', 'dp')
- token_grad: bfloat16 [2, 16, 1024, 1024], P(None, 'shard', 'dp')
- grad_w_query: float32 [1024, 1024], P(('dp', 'shard'))
- grad_w_key: float32 [1024, 1024], P(('dp', 'shard'))
- grad_w_value: float32 [1024, 1024], P(('dp', 'shard'))
- grad_w_output: float32 [1024, 1024], P(('dp', 'shard'))
- grad_b_query: float32 [1024], P(('dp', 'shard'))
- grad_b_value: float32 [1024], P(('dp', 'shard'))
- grad_b_output: float32 [1024], P(('dp', 'shard'))
- grad_gain_one: float32 [1024], P(('dp', 'shard'))
- grad_shift_one: float32 [1024], P(('dp', 'shard'))
- grad_w_inner: float32 [1024, 4096], P(('dp', 'shard'))
- grad_b_inner: float32 [4096], P(('dp', 'shard'))
- grad_w_outer: float32 [4096, 1024], P(('dp', 'shard'))
- grad_b_outer: float32 [1024], P(('dp', 'shard'))
- grad_gain_two: float32 [1024], P(('dp', 'shard'))
- grad_shift_two: float32 [1024], P(('dp', 'shard'))
The draws below stay inside these ranges and needn't reach their ends.
Inputs may be any that keep to these rules, and one draw needn't show every extreme that they name: `seq_lengths`: the sequences 2 d and 2 d + 1 of a group belong to block d; their lengths sum to at most 256, all lengths of a group sum to 1024, and in every group one block holds exactly 256 tokens. block_offsets[2 d + 1] = block_offsets[2 d] + seq_lengths[2 d] and block_offsets[2 d + 1] + seq_lengths[2 d + 1] <= 256. Each group's deal_order is a permutation of its sequences.
All inputs are finite; a program needn't handle non-finite values.
Results may differ from the reference program's by a relative error of at most 0.015.
Values may be sent and summed in bfloat16 or wider, within the bound.
A program may use at most 320 MiB of HBM per device.

```python
import math
import jax
import jax.numpy as jnp
from jax import lax

D = 1024
HEADS = 16
FF = 4096
TOK_DEV = 128
MICRO = 2
GROUPS = 16
GROUP_TOK = 1024
BLOCK = 256
SEQS_G = 16


def deal_tables(key):
    device_count = SEQS_G // 2
    half_tok = TOK_DEV // 2

    def one_group(group_key):
        sub_keys = jax.random.split(group_key, 5)
        shift_amount = jax.random.randint(sub_keys[0], ((device_count - 4) // 2,), 0, half_tok + 1)
        paired = jnp.stack([TOK_DEV + shift_amount, TOK_DEV - shift_amount], axis=1).reshape(-1)
        role_loads = jnp.concatenate([jnp.array([2 * TOK_DEV, half_tok, half_tok, TOK_DEV], jnp.int32), paired.astype(jnp.int32)])
        shuffle = jax.random.permutation(sub_keys[1], device_count)
        device_loads = jnp.zeros((device_count,), jnp.int32).at[shuffle].set(role_loads)
        pushed = jnp.zeros((device_count,), jnp.int32).at[shuffle[1]].set(1) == 1
        lower_len = (device_loads + 3) // 4
        upper_len = 3 * device_loads // 4
        first_len = jax.random.randint(sub_keys[2], (device_count,), lower_len, upper_len + 1)
        first_len = jnp.where(pushed, upper_len, first_len)
        first_len = jnp.where(device_loads == 2 * TOK_DEV, 3 * TOK_DEV // 2, first_len).astype(jnp.int32)
        lengths_all = jnp.stack([first_len, device_loads - first_len], axis=1).reshape(-1)
        first_offset = jax.random.randint(sub_keys[3], (device_count,), 0, 2 * TOK_DEV - device_loads + 1)
        first_offset = jnp.where(pushed, 2 * TOK_DEV - device_loads, first_offset).astype(jnp.int32)
        offsets_all = jnp.stack([first_offset, first_offset + first_len], axis=1).reshape(-1)
        deal_seq = jax.random.permutation(sub_keys[4], 2 * device_count)
        return (lengths_all.astype(jnp.int32), offsets_all.astype(jnp.int32), deal_seq.astype(jnp.int32))
    group_keys = jax.random.split(key, MICRO * GROUPS)
    lengths_all, offsets_all, deal_seq = jax.vmap(one_group)(group_keys)
    shape_out = (MICRO, GROUPS, SEQS_G)
    return (lengths_all.reshape(shape_out), offsets_all.reshape(shape_out), deal_seq.reshape(shape_out))


def draw_seq_lengths(key, part):
    tables = deal_tables(key)
    return tables[0]


def draw_block_offsets(key, part):
    tables = deal_tables(key)
    return tables[1]


def draw_deal_order(key, part):
    tables = deal_tables(key)
    return tables[2]


def level_of(rng, shape, pieces, least, top_value):
    level, own = 1.0, jax.random.fold_in(rng, 6)
    for dim, shards_of in pieces:
        draws = jnp.exp(jax.random.uniform(jax.random.fold_in(own, dim), (shards_of,), jnp.float32, least / len(pieces), top_value / len(pieces)))
        level = level * jnp.repeat(draws, shape[dim] // shards_of).reshape([-1 if axis == dim else 1 for axis in range(len(shape))])
    return level


def normal_values(stream_key, dims, spread, limit, cuts=(), kind=jnp.bfloat16):
    drawn = spread * jax.random.normal(stream_key, dims, jnp.float32)
    if cuts:
        drawn = drawn * level_of(stream_key, dims, cuts, -0.22, 0.18)
    return jnp.clip(drawn, -limit, limit).astype(kind)


def setup_inputs(seed: int = 0) -> dict:
    arg_keys = jax.random.split(jax.random.key(seed), 21)
    tokens = normal_values(arg_keys[0], (MICRO, GROUPS, GROUP_TOK, D), 1.0, 6.0, ((1, 16), (2, 8)))
    cotangent = normal_values(arg_keys[1], (MICRO, GROUPS, GROUP_TOK, D), 1.0, 6.0, ((1, 16), (2, 8)))
    seq_lengths = draw_seq_lengths(jax.random.fold_in(arg_keys[20], 71), 0)
    block_offsets = draw_block_offsets(jax.random.fold_in(arg_keys[20], 71), 0)
    deal_order = draw_deal_order(jax.random.fold_in(arg_keys[20], 71), 0)
    w_query = normal_values(arg_keys[5], (D, D), (D // 2) ** -0.5, 0.25, ((0, 128),))
    w_key = normal_values(arg_keys[6], (D, D), (D // 2) ** -0.5, 0.25, ((0, 128),))
    w_value = normal_values(arg_keys[7], (D, D), D ** -0.5, 0.1875, ((0, 128),))
    w_output = normal_values(arg_keys[8], (D, D), (D // 8) ** -0.5, 0.5, ((0, 128),))
    b_query = normal_values(arg_keys[9], (D,), 0.5, 3.0, ((0, 128),))
    b_value = normal_values(arg_keys[10], (D,), 0.5, 3.0, ((0, 128),))
    b_output = normal_values(arg_keys[11], (D,), 0.5, 3.0, ((0, 128),))
    gain_one = jnp.clip(1.0 + 0.15 * jax.random.normal(arg_keys[12], (D,), jnp.float32), 0.25, 1.75).astype(jnp.bfloat16)
    shift_one = normal_values(arg_keys[13], (D,), 0.5, 3.0, ((0, 128),))
    w_inner = normal_values(arg_keys[14], (D, FF), D ** -0.5, 0.1875, ((0, 128),))
    b_inner = normal_values(arg_keys[15], (FF,), 0.5, 3.0, ((0, 128),))
    w_outer = normal_values(arg_keys[16], (FF, D), FF ** -0.5, 0.09375, ((0, 128),))
    b_outer = normal_values(arg_keys[17], (D,), 0.5, 3.0, ((0, 128),))
    gain_two = jnp.clip(1.0 + 0.15 * jax.random.normal(arg_keys[18], (D,), jnp.float32), 0.25, 1.75).astype(jnp.bfloat16)
    shift_two = normal_values(arg_keys[19], (D,), 0.5, 3.0, ((0, 128),))
    return {"tokens": tokens, "cotangent": cotangent, "seq_lengths": seq_lengths, "block_offsets": block_offsets, "deal_order": deal_order, "w_query": w_query, "w_key": w_key, "w_value": w_value, "w_output": w_output, "b_query": b_query, "b_value": b_value, "b_output": b_output, "gain_one": gain_one, "shift_one": shift_one, "w_inner": w_inner, "b_inner": b_inner, "w_outer": w_outer, "b_outer": b_outer, "gain_two": gain_two, "shift_two": shift_two}


@jax.custom_vjp
def low(v):
    return lax.optimization_barrier(v.astype(jnp.bfloat16)).astype(jnp.float32)

@jax.custom_vjp
def low_back(v):
    return v

def low_keep(v):
    return (low(v), None)

def low_pass(kept, grad):
    return (grad,)

def back_keep(v):
    return (v, None)

def back_low(kept, grad):
    return (low(grad),)
low.defvjp(low_keep, low_pass)
low_back.defvjp(back_keep, back_low)
norm_eps = 1e-05
masked_fill = -1e+30

def matmul(left, right):
    return jnp.dot(left, right, precision=lax.Precision.HIGHEST)

def layer_norm(row_block, gain, shift):
    row_mean = lax.optimization_barrier(jnp.mean(row_block, axis=-1, keepdims=True))
    centred = row_block - row_mean
    variance = lax.optimization_barrier(jnp.mean(centred * centred, axis=-1, keepdims=True))
    return centred * lax.rsqrt(variance + norm_eps) * gain + shift

def route_tables(group_lengths, group_order):
    seq_count = group_order.shape[0]
    ordered = jnp.take(group_lengths, group_order).astype(jnp.int32)
    starts = (jnp.cumsum(ordered) - ordered).astype(jnp.int32)
    picked = group_order[:, None] == jnp.arange(seq_count).astype(jnp.int32)[None, :]
    anchor = lax.optimization_barrier(jnp.sum(jnp.where(picked, starts[:, None], 0), axis=0)).astype(jnp.int32)
    return (ordered, starts, anchor)

def device_rows(group_lengths, group_offsets, anchor, device, block_rows):
    positions = jnp.arange(block_rows).astype(jnp.int32)
    pair_ids = (2 * device + jnp.arange(2).astype(jnp.int32)).astype(jnp.int32)
    first_row = jnp.take(group_offsets, pair_ids)
    counts = jnp.take(group_lengths, pair_ids)
    source_begin = jnp.take(anchor, pair_ids)
    inside = (positions[None, :] >= first_row[:, None]) & (positions[None, :] < (first_row + counts)[:, None])
    segment = lax.optimization_barrier(jnp.max(jnp.where(inside, pair_ids[:, None], -1), axis=0)).astype(jnp.int32)
    source = lax.optimization_barrier(jnp.sum(jnp.where(inside, source_begin[:, None] + positions[None, :] - first_row[:, None], 0), axis=0)).astype(jnp.int32)
    return (segment, source, jnp.any(inside, axis=0))

def return_index(ordered, starts, group_offsets, group_order, positions, block_rows):
    inside = (positions[:, None] >= starts[None, :]) & (positions[:, None] < (starts + ordered)[None, :])
    target = group_order // 2 * block_rows + jnp.take(group_offsets, group_order)
    target = target[None, :] + positions[:, None] - starts[None, :]
    return lax.optimization_barrier(jnp.sum(jnp.where(inside, target, 0), axis=1)).astype(jnp.int32)

def encode_block(row_block, segment, params):
    w_query, w_key, w_value, w_output, b_query, b_value, b_output, gain_one, shift_one, w_inner, b_inner, w_outer, b_outer, gain_two, shift_two = params
    row_count = row_block.shape[0]
    head_dim = D // HEADS
    score_scale = 1.0 / math.sqrt(head_dim)
    queries = low(low_back(matmul(row_block, w_query) + b_query)).reshape(row_count, HEADS, head_dim)
    key_rows = low(low_back(matmul(row_block, w_key))).reshape(row_count, HEADS, head_dim)
    value_rows = low(low_back(matmul(row_block, w_value) + b_value)).reshape(row_count, HEADS, head_dim)
    raw_scores = low_back(jnp.einsum('qhd,khd->hqk', queries, key_rows, precision=lax.Precision.HIGHEST))
    same_seq = (segment[:, None] == segment[None, :])[None]
    scores = jnp.where(same_seq, raw_scores * score_scale, masked_fill)
    highest = lax.optimization_barrier(jnp.max(scores, axis=-1, keepdims=True))
    exp_terms = jnp.exp(scores - highest)
    attn_probs = exp_terms / lax.optimization_barrier(jnp.sum(exp_terms, axis=-1, keepdims=True))
    mixed_heads = jnp.einsum('hqk,khd->qhd', low(attn_probs), value_rows, precision=lax.Precision.HIGHEST)
    context = low(low_back(mixed_heads.reshape(row_count, D)))
    attended = row_block + low_back(matmul(context, w_output) + b_output)
    normed = layer_norm(attended, gain_one, shift_one)
    inner_pre = low_back(matmul(low(normed), w_inner) + b_inner)
    activated = low(jax.nn.gelu(inner_pre, approximate=False))
    outer_out = low_back(matmul(activated, w_outer) + b_outer)
    return layer_norm(normed + outer_out, gain_two, shift_two)

def reference(tokens, cotangent, seq_lengths, block_offsets, deal_order, w_query, w_key, w_value, w_output, b_query, b_value, b_output, gain_one, shift_one, w_inner, b_inner, w_outer, b_outer, gain_two, shift_two):
    params = (w_query.astype(jnp.float32), w_key.astype(jnp.float32), w_value.astype(jnp.float32), w_output.astype(jnp.float32), b_query.astype(jnp.float32), b_value.astype(jnp.float32), b_output.astype(jnp.float32), gain_one.astype(jnp.float32), shift_one.astype(jnp.float32), w_inner.astype(jnp.float32), b_inner.astype(jnp.float32), w_outer.astype(jnp.float32), b_outer.astype(jnp.float32), gain_two.astype(jnp.float32), shift_two.astype(jnp.float32))
    flat_lengths = seq_lengths.reshape(MICRO * GROUPS, SEQS_G)
    flat_offsets = block_offsets.reshape(MICRO * GROUPS, SEQS_G)
    flat_order = deal_order.reshape(MICRO * GROUPS, SEQS_G)

    def whole(stream, weights_all):

        def block_pass(row_block, segment):
            return encode_block(row_block, segment, weights_all)
        checked = jax.checkpoint(block_pass)

        def group_pass(items):
            stream_rows, group_lengths, group_offsets, group_order = items
            ordered, starts, anchor = route_tables(group_lengths, group_order)

            def device_block(device):
                segment, source, valid = device_rows(group_lengths, group_offsets, anchor, device, BLOCK)
                taken = jnp.take(stream_rows, source, axis=0)
                return (jnp.where(valid[:, None], taken, jnp.zeros_like(taken)), segment)
            blocks, segments = jax.vmap(device_block)(jnp.arange(SEQS_G // 2).astype(jnp.int32))
            encoded = lax.map(lambda block_pair: checked(block_pair[0], block_pair[1]), (blocks, segments))
            positions = jnp.arange(GROUP_TOK).astype(jnp.int32)
            target = return_index(ordered, starts, group_offsets, group_order, positions, BLOCK)
            return jnp.take(encoded.reshape(-1, D), target, axis=0)
        flat_stream = stream.reshape(MICRO * GROUPS, GROUP_TOK, D)
        results = lax.map(group_pass, (flat_stream, flat_lengths, flat_offsets, flat_order))
        return results.reshape(stream.shape)
    result, pullback = jax.vjp(whole, tokens.astype(jnp.float32), params)
    token_grad, weight_grads = pullback(cotangent.astype(jnp.float32))
    return (result.astype(jnp.bfloat16), token_grad.astype(jnp.bfloat16), weight_grads[0], weight_grads[1], weight_grads[2], weight_grads[3], weight_grads[4], weight_grads[5], weight_grads[6], weight_grads[7], weight_grads[8], weight_grads[9], weight_grads[10], weight_grads[11], weight_grads[12], weight_grads[13], weight_grads[14])
```

```python
import math

import jax
import jax.numpy as jnp
from jax import lax
from jax.experimental import pallas as pl
from jax.experimental.pallas import tpu as pltpu
from jax.sharding import PartitionSpec as P

MESH = pl.DeviceIdType.MESH
BF = jnp.bfloat16
F32 = jnp.float32
D = 1024
FF = 4096
HEADS = 16
HEAD = 64
TOK = 128
OWN = 2 * TOK
HALO = 192
WIN = OWN + 2 * HALO
AXES = ("x", "y", "z")
ORDER = (("z", "y", "x"), ("x", "z", "y"), ("y", "x", "z"))
CHIPS = (4, 2, 2, 4)
N_SEM = 200


def position():
    dp, sh = lax.axis_index("dp"), lax.axis_index("shard")
    return {
        "x": lax.div(dp, 2),
        "y": lax.div(sh, 8) * 2 + lax.rem(dp, 2),
        "z": lax.div(lax.rem(sh, 8), 2),
        "c": lax.rem(sh, 2),
    }


def device_at(at):
    return (
        at["x"] * 2 + lax.rem(at["y"], 2),
        lax.div(at["y"], 2) * 8 + at["z"] * 2 + at["c"],
    )


class Net:
    def __init__(self, send_sem, recv_sem):
        self.me = position()
        self.send_sem, self.recv_sem = send_sem, recv_sem
        self.used = 0
        self.sent = []

    def moved(self, axis, by):
        at = dict(self.me)
        if axis == "c":
            at["c"] = 1 - at["c"]
        else:
            at[axis] = lax.rem(at[axis] + by, 4)
        return at

    def ring(self, axis, by):
        return device_at(self.moved(axis, by))

    def pair(self, by, lo):
        at = self.moved("x", by % 4)
        at["y"] = lax.div(at["y"], 2) * 2 + lo
        return device_at(at)

    def slot(self):
        self.used += 1
        return self.used - 1

    def make(self, src, dst, device, send, recv):
        return pltpu.make_async_remote_copy(
            src_ref=src,
            dst_ref=dst,
            send_sem=self.send_sem.at[send],
            recv_sem=self.recv_sem.at[recv],
            device_id=device,
            device_id_type=MESH,
        )

    def copy(self, src, dst, device):
        k = self.slot()
        moved = self.make(src, dst, device, k, k)
        moved.start()
        self.sent.append(moved)
        return moved

    def barrier(self):
        bar = pltpu.get_barrier_semaphore()
        peers = [self.ring("c", 0)] + [self.ring(a, b) for a in AXES for b in (1, 2, 3)]
        other = 1 - lax.rem(self.me["y"], 2)
        peers += [self.pair(1, other), self.pair(3, other)]
        for p in peers:
            pl.semaphore_signal(bar, inc=1, device_id=p, device_id_type=MESH)
        pl.semaphore_wait(bar, len(peers))

    def finish(self):
        for moved in self.sent:
            moved.wait_send()
        assert self.used <= N_SEM, self.used


def chip_index(at, drop=()):
    out = []
    for axis in AXES:
        if axis in drop:
            continue
        v = at[axis]
        if axis == "y":
            if v is None:
                out += [slice(None), slice(None)]
            elif isinstance(v, tuple):
                out += [v[1], slice(None)]
            else:
                out += [lax.rem(v, 2), lax.div(v, 2)]
        elif v is None:
            out.append(slice(None))
        elif isinstance(v, tuple):
            out.append(pl.ds(2 * v[1], 2))
        else:
            out.append(v)
    return tuple(out)


def chip_shape(drop):
    shape = ()
    for axis in AXES:
        if axis not in drop:
            shape += (2, 2) if axis == "y" else (4,)
    return shape


def columns(base, width):
    return pl.ds(pl.multiple_of(base, 128), width)


class Gather:
    def __init__(self, net, ref, rows, cols, order):
        self.net, self.ref, self.rows, self.cols = net, ref, rows, cols
        self.a, self.b, self.e = order

    def at(self, **over):
        place = {k: self.net.me[k] for k in AXES}
        place.update(over)
        return self.ref.at[chip_index(place) + (self.rows, self.cols)]

    def send(self, region, axis, by):
        return self.net.copy(region, region, self.net.ring(axis, by))

    def p1(self):
        self.c = [self.send(self.at(), self.a, d) for d in (1, 3, 2)]

    def p2(self):
        for moved in self.c:
            moved.wait_recv()
        self.c = [self.send(self.at(**{self.a: None}), self.b, d) for d in (1, 3, 2)]

    def part(self, h, by):
        e = self.net.moved(self.e, by)[self.e]
        return self.at(**{self.a: h if h is None else ("half", h), self.b: None, self.e: e})

    def p3(self):
        for moved in self.c:
            moved.wait_recv()
        self.r0 = self.send(self.part(0, 0), self.e, 1)
        self.l1 = self.send(self.part(1, 0), self.e, 3)
        self.r1 = self.send(self.part(1, 0), self.e, 1)
        self.l0 = self.send(self.part(0, 0), self.e, 3)
        self.core = [self.send(self.part(None, 0), "c", 0)]

    def p3_mid(self):
        self.r0.wait_recv()
        self.f0 = self.send(self.part(0, 3), self.e, 1)
        self.l1.wait_recv()
        self.f1 = self.send(self.part(1, 1), self.e, 3)

    def p3_core(self):
        self.r1.wait_recv()
        self.core.append(self.send(self.part(None, 3), "c", 0))
        self.l0.wait_recv()
        self.core.append(self.send(self.part(None, 1), "c", 0))

    def p3_end(self):
        self.f0.wait_recv()
        self.f1.wait_recv()
        self.core.append(self.send(self.part(None, 2), "c", 0))

    def done(self):
        for moved in self.core:
            moved.wait_recv()


def each(lanes, step):
    for lane in lanes:
        getattr(lane, step)()


def pieces(lo):
    at = TOK * lo
    return (
        (1, pl.ds(TOK // 2, TOK // 2), at + TOK // 2 - (OWN - HALO), None),
        (1, pl.ds(0, TOK // 2), at - (OWN - HALO), 1),
        (-1, pl.ds(0, TOK // 2), at + HALO + OWN, None),
        (-1, pl.ds(TOK // 2, TOK // 2), at + TOK // 2 + HALO + OWN, 0),
    )


def rows_at(base, count):
    return pl.ds(pl.multiple_of(base, TOK // 2), count)


class Window:
    def __init__(self, net, tokens, cotangent, window, cots, local_sem):
        self.net = net
        lo = lax.rem(net.me["y"], 2)
        other = 1 - lo
        self.copies = []
        mine = rows_at(HALO + TOK * lo, TOK)
        theirs = rows_at(TOK * lo, TOK)
        self.local = [
            pltpu.make_async_copy(tokens.at[lo], window.at[mine], local_sem.at[0]),
            pltpu.make_async_copy(cotangent.at[lo], cots.at[theirs], local_sem.at[1]),
        ]
        self.pair = [
            (tokens.at[other], window.at[mine]),
            (cotangent.at[other], cots.at[theirs]),
        ]
        self.halo = []
        for by, rows, to, only in pieces(lo):
            first = net.slot()
            second = net.slot()
            for m in range(2):
                send = first if m == 0 else second
                copy = net.make(
                    tokens.at[m, rows], window.at[rows_at(to, TOK // 2)], net.pair(by, m), send, first + lo
                )
                self.halo.append((copy, only))
        self.gets = []
        for k, (by, rows, to, only) in enumerate(pieces(lo)):
            for source in range(2):
                if only is None or only == source:
                    index = 2 * k + source + (net.used - 8)
                    self.gets.append(
                        net.make(tokens.at[0, rows], window.at[pl.ds(0, TOK // 2)], net.pair(1, other), 0, index)
                    )

    def start(self):
        for copy in self.local:
            copy.start()
        lo = lax.rem(self.net.me["y"], 2)
        self.pair = [self.net.copy(s, d, self.net.pair(0, 1 - lo)) for s, d in self.pair]
        for copy, only in self.halo:
            if only is None:
                copy.start()
            else:
                pl.when(lo == only)(copy.start)

    def done(self):
        for copy in self.local:
            copy.wait()
        for copy in self.pair + self.gets:
            copy.wait_recv()

    def finish(self):
        lo = lax.rem(self.net.me["y"], 2)
        for copy, only in self.halo:
            if only is None:
                copy.wait_send()
            else:
                pl.when(lo == only)(copy.wait_send)


def place_own(me, mine, peer, full):
    here = chip_index(me)
    c = me["c"]
    first = c == 0

    def both(a, b):
        return jnp.concatenate([jnp.where(first, a, b), jnp.where(first, b, a)], axis=0)

    half = columns(c * 512, 512)
    for j in range(4):
        r = slice(8 * j, 8 * j + 8)
        full[j][here + (slice(None), half)] = both(mine[r, half], peer[r, half])
    for t in range(2):
        r, s = slice(32 + 8 * t, 40 + 8 * t), slice(48 + 8 * t, 56 + 8 * t)
        a = jnp.where(first, mine[r, :], mine[s, :])
        b = jnp.where(first, peer[r, :], peer[s, :])
        full[4][here + (slice(None), columns(c * 2048 + 1024 * t, 1024))] = both(a, b)
    full[5][here + (slice(None), half)] = both(mine[64:96, half], peer[64:96, half])


def gather_kernel(own, tokens, cotangent, *refs):
    outs, rest = refs[:8], refs[8:]
    mine, peer = rest[:2]
    full = rest[2:8]
    send_sem, recv_sem, local_sem = rest[8:]
    net = Net(send_sem, recv_sem)
    c = net.me["c"]
    load = pltpu.make_async_copy(own, mine, local_sem.at[0])
    load.start()
    net.barrier()
    load.wait()
    swap = net.copy(mine, peer, net.ring("c", 0))
    window = Window(net, tokens, cotangent, outs[6], outs[7], local_sem)
    window.start()
    swap.wait_recv()
    place_own(net.me, mine, peer, full)
    rows = slice(None)
    half = columns(c * 512, 512)
    wi, wu = full[4], full[5]
    first = [Gather(net, full[j], rows, half, ORDER[j]) for j in range(3)]
    second = [
        Gather(net, full[3], rows, half, ORDER[0]),
        Gather(net, wi, rows, columns(c * 2048 + 512, 1024), ORDER[1]),
        Gather(net, wi, rows, columns(c * 2048 + 1536, 512), ORDER[2]),
        Gather(net, wi, rows, columns(c * 2048, 512), ORDER[0]),
    ]
    third = [
        Gather(net, wu, pl.ds(0, 16), half, ORDER[0]),
        Gather(net, wu, pl.ds(16, 16), half, ORDER[1]),
        Gather(net, wu, pl.ds(32, 32), half, ORDER[2]),
    ]
    for step in ("p1", "p2"):
        for lanes in (first, second, third):
            each(lanes, step)
    each(first, "p3")
    each(second, "p3")
    each(first, "p3_mid")
    each(first, "p3_core")
    each(third, "p3")
    each(first, "p3_end")
    each(first, "done")
    for step in ("p3_mid", "p3_core", "p3_end"):
        each(second, step)
    each(third, "p3_mid")
    each(third, "p3_core")
    each(second, "done")
    each(third, "p3_end")
    each(third, "done")
    window.done()
    stores = [pltpu.make_async_copy(w, o, local_sem.at[2 + k]) for k, (w, o) in enumerate(zip(full, outs))]
    for store in stores:
        store.start()
    for store in stores:
        store.wait()
    window.finish()
    net.finish()


BLOCKS = ((16, 1024),) * 4 + ((16, 4096), (64, 1024))


def gather_all(own, tokens, cotangent):
    any_space = pl.BlockSpec(memory_space=pl.ANY)
    full = [CHIPS + s for s in BLOCKS]
    return pl.pallas_call(
        gather_kernel,
        name="gather_all",
        out_shape=[jax.ShapeDtypeStruct(s, BF) for s in full + [(WIN, D), (OWN, D)]],
        in_specs=[any_space] * 3,
        out_specs=[any_space] * 8,
        scratch_shapes=[pltpu.VMEM((96, 1024), BF)] * 2
        + [pltpu.VMEM(s, BF) for s in full]
        + [
            pltpu.SemaphoreType.DMA((N_SEM,)),
            pltpu.SemaphoreType.DMA((N_SEM,)),
            pltpu.SemaphoreType.DMA((8,)),
        ],
        compiler_params=pltpu.CompilerParams(collective_id=1, has_side_effects=True, vmem_limit_bytes=50 << 20),
    )(own, tokens, cotangent)


def add_into(dst, srcs):
    lead = dst.shape[:-2]
    loop = lead[:-1] if len(lead) > 1 else lead
    total = math.prod(loop)

    def body(k, carry):
        index, rest = (), k
        for n in reversed(loop):
            index = (lax.rem(rest, n),) + index
            rest = lax.div(rest, n)
        value = dst[index].astype(F32)
        for s in srcs:
            value = value + s[index].astype(F32)
        dst[index] = value.astype(BF)
        return carry

    lax.fori_loop(0, total, body, 0)


class Reduce:
    def __init__(self, net, ref, rows, base, width, other_base, order, bufs):
        self.net, self.ref, self.rows, self.width = net, ref, rows, width
        self.mine, self.theirs = columns(base, width), columns(other_base, width)
        self.a, self.b, self.e = order
        self.sib, self.wide, self.mid, self.low = bufs

    def at(self, cols=None, **over):
        place = {k: self.net.me[k] for k in AXES}
        place.update(over)
        return self.ref.at[chip_index(place) + (self.rows, self.mine if cols is None else cols)]

    def near(self, by):
        return self.net.moved(self.a, by)[self.a]

    def quarter(self, by, h):
        b = None if h is None else ("half", h)
        return self.at(**{self.a: self.near(by), self.b: b, self.e: None})

    def buf(self, k, h):
        b = None if h is None else ("half", h)
        return self.wide.at[(k,) + chip_index({self.b: b, self.e: None}, drop=(self.a,))]

    def d0(self):
        every = {k: None for k in AXES}
        self.c = self.net.copy(self.at(cols=self.theirs, **every), self.sib, self.net.ring("c", 0))

    def send(self, by, h, k, to):
        return self.net.copy(self.quarter(by, h), self.buf(k, h), self.net.ring(self.a, to))

    def p1(self):
        self.c.wait_recv()
        add_into(self.at(**{k: None for k in AXES}), [self.sib])
        self.m0 = self.send(2, 0, 0, 1)
        self.m1 = self.send(2, 1, 0, 3)
        self.l1 = self.send(1, 1, 1, 1)
        self.r0 = self.send(3, 0, 2, 3)

    def p1_mid(self):
        self.m0.wait_recv()
        add_into(self.quarter(1, 0), [self.buf(0, 0)])
        self.l0 = self.send(1, 0, 1, 1)
        self.m1.wait_recv()
        add_into(self.quarter(3, 1), [self.buf(0, 1)])
        self.r1 = self.send(3, 1, 2, 3)

    def p2(self):
        for moved in (self.l1, self.r0, self.l0, self.r1):
            moved.wait_recv()
        add_into(self.quarter(0, None), [self.buf(1, None), self.buf(2, None)])
        self.c = []
        for k, d in enumerate((1, 3, 2)):
            there = self.net.moved(self.b, d)[self.b]
            self.c.append(
                self.net.copy(self.at(**{self.b: there, self.e: None}), self.mid.at[k], self.net.ring(self.b, d))
            )

    def p3(self):
        for moved in self.c:
            moved.wait_recv()
        add_into(self.at(**{self.e: None}), [self.mid.at[k] for k in range(3)])
        self.c = []
        for k, d in enumerate((1, 3, 2)):
            there = self.net.moved(self.e, d)[self.e]
            self.c.append(self.net.copy(self.at(**{self.e: there}), self.low.at[k], self.net.ring(self.e, d)))

    def result(self):
        for moved in self.c:
            moved.wait_recv()
        value = self.at()[...].astype(F32)
        for k in range(3):
            value = value + self.low[k].astype(F32)
        return value


RECTS = (
    (5, (0, 16), 512, 0, 512, 0),
    (5, (16, 16), 512, 0, 512, 1),
    (5, (32, 32), 512, 0, 512, 2),
    (4, (0, 16), 2048, 0, 512, 0),
    (4, (0, 16), 2048, 512, 1024, 1),
    (4, (0, 16), 2048, 1536, 512, 2),
    (3, (0, 16), 512, 0, 512, 0),
    (0, (0, 16), 512, 0, 512, 0),
    (1, (0, 16), 512, 0, 512, 1),
    (2, (0, 16), 512, 0, 512, 2),
)
BIG_FIRST = tuple(tuple(reversed(o)) for o in ORDER)


def reduce_buffers():
    shapes = []
    for _, (_, rows), _, _, width, order in RECTS:
        a, b, e = BIG_FIRST[order]
        shapes += [
            CHIPS + (rows, width),
            (3,) + chip_shape((a,)) + (rows, width),
            (3,) + chip_shape((a, b)) + (rows, width),
            (3, rows, width),
        ]
    return shapes


class Return:
    def __init__(self, net, window, encoded, back, out, local_sem):
        self.net = net
        lo = lax.rem(net.me["y"], 2)
        other = 1 - lo
        self.lo = lo
        self.window, self.back = window, back
        self.plain = [
            (window.at[rows_at(HALO + TOK * other, TOK)], back.at[0, lo], net.pair(0, other)),
            (encoded.at[rows_at(TOK * other, TOK)], out.at[lo], net.pair(0, other)),
        ]
        self.local = pltpu.make_async_copy(encoded.at[rows_at(TOK * lo, TOK)], out.at[lo], local_sem)
        self.base = net.used
        net.used += 16

    def start(self):
        net, lo = self.net, self.lo
        self.plain = [net.copy(*p) for p in self.plain]
        self.local.start()
        self.copies = []
        for k in range(4):
            for q in range(2):
                by, rows, to, only = pieces(q)[k]
                if only is not None and only != q:
                    continue
                side = 1 if by == 1 else 2
                copy = net.make(
                    self.window.at[pl.ds(to, TOK // 2)],
                    self.back.at[side, lo, rows],
                    net.pair(-by, q),
                    self.base + 4 * k + q,
                    self.base + 4 * k + 2 + lo,
                )
                copy.start()
                self.copies.append(copy)

    def gets(self):
        net = self.net
        for copy in self.plain:
            copy.wait_recv()
        for k in range(4):
            _, rows, _, only = pieces(0)[k]
            for m in range(2):
                copy = net.make(
                    self.window.at[pl.ds(0, TOK // 2)],
                    self.back.at[1, m, rows],
                    net.pair(1, 0),
                    0,
                    self.base + 4 * k + 2 + m,
                )
                if only is None:
                    copy.wait_recv()
                else:
                    pl.when(self.lo == only)(copy.wait_recv)

    def total(self, token_grad):
        lo = self.lo
        half = TOK // 2
        own = self.window[rows_at(HALO + TOK * lo, TOK), :].astype(F32)
        for m in range(2):
            base = jnp.where(lo == m, own, self.back[0, m].astype(F32))
            right = self.back[1, m].astype(F32)
            left = self.back[2, m].astype(F32)
            low = base[:half] + left[:half] + jnp.where(lo == 1, right[:half], 0.0)
            high = base[half:] + right[half:] + jnp.where(lo == 0, left[half:], 0.0)
            token_grad[m] = jnp.concatenate([low, high], axis=0).astype(BF)

    def finish(self):
        self.local.wait()
        for copy in self.copies:
            copy.wait_send()


def reduce_kernel(*refs):
    grads, (window_hbm, encoded) = refs[:6], refs[6:8]
    outs, out, token_grad = refs[8:14], refs[14], refs[15]
    rest = refs[16:]
    full, rest = rest[:6], rest[6:]
    bufs, rest = rest[:40], rest[40:]
    window, back = rest[:2]
    finals, rest = rest[2:8], rest[8:]
    ends, rest = rest[:6], rest[6:]
    send_sem, recv_sem, local_sem = rest
    net = Net(send_sem, recv_sem)
    c = net.me["c"]
    loads = [pltpu.make_async_copy(g, f, local_sem.at[k]) for k, (g, f) in enumerate(zip(grads, full))]
    loads.append(pltpu.make_async_copy(window_hbm, window, local_sem.at[6]))
    for load in loads:
        load.start()
    net.barrier()
    for load in loads:
        load.wait()
    lanes = []
    for k, (w, (r0, rows), per_core, base, width, order) in enumerate(RECTS):
        lanes.append(
            Reduce(
                net,
                full[w],
                pl.ds(r0, rows),
                c * per_core + base,
                width,
                (1 - c) * per_core + base,
                BIG_FIRST[order],
                bufs[4 * k : 4 * k + 4],
            )
        )
    each(lanes, "d0")
    back_rows = Return(net, window, encoded, back, out, local_sem.at[7])
    back_rows.start()
    first, second, third = lanes[:3], lanes[3:6], lanes[6:]
    each(first, "p1")
    each(second, "p1")
    each(first, "p1_mid")
    each(third, "p1")
    each(first, "p2")
    each(second, "p1_mid")
    each(first, "p3")
    each(third, "p1_mid")
    each(second, "p2")
    each(third, "p2")
    each(second, "p3")
    each(third, "p3")
    for lane, (w, (r0, rows), per_core, base, width, _) in zip(lanes, RECTS):
        finals[w][pl.ds(r0, rows), pl.ds(base, width)] = lane.result()
    swaps = []
    for w in range(6):
        n = finals[w].shape[0] // 2
        width = finals[w].shape[1]
        kept = finals[w].at[pl.ds(pl.multiple_of(n * c, 8), n)]
        given = finals[w].at[pl.ds(pl.multiple_of(n * (1 - c), 8), n)]
        swaps.append(net.copy(given, ends[w].at[:, columns(c * width, width)], net.ring("c", 0)))
        ends[w][:, columns(c * width, width)] = kept[...]
    back_rows.gets()
    back_rows.total(token_grad)
    for swap in swaps:
        swap.wait_recv()
    stores = [pltpu.make_async_copy(e, o, local_sem.at[k]) for k, (e, o) in enumerate(zip(ends, outs))]
    for store in stores:
        store.start()
    for store in stores:
        store.wait()
    back_rows.finish()
    net.finish()


def reduce_all(grads, window, encoded):
    any_space = pl.BlockSpec(memory_space=pl.ANY)
    full = [CHIPS + s for s in BLOCKS]
    owned = [(r // 2, n) for r, n in BLOCKS]
    return pl.pallas_call(
        reduce_kernel,
        name="reduce_all",
        out_shape=[jax.ShapeDtypeStruct(s, F32) for s in owned]
        + [jax.ShapeDtypeStruct((2, TOK, D), BF), jax.ShapeDtypeStruct((2, TOK, D), BF)],
        in_specs=[any_space] * 8,
        out_specs=[any_space] * 7 + [pl.BlockSpec(memory_space=pltpu.VMEM)],
        scratch_shapes=[pltpu.VMEM(s, BF) for s in full]
        + [pltpu.VMEM(s, BF) for s in reduce_buffers()]
        + [pltpu.VMEM((WIN, D), BF), pltpu.VMEM((3, 2, TOK, D), BF)]
        + [pltpu.VMEM((r, n // 2), F32) for r, n in BLOCKS]
        + [pltpu.VMEM(s, F32) for s in owned]
        + [
            pltpu.SemaphoreType.DMA((N_SEM,)),
            pltpu.SemaphoreType.DMA((N_SEM,)),
            pltpu.SemaphoreType.DMA((8,)),
        ],
        compiler_params=pltpu.CompilerParams(collective_id=2, has_side_effects=True, vmem_limit_bytes=62 << 20),
    )(*grads, window, encoded)


def dot(a, b):
    return jnp.dot(a, b, preferred_element_type=F32)


def norm(a, gain, shift):
    centred = a - jnp.mean(a, axis=-1, keepdims=True)
    inv = lax.rsqrt(jnp.mean(centred * centred, axis=-1, keepdims=True) + 1e-05)
    n = centred * inv
    return n * gain + shift, n, inv


def norm_back(d, n, inv, gain):
    dn = d * gain
    da = inv * (dn - jnp.mean(dn, axis=-1, keepdims=True) - n * jnp.mean(dn * n, axis=-1, keepdims=True))
    return da, jnp.sum(d * n, axis=0), jnp.sum(d, axis=0)


def segments(lengths, order, start, count):
    ends = jnp.cumsum(jnp.take(lengths, order))
    at = start + jnp.arange(count)
    segment = jnp.sum((ends[:, None] <= at[None, :]).astype(jnp.int32), axis=0)
    return jnp.where(at < 0, -1, segment)


def layer(window, cots, segment, full, vectors):
    wq, wk, wv, wo, wi, wu = full
    bq, bv, bo, g1, s1, bu, g2, s2, bi = [v.astype(F32) for v in vectors]
    rows = window[HALO : HALO + OWN]
    q = (dot(rows, wq) + bq).astype(BF).reshape(OWN, HEADS, HEAD)
    k = dot(window, wk).astype(BF).reshape(WIN, HEADS, HEAD)
    v = (dot(window, wv) + bv).astype(BF).reshape(WIN, HEADS, HEAD)
    same = (segment[HALO : HALO + OWN, None] == segment[None, :])[None]
    scores = jnp.einsum("qhd,khd->hqk", q, k, preferred_element_type=F32) * 0.125
    scores = jnp.where(same, scores, -1e30)
    e = jnp.exp(scores - jnp.max(scores, axis=-1, keepdims=True))
    probs = e / jnp.sum(e, axis=-1, keepdims=True)
    low = probs.astype(BF)
    mixed = jnp.einsum("hqk,khd->qhd", low, v, preferred_element_type=F32)
    context = mixed.reshape(OWN, D).astype(BF)
    attended = rows.astype(F32) + (dot(context, wo) + bo)
    normed, n1, inv1 = norm(attended, g1, s1)
    normed_low = normed.astype(BF)
    pre = dot(normed_low, wi) + bi
    phi = 0.5 * (1.0 + lax.erf(pre * math.sqrt(0.5)))
    activated = (pre * phi).astype(BF)
    slope = phi + pre * jnp.exp(-0.5 * pre * pre) * (1.0 / math.sqrt(2 * math.pi))
    encoded, n2, inv2 = norm(normed + (dot(activated, wu) + bu), g2, s2)
    d_final, dg2, ds2 = norm_back(cots.astype(F32), n2, inv2, g2)
    d_outer = d_final.astype(BF)
    tdot = lambda a, b: lax.dot_general(a, b, (((0,), (0,)), ((), ())), preferred_element_type=F32)
    dott = lambda a, b: lax.dot_general(a, b, (((1,), (1,)), ((), ())), preferred_element_type=F32)
    gwu = tdot(activated, d_outer).astype(BF)
    dbu = jnp.sum(d_outer.astype(F32), axis=0)
    d_inner = (dott(d_outer, wu) * slope).astype(BF)
    gwi = tdot(normed_low, d_inner).astype(BF)
    dbi = jnp.sum(d_inner.astype(F32), axis=0)
    d_normed = d_final + dott(d_inner, wi)
    d_attended, dg1, ds1 = norm_back(d_normed, n1, inv1, g1)
    d_branch = d_attended.astype(BF)
    gwo = tdot(context, d_branch).astype(BF)
    dbo = jnp.sum(d_branch.astype(F32), axis=0)
    d_context = dott(d_branch, wo).astype(BF)
    dc = d_context.reshape(OWN, HEADS, HEAD)
    dv = jnp.einsum("hqk,qhd->khd", low, dc, preferred_element_type=F32).reshape(WIN, D).astype(BF)
    dp = jnp.einsum("qhd,khd->hqk", dc, v, preferred_element_type=F32)
    dsum = jnp.sum((d_context.astype(F32) * context.astype(F32)).reshape(OWN, HEADS, HEAD), axis=-1)
    dr = (probs * (dp - dsum.T[:, :, None]) * 0.125).astype(BF)
    dq = jnp.einsum("hqk,khd->qhd", dr, k, preferred_element_type=F32).reshape(OWN, D).astype(BF)
    dk = jnp.einsum("hqk,qhd->khd", dr, q, preferred_element_type=F32).reshape(WIN, D).astype(BF)
    gwq = tdot(rows, dq).astype(BF)
    gwk = tdot(window, dk).astype(BF)
    gwv = tdot(window, dv).astype(BF)
    dbq = jnp.sum(dq.astype(F32), axis=0)
    dbv = jnp.sum(dv.astype(F32), axis=0)
    dx = dott(dk, wk) + dott(dv, wv)
    mid = dx[HALO : HALO + OWN] + d_attended + dott(dq, wq)
    dx = jnp.concatenate([dx[:HALO], mid, dx[HALO + OWN :]], axis=0).astype(BF)
    grads = (gwq, gwk, gwv, gwo, gwi, gwu)
    return encoded.astype(BF), dx, grads, (dbq, dbv, dbo, dg1, ds1, dbu, dg2, ds2, dbi)


def local(
    tokens, cotangent, seq_lengths, block_offsets, deal_order, wq, wk, wv, wo, bq, bv, bo, g1, s1, wi, bi, wu, bu, g2, s2
):
    lo = lax.rem(lax.axis_index("dp"), 2)
    own = jnp.concatenate([wq, wk, wv, wo] + [wi[:, D * j : D * j + D] for j in range(4)] + [wu], axis=0)
    gathered = gather_all(own, tokens[:, 0], cotangent[:, 0])
    full = [w.reshape(-1, w.shape[-1]) for w in gathered[:6]]
    window, cots = gathered[6:]
    small = jnp.concatenate([bq, bv, bo, g1, s1, bu, g2, s2, bi])
    both = lax.all_gather(small, ("dp", "shard"), axis=0)
    vectors = [both[:, 8 * j : 8 * j + 8].reshape(-1) for j in range(8)] + [both[:, 64:].reshape(-1)]
    lengths = lax.dynamic_index_in_dim(seq_lengths[:, 0], lo, 0, keepdims=False)
    order = lax.dynamic_index_in_dim(deal_order[:, 0], lo, 0, keepdims=False)
    start = lax.div(lax.axis_index("dp"), 2) * OWN - HALO
    segment = segments(lengths, order, start, WIN)
    encoded, dx, grads, small_grads = layer(window, cots, segment, full, vectors)
    blocked = [g.reshape(CHIPS + s) for g, s in zip(grads, BLOCKS)]
    *owned, out, token_grad = reduce_all(blocked, dx, encoded)
    lines = jnp.concatenate([g.reshape(128, -1) for g in small_grads], axis=1)
    mine = lax.psum_scatter(lines, ("dp", "shard"), scatter_dimension=0, tiled=True)[0]
    sbq, sbv, sbo, sg1, ss1, sbu, sg2, ss2 = [mine[8 * j : 8 * j + 8] for j in range(8)]
    return (out[:, None], token_grad[:, None], *owned[:4], sbq, sbv, sbo, sg1, ss1, owned[4], mine[64:], owned[5], sbu, sg2, ss2)


def solution(mesh):
    rows = P(None, "shard", "dp", None)
    table = P(None, "shard", None)
    matrix, vector = P(("dp", "shard"), None), P(("dp", "shard"))
    in_specs = (rows, rows) + (table,) * 3 + (matrix,) * 4 + (vector,) * 5 + (matrix, vector, matrix) + (vector,) * 3
    out_specs = (rows, rows) + (matrix,) * 4 + (vector,) * 5 + (matrix, vector, matrix) + (vector,) * 3
    return jax.shard_map(local, mesh=mesh, in_specs=in_specs, out_specs=out_specs, check_vma=False)
```

```python
import math

import jax
import jax.numpy as jnp
from jax import lax
from jax.experimental import pallas as pl
from jax.experimental.pallas import tpu as pltpu
from jax.sharding import PartitionSpec as P

MESH = pl.DeviceIdType.MESH
BF = jnp.bfloat16
F32 = jnp.float32
D = 1024
FF = 4096
HEADS = 16
HEAD = 64
TOK = 128
OWN = 2 * TOK
HALO = 192
WIN = OWN + 2 * HALO
AXES = ("x", "y", "z")
ORDER = (("z", "y", "x"), ("x", "z", "y"), ("y", "x", "z"))
CHIPS = (4, 2, 2, 4)
N_SEM = 200


def position():
    dp, sh = lax.axis_index("dp"), lax.axis_index("shard")
    return {
        "x": lax.div(dp, 2),
        "y": lax.div(sh, 8) * 2 + lax.rem(dp, 2),
        "z": lax.div(lax.rem(sh, 8), 2),
        "c": lax.rem(sh, 2),
    }


def device_at(at):
    return (
        at["x"] * 2 + lax.rem(at["y"], 2),
        lax.div(at["y"], 2) * 8 + at["z"] * 2 + at["c"],
    )


class Net:
    def __init__(self, send_sem, recv_sem):
        self.me = position()
        self.send_sem, self.recv_sem = send_sem, recv_sem
        self.used = 0
        self.sent = []

    def moved(self, axis, by):
        at = dict(self.me)
        if axis == "c":
            at["c"] = 1 - at["c"]
        else:
            at[axis] = lax.rem(at[axis] + by, 4)
        return at

    def ring(self, axis, by):
        return device_at(self.moved(axis, by))

    def pair(self, by, lo):
        at = self.moved("x", by % 4)
        at["y"] = lax.div(at["y"], 2) * 2 + lo
        return device_at(at)

    def slot(self):
        self.used += 1
        return self.used - 1

    def make(self, src, dst, device, send, recv):
        return pltpu.make_async_remote_copy(
            src_ref=src,
            dst_ref=dst,
            send_sem=self.send_sem.at[send],
            recv_sem=self.recv_sem.at[recv],
            device_id=device,
            device_id_type=MESH,
        )

    def copy(self, src, dst, device):
        k = self.slot()
        moved = self.make(src, dst, device, k, k)
        moved.start()
        self.sent.append(moved)
        return moved

    def barrier(self):
        bar = pltpu.get_barrier_semaphore()
        peers = [self.ring("c", 0)] + [self.ring(a, b) for a in AXES for b in (1, 2, 3)]
        other = 1 - lax.rem(self.me["y"], 2)
        peers += [self.pair(1, other), self.pair(3, other)]
        for p in peers:
            pl.semaphore_signal(bar, inc=1, device_id=p, device_id_type=MESH)
        pl.semaphore_wait(bar, len(peers))

    def finish(self):
        for moved in self.sent:
            moved.wait_send()
        assert self.used <= N_SEM, self.used


def chip_index(at, drop=()):
    out = []
    for axis in AXES:
        if axis in drop:
            continue
        v = at[axis]
        if axis == "y":
            if v is None:
                out += [slice(None), slice(None)]
            elif isinstance(v, tuple):
                out += [v[1], slice(None)]
            else:
                out += [lax.rem(v, 2), lax.div(v, 2)]
        elif v is None:
            out.append(slice(None))
        elif isinstance(v, tuple):
            out.append(pl.ds(2 * v[1], 2))
        else:
            out.append(v)
    return tuple(out)


def chip_shape(drop):
    shape = ()
    for axis in AXES:
        if axis not in drop:
            shape += (2, 2) if axis == "y" else (4,)
    return shape


def columns(base, width):
    return pl.ds(pl.multiple_of(base, 128), width)


class Gather:
    def __init__(self, net, ref, rows, cols, order):
        self.net, self.ref, self.rows, self.cols = net, ref, rows, cols
        self.a, self.b, self.e = order

    def at(self, **over):
        place = {k: self.net.me[k] for k in AXES}
        place.update(over)
        return self.ref.at[chip_index(place) + (self.rows, self.cols)]

    def send(self, region, axis, by):
        return self.net.copy(region, region, self.net.ring(axis, by))

    def p1(self):
        self.c = [self.send(self.at(), self.a, d) for d in (1, 3, 2)]

    def p2(self):
        for moved in self.c:
            moved.wait_recv()
        self.c = [self.send(self.at(**{self.a: None}), self.b, d) for d in (1, 3, 2)]

    def part(self, h, by):
        e = self.net.moved(self.e, by)[self.e]
        return self.at(**{self.a: h if h is None else ("half", h), self.b: None, self.e: e})

    def p3(self):
        for moved in self.c:
            moved.wait_recv()
        self.r0 = self.send(self.part(0, 0), self.e, 1)
        self.l1 = self.send(self.part(1, 0), self.e, 3)
        self.r1 = self.send(self.part(1, 0), self.e, 1)
        self.l0 = self.send(self.part(0, 0), self.e, 3)
        self.core = [self.send(self.part(None, 0), "c", 0)]

    def p3_mid(self):
        self.r0.wait_recv()
        self.f0 = self.send(self.part(0, 3), self.e, 1)
        self.l1.wait_recv()
        self.f1 = self.send(self.part(1, 1), self.e, 3)

    def p3_core(self):
        self.r1.wait_recv()
        self.core.append(self.send(self.part(None, 3), "c", 0))
        self.l0.wait_recv()
        self.core.append(self.send(self.part(None, 1), "c", 0))

    def p3_end(self):
        self.f0.wait_recv()
        self.f1.wait_recv()
        self.core.append(self.send(self.part(None, 2), "c", 0))

    def done(self):
        for moved in self.core:
            moved.wait_recv()


def each(lanes, step):
    for lane in lanes:
        getattr(lane, step)()


def pieces(lo):
    at = TOK * lo
    return (
        (1, pl.ds(TOK // 2, TOK // 2), at + TOK // 2 - (OWN - HALO), None),
        (1, pl.ds(0, TOK // 2), at - (OWN - HALO), 1),
        (-1, pl.ds(0, TOK // 2), at + HALO + OWN, None),
        (-1, pl.ds(TOK // 2, TOK // 2), at + TOK // 2 + HALO + OWN, 0),
    )


def rows_at(base, count):
    return pl.ds(pl.multiple_of(base, TOK // 2), count)


class Window:
    def __init__(self, net, tokens, cotangent, window, cots, local_sem):
        self.net = net
        lo = lax.rem(net.me["y"], 2)
        other = 1 - lo
        self.copies = []
        mine = rows_at(HALO + TOK * lo, TOK)
        theirs = rows_at(TOK * lo, TOK)
        self.local = [
            pltpu.make_async_copy(tokens.at[lo], window.at[mine], local_sem.at[0]),
            pltpu.make_async_copy(cotangent.at[lo], cots.at[theirs], local_sem.at[1]),
        ]
        self.pair = [
            (tokens.at[other], window.at[mine]),
            (cotangent.at[other], cots.at[theirs]),
        ]
        self.halo = []
        for by, rows, to, only in pieces(lo):
            first = net.slot()
            second = net.slot()
            for m in range(2):
                send = first if m == 0 else second
                copy = net.make(
                    tokens.at[m, rows], window.at[rows_at(to, TOK // 2)], net.pair(by, m), send, first + lo
                )
                self.halo.append((copy, only))
        self.gets = []
        for k, (by, rows, to, only) in enumerate(pieces(lo)):
            for source in range(2):
                if only is None or only == source:
                    index = 2 * k + source + (net.used - 8)
                    self.gets.append(
                        net.make(tokens.at[0, rows], window.at[pl.ds(0, TOK // 2)], net.pair(1, other), 0, index)
                    )

    def start(self):
        for copy in self.local:
            copy.start()
        lo = lax.rem(self.net.me["y"], 2)
        self.pair = [self.net.copy(s, d, self.net.pair(0, 1 - lo)) for s, d in self.pair]
        for copy, only in self.halo:
            if only is None:
                copy.start()
            else:
                pl.when(lo == only)(copy.start)

    def done(self):
        for copy in self.local:
            copy.wait()
        for copy in self.pair + self.gets:
            copy.wait_recv()

    def finish(self):
        lo = lax.rem(self.net.me["y"], 2)
        for copy, only in self.halo:
            if only is None:
                copy.wait_send()
            else:
                pl.when(lo == only)(copy.wait_send)


def place_own(me, mine, peer, full):
    here = chip_index(me)
    c = me["c"]
    first = c == 0

    def both(a, b):
        return jnp.concatenate([jnp.where(first, a, b), jnp.where(first, b, a)], axis=0)

    half = columns(c * 512, 512)
    for j in range(4):
        r = slice(8 * j, 8 * j + 8)
        full[j][here + (slice(None), half)] = both(mine[r, half], peer[r, half])
    for t in range(2):
        r, s = slice(32 + 8 * t, 40 + 8 * t), slice(48 + 8 * t, 56 + 8 * t)
        a = jnp.where(first, mine[r, :], mine[s, :])
        b = jnp.where(first, peer[r, :], peer[s, :])
        full[4][here + (slice(None), columns(c * 2048 + 1024 * t, 1024))] = both(a, b)
    full[5][here + (slice(None), half)] = both(mine[64:96, half], peer[64:96, half])


BLOCKS = ((16, 1024),) * 4 + ((16, 4096), (64, 1024))


SPAN = TOK + 2 * HALO
NT = (((1,), (1,)), ((), ()))
TN = (((0,), (0,)), ((), ()))
NN = (((1,), (0,)), ((), ()))


def mm(a, b, dims=NN):
    return lax.dot_general(a, b, dims, preferred_element_type=F32)


def tile(w, n0, n):
    return w[:, :, :, :, :, columns(n0, n)].reshape(-1, n)


def project(rows, w, out, bias=None, n=512):
    def body(t, carry):
        cols = columns(t * n, n)
        y = mm(rows[...], tile(w, t * n, n))
        if bias is not None:
            y = y + bias[:, cols]
        out[:, cols] = y.astype(BF)
        return carry

    lax.fori_loop(0, out.shape[1] // n, body, 0)


def lane_split(x):
    low = lax.broadcasted_iota(jnp.int32, x.shape, 1) < HEAD
    zero = jnp.zeros_like(x)
    return jnp.concatenate([jnp.where(low, x, zero), jnp.where(low, zero, x)], axis=0)


def lane_join(x):
    n = x.shape[0] // 2
    low = lax.broadcasted_iota(jnp.int32, (n, x.shape[1]), 1) < HEAD
    return jnp.where(low, x[:n], x[n:])


def attention(q, k, v, bias, probs, context, first, last):
    def body(h, carry):
        cols = columns(h * 128, 128)
        for b in range(2):
            mine, near = pl.ds(b * TOK, TOK), pl.ds(b * TOK, SPAN)
            pen = bias[b]
            s = mm(k[near, cols], lane_split(q[mine, cols]), NT) * 0.125 + jnp.concatenate([pen, pen], axis=1)
            e = jnp.exp(s - jnp.max(s, axis=0, keepdims=True))
            p = (e * (1.0 / jnp.sum(e, axis=0, keepdims=True))).astype(BF)
            at = columns((2 * h + b) * OWN, OWN)
            probs[0, :, at], probs[1, :, at] = p[:OWN], p[OWN:]
            y = mm(v[near, cols], p, TN)
            y = jnp.concatenate([y[:HEAD, :TOK], y[HEAD:, TOK:]], axis=0)
            context[mine, cols] = y.T.astype(BF)
        return carry

    lax.fori_loop(first, last, body, 0)


def normalized(a):
    centred = a - jnp.mean(a, axis=-1, keepdims=True)
    inv = lax.rsqrt(jnp.mean(centred * centred, axis=-1, keepdims=True) + 1e-05)
    return centred * inv, inv


def norm_back(dn, n, inv):
    return inv * (dn - jnp.mean(dn, axis=-1, keepdims=True) - n * jnp.mean(dn * n, axis=-1, keepdims=True))


def feed_in(low, wi, bi, act, slope, first, last, n=512):
    def body(t, carry):
        cols = columns(t * n, n)
        u = mm(low[...], tile(wi, t * n, n)) + bi[:, cols]
        phi = 0.5 + 0.5 * lax.erf(u * math.sqrt(0.5))
        act[:, cols] = (u * phi).astype(BF)
        slope[:, cols] = (phi + u * (jnp.exp(-0.5 * (u * u)) * (1.0 / math.sqrt(2 * math.pi)))).astype(BF)
        return carry

    lax.fori_loop(first, last, body, 0)


ROWS = 32


def some_rows(t):
    return pl.ds(pl.multiple_of(t * ROWS, ROWS), ROWS)


def segment_bias(lengths, order, start, lo, bias):
    ends, total = [], 0
    for k in range(16):
        total = total + lengths[lo, order[lo, k]]
        ends.append(total)

    def which(at):
        found = jnp.where(at < 0, -1, 0)
        for e in ends:
            found = found + (at >= e).astype(jnp.int32)
        return found

    keys = which(start + lax.broadcasted_iota(jnp.int32, (WIN, TOK), 0))
    queries = which(start + HALO + lax.broadcasted_iota(jnp.int32, (8, OWN), 1))[:1]
    for b in range(2):
        same = keys[b * TOK : b * TOK + SPAN] == queries[:, b * TOK : b * TOK + TOK]
        bias[b] = jnp.where(same, 0.0, -1e30)


class Vectors:
    def __init__(self, net, small, tiles, vec, inner):
        self.net, self.small = net, small
        self.own, self.sib, self.tz, self.ty, self.tx = tiles
        self.vec, self.inner = vec, inner

    def around(self, axis, block):
        return [self.net.copy(block, block, self.net.ring(axis, d)) for d in (1, 3, 2)]

    def start(self):
        sh = lax.axis_index("shard")
        r = lax.broadcasted_iota(jnp.int32, (16, 128), 0)
        i = lax.broadcasted_iota(jnp.int32, (16, 128), 1)
        value = jnp.broadcast_to(self.small[0:1, :].astype(F32), (16, 128))
        part = (i < 64) & (lax.shift_right_logical(i, 3) == r)
        inner = (i >= 64) & (i < 96) & (r == 8 + lax.div(sh, 4))
        picked = jnp.where(part | inner, value, 0.0).astype(BF)
        i = lax.broadcasted_iota(jnp.int32, (128, 128), 0)
        to = lax.broadcasted_iota(jnp.int32, (128, 128), 1)
        place = jnp.where(i < 64, 8 * sh + (i & 7), 32 * lax.rem(sh, 4) + i - 64)
        self.own[...] = mm(picked, jnp.where((place == to) & (i < 96), 1.0, 0.0).astype(BF)).astype(BF)
        self.c = [self.net.copy(self.own, self.sib, self.net.ring("c", 0))]

    def wait(self):
        for moved in self.c:
            moved.wait_recv()

    def along_z(self):
        self.wait()
        z = self.net.me["z"]
        self.tz[z] = self.own[...] + self.sib[...]
        self.c = self.around("z", self.tz.at[z])

    def along_y(self):
        self.wait()
        y = self.net.me["y"]
        self.ty[y] = (self.tz[0] + self.tz[1]) + (self.tz[2] + self.tz[3])
        self.c = self.around("y", self.ty.at[y])

    def along_x(self):
        self.wait()
        x = self.net.me["x"]
        self.tx[x, 0] = self.ty[0] + self.ty[2]
        self.tx[x, 1] = self.ty[1] + self.ty[3]
        self.c = self.around("x", self.tx.at[x])

    def done(self):
        self.wait()
        for dp in range(8):
            got = self.tx[dp // 2, dp % 2].astype(F32)
            self.vec[:, 128 * dp : 128 * dp + 128] = got[:8]
            for t in range(4):
                at = 512 * dp + 128 * t
                self.inner[:, at : at + 128] = got[8 + t : 9 + t]


BQ, BV, BO, G1, S1, BU, G2, S2 = range(8)


def forward_kernel(*refs):
    tokens, cotangent, lengths, order, small = refs[:5]
    own, refs = refs[5:11], refs[11:]
    outs, refs = refs[:21], refs[21:]
    weights_out, refs_out = outs[:6], outs[6:]
    (x_out, q_out, k_out, v_out, probs_out, context_out, low_out, act_out, slope_out) = refs_out[:9]
    (n1_out, inv1_out, d_final_out, encoded_out, vec_out, two_out) = refs_out[9:]
    mine, peer = refs[:2]
    full, refs = refs[2:8], refs[8:]
    window, cots, q, k, v, probs, context, low, act, slope, bias, refs = *refs[:11], refs[11:]
    n1, inv1, normed, total, encoded, vec, inner, two, refs = *refs[:8], refs[8:]
    tiles, refs = refs[:5], refs[5:]
    send_sem, recv_sem, local_sem = refs
    net = Net(send_sem, recv_sem)
    me, c = net.me, net.me["c"]
    lo = lax.rem(me["y"], 2)
    stores = []

    def store(src, dst):
        move = pltpu.make_async_copy(src, dst, local_sem.at[2 + len(stores)])
        move.start()
        stores.append(move)

    def both(src, dst):
        net.copy(src, dst.at[c], net.ring("c", 0))
        store(src, dst.at[c])
        return net.sent[-1]

    for j in range(4):
        mine[8 * j : 8 * j + 8, :] = own[j][...]
        mine[32 + 8 * j : 40 + 8 * j, :] = own[4][:, 1024 * j : 1024 * j + 1024]
    mine[64:96, :] = own[5][...]
    net.barrier()
    swap = net.copy(mine, peer, net.ring("c", 0))
    vectors = Vectors(net, small, tiles, vec, inner)
    vectors.start()
    swap.wait_recv()
    place_own(me, mine, peer, full)
    rows = slice(None)
    half = columns(c * 512, 512)
    wi, wu = full[4], full[5]
    first = [Gather(net, full[j], rows, half, ORDER[j]) for j in range(3)]
    second = [
        Gather(net, full[3], rows, half, ORDER[0]),
        Gather(net, wi, rows, columns(c * 2048 + 512, 1024), ORDER[1]),
        Gather(net, wi, rows, columns(c * 2048 + 1536, 512), ORDER[2]),
        Gather(net, wi, rows, columns(c * 2048, 512), ORDER[0]),
    ]
    third = [
        Gather(net, wu, pl.ds(0, 16), half, ORDER[0]),
        Gather(net, wu, pl.ds(16, 16), half, ORDER[1]),
        Gather(net, wu, pl.ds(32, 32), half, ORDER[2]),
    ]
    for lanes in (first, second, third):
        each(lanes, "p1")
    view = Window(net, tokens, cotangent, window, cots, local_sem)
    view.start()
    vectors.along_z()
    segment_bias(lengths, order, me["x"] * OWN - HALO, lo, bias)
    each(first, "p2")
    vectors.along_y()
    each(second, "p2")
    each(third, "p2")
    vectors.along_x()
    each(first, "p3")
    each(second, "p3")
    each(first, "p3_mid")
    each(third, "p3")
    each(first, "p3_core")
    vectors.done()
    view.done()
    each(second, "p3_mid")
    each(first, "p3_end")
    got_x = both(window, x_out)
    each(first, "done")
    project(window.at[pl.ds(HALO, OWN)], full[0], q, vec.at[BQ : BQ + 1])
    each(third, "p3_mid")
    project(window, full[1], k)
    each(second, "p3_core")
    project(window, full[2], v, vec.at[BV : BV + 1])
    for j in range(3):
        store(full[j], weights_out[j])
    store(q, q_out)
    store(k, k_out)
    store(v, v_out)
    attention(q, k, v, bias, probs, context, 0, 2)
    each(second, "p3_end")
    each(third, "p3_core")
    attention(q, k, v, bias, probs, context, 2, 5)
    each(third, "p3_end")
    attention(q, k, v, bias, probs, context, 5, 8)
    got_context = both(context, context_out)
    store(probs, probs_out)
    each(second, "done")
    store(full[3], weights_out[3])
    store(full[4], weights_out[4])

    def attend(t, carry):
        cols = columns(t * 512, 512)
        y = mm(context[...], tile(full[3], t * 512, 512)) + vec[BO : BO + 1, cols]
        total[:, cols] = y + window[pl.ds(HALO, OWN), cols].astype(F32)
        return carry

    lax.fori_loop(0, 2, attend, 0)

    def norm_one(t, carry):
        r = some_rows(t)
        n, inv = normalized(total[r, :])
        n1[r, :] = n
        inv1[r, :] = jnp.broadcast_to(inv, (ROWS, 128))
        y = n * vec[G1 : G1 + 1, :] + vec[S1 : S1 + 1, :]
        normed[r, :] = y
        low[r, :] = y.astype(BF)
        return carry

    lax.fori_loop(0, OWN // ROWS, norm_one, 0)
    got_low = both(low, low_out)
    store(n1, n1_out)
    store(inv1, inv1_out)
    feed_in(low, wi, inner, act, slope, 0, FF // 512)
    got_act = both(act, act_out)
    store(slope, slope_out)
    store(vec, vec_out)
    each(third, "done")
    store(full[5], weights_out[5])

    def feed_out(t, carry):
        cols = columns(t * 512, 512)
        y = mm(act[...], tile(wu, t * 512, 512)) + vec[BU : BU + 1, cols]
        total[:, cols] = y + normed[:, cols]
        return carry

    lax.fori_loop(0, 2, feed_out, 0)

    def norm_two(t, carry):
        r = some_rows(t)
        n, inv = normalized(total[r, :])
        gain = vec[G2 : G2 + 1, :]
        encoded[r, :] = (n * gain + vec[S2 : S2 + 1, :]).astype(BF)
        d = cots[r, :].astype(F32)
        normed[r, :] = norm_back(d * gain, n, inv)
        dn = jnp.sum((d * n).reshape(ROWS // 8, 8, D), axis=0)
        return carry[0] + dn, carry[1] + jnp.sum(d.reshape(ROWS // 8, 8, D), axis=0)

    zero = jnp.zeros((8, D), F32)
    gain_sum, shift_sum = lax.fori_loop(0, OWN // ROWS, norm_two, (zero, zero))
    two[0:1, :] = jnp.sum(gain_sum, axis=0, keepdims=True)
    two[1:2, :] = jnp.sum(shift_sum, axis=0, keepdims=True)
    two[2:8, :] = jnp.zeros((6, D), F32)
    store(normed, d_final_out)
    store(encoded, encoded_out)
    store(two, two_out)
    for got in (got_x, got_context, got_low, got_act):
        got.wait_recv()
    for move in stores:
        move.wait()
    view.finish()
    net.finish()


def forward_all(tokens, cotangent, lengths, order, small, own):
    any_space = pl.BlockSpec(memory_space=pl.ANY)
    vmem = pl.BlockSpec(memory_space=pltpu.VMEM)
    smem = pl.BlockSpec(memory_space=pltpu.SMEM)
    full = [(CHIPS + s, BF) for s in BLOCKS]
    kept = [
        ((2, WIN, D), BF),
        ((OWN, D), BF),
        ((WIN, D), BF),
        ((WIN, D), BF),
        ((2, OWN, FF), BF),
        ((2, OWN, D), BF),
        ((2, OWN, D), BF),
        ((2, OWN, FF), BF),
        ((OWN, FF), BF),
        ((OWN, D), F32),
        ((OWN, 128), F32),
        ((OWN, D), F32),
        ((OWN, D), BF),
        ((8, D), F32),
        ((8, D), F32),
    ]
    scratch = [((96, 1024), BF)] * 2 + full
    scratch += [((WIN, D), BF), ((OWN, D), BF), ((OWN, D), BF), ((WIN, D), BF), ((WIN, D), BF)]
    scratch += [((2, OWN, FF), BF), ((OWN, D), BF), ((OWN, D), BF), ((OWN, FF), BF), ((OWN, FF), BF)]
    scratch += [((2, SPAN, TOK), F32), ((OWN, D), F32), ((OWN, 128), F32), ((OWN, D), F32), ((OWN, D), F32)]
    scratch += [((OWN, D), BF), ((8, D), F32), ((1, FF), F32), ((8, D), F32)]
    scratch += [((16, 128), BF)] * 2 + [((4, 16, 128), BF)] * 2 + [((4, 2, 16, 128), BF)]
    return pl.pallas_call(
        forward_kernel,
        name="forward_all",
        out_shape=[jax.ShapeDtypeStruct(s, t) for s, t in full + kept],
        in_specs=[any_space] * 2 + [smem] * 2 + [vmem] * 7,
        out_specs=[any_space] * 21,
        scratch_shapes=[pltpu.VMEM(s, t) for s, t in scratch]
        + [
            pltpu.SemaphoreType.DMA((N_SEM,)),
            pltpu.SemaphoreType.DMA((N_SEM,)),
            pltpu.SemaphoreType.DMA((32,)),
        ],
        compiler_params=pltpu.CompilerParams(collective_id=1, has_side_effects=True, vmem_limit_bytes=62 << 20),
    )(tokens, cotangent, lengths, order, small, *own)


def add_into(dst, srcs):
    lead = dst.shape[:-2]
    loop = lead[:-1] if len(lead) > 1 else lead
    total = math.prod(loop)

    def body(k, carry):
        index, rest = (), k
        for n in reversed(loop):
            index = (lax.rem(rest, n),) + index
            rest = lax.div(rest, n)
        value = dst[index].astype(F32)
        for s in srcs:
            value = value + s[index].astype(F32)
        dst[index] = value.astype(BF)
        return carry

    lax.fori_loop(0, total, body, 0)


class Reduce:
    def __init__(self, net, ref, rows, cols, order, bufs):
        self.net, self.ref, self.rows, self.cols = net, ref, rows, cols
        self.a, self.b, self.e = order
        self.wide, self.mid, self.low = bufs

    def at(self, **over):
        place = {k: self.net.me[k] for k in AXES}
        place.update(over)
        return self.ref.at[chip_index(place) + (self.rows, self.cols)]

    def quarter(self, by, h):
        b = None if h is None else ("half", h)
        return self.at(**{self.a: self.net.moved(self.a, by)[self.a], self.b: b, self.e: None})

    def buf(self, k, h):
        b = None if h is None else ("half", h)
        return self.wide.at[(k,) + chip_index({self.b: b, self.e: None}, drop=(self.a,))]

    def send(self, by, h, k, to):
        return self.net.copy(self.quarter(by, h), self.buf(k, h), self.net.ring(self.a, to))

    def p1(self):
        self.m0 = self.send(2, 0, 0, 1)
        self.m1 = self.send(2, 1, 0, 3)
        self.l1 = self.send(1, 1, 1, 1)
        self.r0 = self.send(3, 0, 2, 3)

    def p1_mid(self):
        self.m0.wait_recv()
        add_into(self.quarter(1, 0), [self.buf(0, 0)])
        self.l0 = self.send(1, 0, 1, 1)
        self.m1.wait_recv()
        add_into(self.quarter(3, 1), [self.buf(0, 1)])
        self.r1 = self.send(3, 1, 2, 3)

    def p2(self):
        for moved in (self.l1, self.r0, self.l0, self.r1):
            moved.wait_recv()
        add_into(self.quarter(0, None), [self.buf(1, None), self.buf(2, None)])
        self.c = []
        for k, d in enumerate((1, 3, 2)):
            there = self.net.moved(self.b, d)[self.b]
            self.c.append(
                self.net.copy(self.at(**{self.b: there, self.e: None}), self.mid.at[k], self.net.ring(self.b, d))
            )

    def p3(self):
        for moved in self.c:
            moved.wait_recv()
        add_into(self.at(**{self.e: None}), [self.mid.at[k] for k in range(3)])
        self.c = []
        for k, d in enumerate((1, 3, 2)):
            there = self.net.moved(self.e, d)[self.e]
            self.c.append(self.net.copy(self.at(**{self.e: there}), self.low.at[k], self.net.ring(self.e, d)))

    def result(self):
        for moved in self.c:
            moved.wait_recv()
        value = self.at()[...].astype(F32)
        for k in range(3):
            value = value + self.low[k].astype(F32)
        return value


RECTS = (
    (5, (0, 16), (0, 512), 0),
    (5, (16, 16), (0, 512), 1),
    (5, (32, 32), (0, 512), 2),
    (4, (0, 16), (0, 512), 0),
    (4, (0, 16), (512, 1024), 1),
    (4, (0, 16), (1536, 512), 2),
    (3, (0, 16), (0, 512), 0),
    (0, (0, 16), (0, 512), 0),
    (1, (0, 16), (0, 512), 1),
    (2, (0, 16), (0, 512), 2),
)
BIG_FIRST = tuple(tuple(reversed(o)) for o in ORDER)


def reduce_buffers():
    shapes = []
    for _, (_, rows), (_, width), order in RECTS:
        a, b, e = BIG_FIRST[order]
        shapes += [
            (3,) + chip_shape((a,)) + (rows, width),
            (3,) + chip_shape((a, b)) + (rows, width),
            (3, rows, width),
        ]
    return shapes


class VectorSum:
    def __init__(self, net, total, bufs):
        self.net, self.total = net, total
        self.sib, self.whole, self.vx, self.half, self.vy, self.one, self.vz = bufs

    def start(self):
        self.c = [self.net.copy(self.total, self.sib, self.net.ring("c", 0))]

    def wait(self):
        for moved in self.c:
            moved.wait_recv()

    def along_x(self):
        self.wait()
        self.whole[...] = self.total[...] + self.sib[...]
        self.c = []
        for k, d in enumerate((1, 3, 2)):
            x = self.net.moved("x", d)["x"]
            self.c.append(self.net.copy(self.whole.at[:, columns(256 * x, 256)], self.vx.at[k], self.net.ring("x", d)))

    def along_y(self):
        self.wait()
        mine = self.whole[:, columns(256 * self.net.me["x"], 256)]
        for k in range(3):
            mine = mine + self.vx[k]
        self.half[0], self.half[1] = mine[:, :128], mine[:, 128:]
        self.c = []
        for k, d in enumerate((1, 3, 2)):
            lo = lax.rem(self.net.moved("y", d)["y"], 2)
            self.c.append(self.net.copy(self.half.at[lo], self.vy.at[k], self.net.ring("y", d)))

    def along_z(self):
        self.wait()
        mine = self.half[lax.rem(self.net.me["y"], 2)]
        for k in range(3):
            mine = mine + self.vy[k]
        self.one[...] = mine
        self.c = [self.net.copy(self.one, self.vz.at[k], self.net.ring("z", d)) for k, d in enumerate((1, 3, 2))]

    def done(self, out):
        self.wait()
        t = (self.one[...] + self.vz[0]) + (self.vz[1] + self.vz[2])
        sh = lax.axis_index("shard")
        to = lax.broadcasted_iota(jnp.int32, (128, 128), 0)
        i = lax.broadcasted_iota(jnp.int32, (128, 128), 1)
        place = jnp.where(i < 64, 8 * sh + (i & 7), 32 * lax.rem(sh, 4) + i - 64)
        pick = jnp.where((place == to) & (i < 96), 1.0, 0.0).astype(BF)
        high = t.astype(BF)
        rest = t - high.astype(F32)
        mid = rest.astype(BF)
        last = (rest - mid.astype(F32)).astype(BF)
        got = (mm(high, pick) + mm(mid, pick)) + mm(last, pick)
        r = lax.broadcasted_iota(jnp.int32, (16, 128), 0)
        i = lax.broadcasted_iota(jnp.int32, (16, 128), 1)
        keep = ((i < 64) & (lax.shift_right_logical(i, 3) == r)) | ((i >= 64) & (r == 8 + lax.div(sh, 4)))
        out[...] = jnp.broadcast_to(jnp.sum(jnp.where(keep, got, 0.0), axis=0, keepdims=True), (8, 128))


def attention_back(q, k, v, probs, context, d_context, dq, dk, dv, first, last):
    def body(h, carry):
        cols = columns(h * 128, 128)
        dks, dvs = [], []
        for b in range(2):
            mine, near = pl.ds(b * TOK, TOK), pl.ds(b * TOK, SPAN)
            at = columns((2 * h + b) * OWN, OWN)
            p = jnp.concatenate([probs[0, :, at], probs[1, :, at]], axis=0)
            dc = d_context[mine, cols]
            dc2 = lane_split(dc)
            prod = (dc.astype(F32) * context[mine, cols].astype(F32)).T
            dsum = [jnp.sum(prod[s * HEAD : s * HEAD + HEAD], axis=0, keepdims=True) for s in range(2)]
            dp = mm(v[near, cols], dc2, NT)
            dr = (p.astype(F32) * ((dp - jnp.concatenate(dsum, axis=1)) * 0.125)).astype(BF)
            dvs.append(mm(p, dc2))
            dks.append(mm(dr, lane_split(q[mine, cols])))
            g = mm(k[near, cols], dr, TN)
            g = jnp.concatenate([g[:HEAD, :TOK], g[HEAD:, TOK:]], axis=0)
            dq[mine, cols] = g.T.astype(BF)
        for d, o in ((dks, dk), (dvs, dv)):
            o[0:TOK, cols] = d[0][:TOK].astype(BF)
            o[TOK:SPAN, cols] = (d[0][TOK:] + d[1][: SPAN - TOK]).astype(BF)
            o[SPAN:WIN, cols] = d[1][SPAN - TOK :].astype(BF)
        return carry

    lax.fori_loop(first, last, body, 0)


def column_sum(x):
    n, width = x.shape
    return jnp.sum(jnp.sum(x.astype(F32).reshape(n // 8, 8, width), axis=0), axis=0, keepdims=True)


class Return:
    def __init__(self, net, window, encoded, back, out, local_sem):
        self.net = net
        lo = lax.rem(net.me["y"], 2)
        other = 1 - lo
        self.lo = lo
        self.window, self.back = window, back
        self.plain = [(window.at[rows_at(HALO + TOK * other, TOK)], back.at[0, lo], net.pair(0, other))]
        self.encoded = (encoded.at[rows_at(TOK * other, TOK)], out.at[lo], net.pair(0, other))
        self.local = pltpu.make_async_copy(encoded.at[rows_at(TOK * lo, TOK)], out.at[lo], local_sem)
        self.base = net.used
        net.used += 16

    def start_encoded(self):
        self.encoded = self.net.copy(*self.encoded)
        self.local.start()

    def start(self):
        net, lo = self.net, self.lo
        self.plain = [net.copy(*p) for p in self.plain] + [self.encoded]
        self.copies = []
        for k in range(4):
            for q in range(2):
                by, rows, to, only = pieces(q)[k]
                if only is not None and only != q:
                    continue
                side = 1 if by == 1 else 2
                copy = net.make(
                    self.window.at[pl.ds(to, TOK // 2)],
                    self.back.at[side, lo, rows],
                    net.pair(-by, q),
                    self.base + 4 * k + q,
                    self.base + 4 * k + 2 + lo,
                )
                copy.start()
                self.copies.append(copy)

    def gets(self):
        net = self.net
        for copy in self.plain:
            copy.wait_recv()
        for k in range(4):
            _, rows, _, only = pieces(0)[k]
            for m in range(2):
                copy = net.make(
                    self.window.at[pl.ds(0, TOK // 2)],
                    self.back.at[1, m, rows],
                    net.pair(1, 0),
                    0,
                    self.base + 4 * k + 2 + m,
                )
                if only is None:
                    copy.wait_recv()
                else:
                    pl.when(self.lo == only)(copy.wait_recv)

    def total(self, token_grad):
        lo = self.lo
        half = TOK // 2
        own = self.window[rows_at(HALO + TOK * lo, TOK), :].astype(F32)
        for m in range(2):
            base = jnp.where(lo == m, own, self.back[0, m].astype(F32))
            right = self.back[1, m].astype(F32)
            left = self.back[2, m].astype(F32)
            low = base[:half] + left[:half] + jnp.where(lo == 1, right[:half], 0.0)
            high = base[half:] + right[half:] + jnp.where(lo == 0, left[half:], 0.0)
            token_grad[m] = jnp.concatenate([low, high], axis=0).astype(BF)

    def finish(self):
        self.local.wait()
        for copy in self.copies:
            copy.wait_send()


class Stream:
    SLOTS = 4

    def __init__(self, full, ring, sems):
        wq, wk, wv, wo, wi, wu = full
        self.ring = ring
        self.moves = []
        for n in range(12):
            slot = ring.at[n % self.SLOTS]
            if n < 4:
                pairs = [(wu.at[n], slot)]
            elif n < 8:
                pairs = [
                    (wi.at[n - 4, :, :, :, :, pl.ds(1024 * j, 1024)], slot.at[:, :, :, pl.ds(16 * j, 16)])
                    for j in range(4)
                ]
            else:
                w = (wo, wk, wv, wq)[n - 8]
                pairs = [(w.at[x], slot.at[:, :, :, pl.ds(16 * x, 16)]) for x in range(4)]
            self.moves.append([pltpu.make_async_copy(s, d, sems.at[4 * n + j]) for j, (s, d) in enumerate(pairs)])

    def start(self, n):
        for move in self.moves[n]:
            move.start()

    def wait(self, n):
        for move in self.moves[n]:
            move.wait()

    def part(self, n, j):
        return self.ring[n % self.SLOTS, :, :, :, 16 * j : 16 * j + 16].reshape(256, 1024)


class Backward:
    def __init__(self, ins, outs, scratch):
        self.weights = ins[:6]
        (self.x_in, self.q_in, self.k_in, self.v_in, self.probs_in, self.context_in, self.low_in, self.act_in) = ins[6:14]
        (self.slope_in, self.n1_in, self.inv1_in, self.d_in, self.encoded, self.vec, self.two) = ins[14:]
        self.owned, (self.out, self.token_grad, self.small) = outs[:6], outs[6:]
        take = iter(scratch)
        nxt = lambda n: [next(take) for _ in range(n)]
        (self.ring,) = nxt(1)
        self.g = nxt(6)
        self.bufs = nxt(3 * len(RECTS))
        self.x, self.q, self.k, self.v, self.context, self.low, self.act, self.inner, self.n1, self.inv1, self.d = nxt(11)
        self.outer, self.outer_sib, self.inner_sib, self.branch, self.branch_sib, self.d_context = nxt(6)
        self.dq, self.dk, self.dv, self.dq_sib, self.dk_sib, self.dv_sib, self.dx, self.back = nxt(8)
        self.total, *vector_bufs = nxt(8)
        self.finals, self.ends = nxt(6), nxt(6)
        send_sem, recv_sem, self.local_sem = nxt(3)
        self.net = Net(send_sem, recv_sem)
        self.c = self.net.me["c"]
        self.loads = 0
        self.stream = Stream(self.weights, self.ring, self.local_sem.at[pl.ds(0, 48)])
        self.vectors = VectorSum(self.net, self.total, vector_bufs)
        self.back_rows = Return(self.net, self.dx, self.encoded, self.back, self.out, self.local_sem.at[48])
        lanes = []
        for n, (w, (r0, rows), (base, width), order) in enumerate(RECTS):
            lanes.append(
                Reduce(
                    self.net,
                    self.g[w],
                    pl.ds(r0, rows),
                    pl.ds(base, width),
                    BIG_FIRST[order],
                    self.bufs[3 * n : 3 * n + 3],
                )
            )
        self.lanes = {"u": lanes[:3], "i": lanes[3:6], "o": lanes[6:7], "a": lanes[7:]}

    def load(self, src, dst):
        move = pltpu.make_async_copy(src, dst, self.local_sem.at[49 + self.loads])
        self.loads += 1
        move.start()
        return move

    def half(self, which, width):
        return columns(which * width, width)

    def share(self, src, dst, width):
        return self.net.copy(src.at[:, self.half(1 - self.c, width)], dst, self.net.ring("c", 0))

    def begin(self):
        self.at_d = self.load(self.d_in, self.d)
        for n in range(4):
            self.stream.start(n)
        self.at_slope = self.load(self.slope_in, self.inner)
        self.at_act = self.load(self.act_in, self.act)
        self.at_low = self.load(self.low_in, self.low)
        self.at_n1 = [self.load(self.n1_in, self.n1), self.load(self.inv1_in, self.inv1)]
        self.at_rest = [
            self.load(self.context_in, self.context),
            self.load(self.x_in, self.x),
            self.load(self.q_in, self.q),
            self.load(self.k_in, self.k),
            self.load(self.v_in, self.v),
        ]
        self.total[...] = jnp.zeros((16, D), F32)
        self.total[G2 : G2 + 2, :] = self.two[0:2, :]
        self.at_d.wait()

        def body(t, carry):
            r = some_rows(t)
            low = self.d[r, :].astype(BF)
            self.outer[r, :] = low
            return carry + jnp.sum(low.astype(F32).reshape(ROWS // 8, 8, D), axis=0)

        s = lax.fori_loop(0, OWN // ROWS, body, jnp.zeros((8, D), F32))
        self.total[BU : BU + 1, :] = jnp.sum(s, axis=0, keepdims=True)
        self.net.barrier()
        self.got_outer = self.share(self.outer, self.outer_sib, 512)
        self.back_rows.start_encoded()

    def d_inner(self):
        self.at_slope.wait()
        for n in range(4):
            self.stream.wait(n)

            def body(lo, carry, n=n):
                at = n * 1024 + lo * 512
                cols = columns(at, 512)
                y = mm(self.outer[...], self.ring[n, lo].reshape(512, 1024), NT)
                y = (y * self.inner[:, cols].astype(F32)).astype(BF)
                self.inner[:, cols] = y
                s = column_sum(y)
                for j in range(4):
                    dp, t = 2 * n + lo, j
                    self.total[8 + t : 9 + t, columns(dp * 128, 128)] = s[:, 128 * j : 128 * j + 128]
                return carry

            lax.fori_loop(0, 2, body, 0)
            self.stream.start(n + 4)
        self.got_inner = self.share(self.inner, self.inner_sib, 2048)

    def grad_outer(self):
        self.at_act.wait()
        self.got_outer.wait_recv()
        c = self.c
        mine = self.outer.at[:, self.half(c, 512)]

        def body(t, carry):
            cols = columns(t * 512, 512)
            y = mm(self.act[c, :, cols], mine[...], TN) + mm(self.act[1 - c, :, cols], self.outer_sib[...], TN)
            self.g[5][lax.div(t, 2), lax.rem(t, 2)] = y.astype(BF).reshape(2, 4, 64, 512)
            return carry

        lax.fori_loop(0, 8, body, 0)
        self.at_probs = self.load(self.probs_in, self.act)

    def d_normed(self):
        for n in range(4):
            self.stream.wait(4 + n)
            cols = slice(256 * n, 256 * n + 256)
            y = self.d[:, cols]
            for j in range(4):
                y = y + mm(self.inner[:, 1024 * j : 1024 * j + 1024], self.stream.part(4 + n, j), NT)
            self.d[:, cols] = y
            self.stream.start(8 + n)

    def grad_inner(self):
        self.at_low.wait()
        self.got_inner.wait_recv()
        c = self.c

        def body(t, carry):
            x, j = lax.div(t, 4), lax.rem(t, 4)
            rows, cols = columns(x * 256, 256), columns(j * 512, 512)
            y = mm(self.low[c, :, rows], self.inner[:, columns(c * 2048 + j * 512, 512)], TN)
            y = y + mm(self.low[1 - c, :, rows], self.inner_sib[:, cols], TN)
            self.g[4][x, :, :, :, :, cols] = y.astype(BF).reshape(2, 2, 4, 16, 512)
            return carry

        lax.fori_loop(0, 16, body, 0)

    def norm_one(self):
        for move in self.at_n1:
            move.wait()

        def body(t, carry):
            r = some_rows(t)
            d, n = self.d[r, :], self.n1[r, :]
            da = norm_back(d * self.vec[G1 : G1 + 1, :], n, self.inv1[r, :1])
            low = da.astype(BF)
            self.d[r, :] = da
            self.branch[r, :] = low
            new = (d * n, d, low.astype(F32))
            return tuple(a + jnp.sum(b.reshape(ROWS // 8, 8, D), axis=0) for a, b in zip(carry, new))

        zero = jnp.zeros((8, D), F32)
        sums = lax.fori_loop(0, OWN // ROWS, body, (zero, zero, zero))
        for row, s in zip((G1, S1, BO), sums):
            self.total[row : row + 1, :] = jnp.sum(s, axis=0, keepdims=True)
        self.got_branch = self.share(self.branch, self.branch_sib, 512)

    def d_mixed(self):
        self.stream.wait(8)
        for x in range(4):
            self.d_context[:, 256 * x : 256 * x + 256] = mm(self.branch[...], self.stream.part(8, x), NT).astype(BF)

    def grad_rows(self, left, right, sib, out):
        mine = right.at[:, self.half(self.c, 512)]

        def body(x, carry):
            rows = columns(x * 256, 256)
            y = mm(left[0][:, rows], mine[...], TN) + mm(left[1][:, rows], sib[...], TN)
            out[x] = y.astype(BF).reshape(2, 2, 4, 16, 512)
            return carry

        lax.fori_loop(0, 4, body, 0)

    def pair(self, ref):
        return ref.at[self.c], ref.at[1 - self.c]

    def grad_output(self):
        self.got_branch.wait_recv()
        for move in self.at_rest:
            move.wait()
        self.grad_rows(self.pair(self.context), self.branch, self.branch_sib, self.g[3])

    def attend(self, first, last):
        if first == 0:
            self.at_probs.wait()
        attention_back(
            self.q,
            self.k,
            self.v,
            self.act,
            self.context.at[self.c],
            self.d_context,
            self.dq,
            self.dk,
            self.dv,
            first,
            last,
        )

    def share_heads(self):
        self.got_heads = [
            self.share(self.dk, self.dk_sib, 512),
            self.share(self.dv, self.dv_sib, 512),
            self.share(self.dq, self.dq_sib, 512),
        ]
        self.total[BQ : BQ + 1, :] = column_sum(self.dq[...])
        self.total[BV : BV + 1, :] = column_sum(self.dv[...])
        self.vectors.start()

    def grad_key(self):
        self.got_heads[0].wait_recv()
        self.grad_rows(self.pair(self.x), self.dk, self.dk_sib, self.g[1])

    def grad_value(self):
        self.got_heads[1].wait_recv()
        self.grad_rows(self.pair(self.x), self.dv, self.dv_sib, self.g[2])

    def grad_query(self):
        self.got_heads[2].wait_recv()
        own = pl.ds(HALO, OWN)
        rows = (self.x.at[self.c, own], self.x.at[1 - self.c, own])
        self.grad_rows(rows, self.dq, self.dq_sib, self.g[0])

    def d_tokens(self):
        for n in (9, 10, 11):
            self.stream.wait(n)
        for x in range(4):
            cols = slice(256 * x, 256 * x + 256)
            y = mm(self.dk[...], self.stream.part(9, x), NT) + mm(self.dv[...], self.stream.part(10, x), NT)
            own = self.d[:, cols] + mm(self.dq[...], self.stream.part(11, x), NT)
            self.dx[:HALO, cols] = y[:HALO].astype(BF)
            self.dx[HALO : HALO + OWN, cols] = (y[HALO : HALO + OWN] + own).astype(BF)
            self.dx[HALO + OWN :, cols] = y[HALO + OWN :].astype(BF)
        self.back_rows.start()

    def finish(self):
        c, net = self.c, self.net
        done = [lane for group in ("u", "i", "o", "a") for lane in self.lanes[group]]
        swaps = []
        rects = list(zip(done, RECTS))
        for w in (5, 4, 3, 0, 1, 2):
            final, end = self.finals[w], self.ends[w]
            for lane, (of, (r0, rows), (base, width), _) in rects:
                if of == w:
                    final[pl.ds(r0, rows), pl.ds(base, width)] = lane.result()
            n, width = final.shape[0] // 2, final.shape[1]
            kept = final.at[pl.ds(pl.multiple_of(n * c, 8), n)]
            given = final.at[pl.ds(pl.multiple_of(n * (1 - c), 8), n)]
            swaps.append((w, net.copy(given, end.at[:, columns(c * width, width)], net.ring("c", 0))))
            end[:, columns(c * width, width)] = kept[...]
        self.back_rows.gets()
        self.back_rows.total(self.token_grad)
        self.vectors.done(self.small)
        stores = []
        for w, swap in swaps:
            swap.wait_recv()
            stores.append(self.load(self.ends[w], self.owned[w]))
        for store in stores:
            store.wait()
        self.back_rows.finish()
        net.finish()


BACK = (
    "begin", "d_inner", "grad_outer", "u.p1", "d_normed", "u.p1_mid", "grad_inner", "i.p1", "norm_one",
    "d_mixed", "u.p2", "i.p1_mid", "grad_output", "o.p1", "attend.0.3", "u.p3", "i.p2", "attend.3.6",
    "o.p1_mid", "i.p3", "attend.6.8", "share_heads", "d_tokens", "grad_key", "grad_value", "grad_query",
    "a.p1", "vectors.along_x", "o.p2", "vectors.along_y", "a.p1_mid", "o.p3", "vectors.along_z", "a.p2",
    "a.p3", "finish",
)


def run_steps(work, steps):
    for step in steps:
        name, *rest = step.split(".")
        if name in work.lanes:
            each(work.lanes[name], rest[0])
        elif name == "vectors":
            getattr(work.vectors, rest[0])()
        else:
            getattr(work, name)(*map(int, rest))


def backward_kernel(*refs):
    run_steps(Backward(refs[:21], refs[21:30], refs[30:]), BACK)


def backward_all(kept):
    any_space = pl.BlockSpec(memory_space=pl.ANY)
    vmem = pl.BlockSpec(memory_space=pltpu.VMEM)
    owned = [(r // 2, n) for r, n in BLOCKS]
    scratch = [((4, 2, 2, 4, 64, 1024), BF)]
    scratch += [(CHIPS + (r, n // 2), BF) for r, n in BLOCKS]
    scratch += [(s, BF) for s in reduce_buffers()]
    scratch += [((2, WIN, D), BF), ((OWN, D), BF), ((WIN, D), BF), ((WIN, D), BF), ((2, OWN, D), BF), ((2, OWN, D), BF)]
    scratch += [((2, OWN, FF), BF), ((OWN, FF), BF), ((OWN, D), F32), ((OWN, 128), F32), ((OWN, D), F32)]
    scratch += [((OWN, D), BF), ((OWN, 512), BF), ((OWN, 2048), BF), ((OWN, D), BF), ((OWN, 512), BF), ((OWN, D), BF)]
    scratch += [((OWN, D), BF), ((WIN, D), BF), ((WIN, D), BF), ((OWN, 512), BF), ((WIN, 512), BF), ((WIN, 512), BF)]
    scratch += [((WIN, D), BF), ((3, 2, TOK, D), BF)]
    scratch += [((16, D), F32), ((16, D), F32), ((16, D), F32), ((3, 16, 256), F32), ((2, 16, 128), F32), ((3, 16, 128), F32)]
    scratch += [((16, 128), F32), ((3, 16, 128), F32)]
    scratch += [((r, n // 2), F32) for r, n in BLOCKS] + [(s, F32) for s in owned]
    return pl.pallas_call(
        backward_kernel,
        name="backward_all",
        out_shape=[jax.ShapeDtypeStruct(s, F32) for s in owned]
        + [jax.ShapeDtypeStruct((2, TOK, D), BF)] * 2
        + [jax.ShapeDtypeStruct((8, 128), F32)],
        in_specs=[any_space] * 19 + [vmem] * 2,
        out_specs=[any_space] * 7 + [vmem] * 2,
        scratch_shapes=[pltpu.VMEM(s, t) for s, t in scratch]
        + [
            pltpu.SemaphoreType.DMA((N_SEM,)),
            pltpu.SemaphoreType.DMA((N_SEM,)),
            pltpu.SemaphoreType.DMA((80,)),
        ],
        compiler_params=pltpu.CompilerParams(collective_id=2, has_side_effects=True, vmem_limit_bytes=63 << 20),
    )(*kept)


def local(
    tokens, cotangent, seq_lengths, block_offsets, deal_order, wq, wk, wv, wo, bq, bv, bo, g1, s1, wi, bi, wu, bu, g2, s2
):
    small = jnp.pad(jnp.concatenate([bq, bv, bo, g1, s1, bu, g2, s2, bi]), (0, 32))[None]
    kept = forward_all(
        tokens[:, 0], cotangent[:, 0], seq_lengths[:, 0], deal_order[:, 0], small, (wq, wk, wv, wo, wi, wu)
    )
    *owned, out, token_grad, sums = backward_all(kept)
    mine = sums[0]
    sbq, sbv, sbo, sg1, ss1, sbu, sg2, ss2 = [mine[8 * j : 8 * j + 8] for j in range(8)]
    return (
        out[:, None],
        token_grad[:, None],
        *owned[:4],
        sbq,
        sbv,
        sbo,
        sg1,
        ss1,
        owned[4],
        mine[64:96],
        owned[5],
        sbu,
        sg2,
        ss2,
    )


def solution(mesh):
    rows = P(None, "shard", "dp", None)
    table = P(None, "shard", None)
    matrix, vector = P(("dp", "shard"), None), P(("dp", "shard"))
    in_specs = (rows, rows) + (table,) * 3 + (matrix,) * 4 + (vector,) * 5 + (matrix, vector, matrix) + (vector,) * 3
    out_specs = (rows, rows) + (matrix,) * 4 + (vector,) * 5 + (matrix, vector, matrix) + (vector,) * 3
    return jax.shard_map(local, mesh=mesh, in_specs=in_specs, out_specs=out_specs, check_vma=False)
```

```python
import math

import jax
import jax.numpy as jnp
from jax import lax
from jax.experimental import pallas as pl
from jax.experimental.pallas import tpu as pltpu
from jax.sharding import PartitionSpec as P

MESH = pl.DeviceIdType.MESH
BF = jnp.bfloat16
F32 = jnp.float32
D = 1024
FF = 4096
HEADS = 16
HEAD = 64
TOK = 128
OWN = 2 * TOK
HALO = 192
WIN = OWN + 2 * HALO
AXES = ("x", "y", "z")
ORDER = (("z", "y", "x"), ("x", "z", "y"), ("y", "x", "z"))
CHIPS = (4, 2, 2, 4)
N_SEM = 200


def position():
    dp, sh = lax.axis_index("dp"), lax.axis_index("shard")
    return {
        "x": lax.div(dp, 2),
        "y": lax.div(sh, 8) * 2 + lax.rem(dp, 2),
        "z": lax.div(lax.rem(sh, 8), 2),
        "c": lax.rem(sh, 2),
    }


def device_at(at):
    return (
        at["x"] * 2 + lax.rem(at["y"], 2),
        lax.div(at["y"], 2) * 8 + at["z"] * 2 + at["c"],
    )


class Net:
    def __init__(self, send_sem, recv_sem):
        self.me = position()
        self.send_sem, self.recv_sem = send_sem, recv_sem
        self.used = 0
        self.sent = []

    def moved(self, axis, by):
        at = dict(self.me)
        if axis == "c":
            at["c"] = 1 - at["c"]
        else:
            at[axis] = lax.rem(at[axis] + by, 4)
        return at

    def ring(self, axis, by):
        return device_at(self.moved(axis, by))

    def pair(self, lo):
        at = dict(self.me)
        at["y"] = lax.div(at["y"], 2) * 2 + lo
        return device_at(at)

    def copy(self, src, dst, device):
        k = self.used
        self.used += 1
        moved = pltpu.make_async_remote_copy(
            src_ref=src,
            dst_ref=dst,
            send_sem=self.send_sem.at[k],
            recv_sem=self.recv_sem.at[k],
            device_id=device,
            device_id_type=MESH,
        )
        moved.start()
        self.sent.append(moved)
        return moved

    def greet(self):
        bar = pltpu.get_barrier_semaphore()
        peers = [self.ring("c", 0)] + [self.ring(a, b) for a in AXES for b in (1, 2, 3)]
        for p in peers:
            pl.semaphore_signal(bar, inc=1, device_id=p, device_id_type=MESH)
        return lambda: pl.semaphore_wait(bar, len(peers))

    def finish(self):
        for moved in self.sent:
            moved.wait_send()
        assert self.used <= N_SEM, self.used


def chip_index(at, drop=()):
    out = []
    for axis in AXES:
        if axis in drop:
            continue
        v = at[axis]
        if axis == "y":
            if v is None:
                out += [slice(None), slice(None)]
            elif isinstance(v, tuple):
                out += [v[1], slice(None)]
            else:
                out += [lax.rem(v, 2), lax.div(v, 2)]
        elif v is None:
            out.append(slice(None))
        elif isinstance(v, tuple):
            out.append(pl.ds(2 * v[1], 2))
        else:
            out.append(v)
    return tuple(out)


def chip_shape(drop):
    shape = ()
    for axis in AXES:
        if axis not in drop:
            shape += (2, 2) if axis == "y" else (4,)
    return shape


def columns(base, width):
    return pl.ds(pl.multiple_of(base, 128), width)


class Gather:
    def __init__(self, net, ref, rows, cols, order):
        self.net, self.ref, self.rows, self.cols = net, ref, rows, cols
        self.a, self.b, self.e = order

    def at(self, **over):
        place = {k: self.net.me[k] for k in AXES}
        place.update(over)
        return self.ref.at[chip_index(place) + (self.rows, self.cols)]

    def send(self, region, axis, by):
        return self.net.copy(region, region, self.net.ring(axis, by))

    def p1(self):
        self.c = [self.send(self.at(), self.a, d) for d in (1, 3, 2)]

    def p2(self):
        for moved in self.c:
            moved.wait_recv()
        self.c = [self.send(self.at(**{self.a: None}), self.b, d) for d in (1, 3, 2)]

    def p2_ring(self):
        for moved in self.c:
            moved.wait_recv()
        self.c = [self.send(self.at(**{self.a: None}), self.b, d) for d in (1, 3)]

    def p2_mid(self):
        for h, (moved, to) in enumerate(zip(self.c, (1, 3))):
            moved.wait_recv()
            b = self.net.moved(self.b, 4 - to)[self.b]
            self.c.append(self.send(self.at(**{self.a: ("half", h), self.b: b}), self.b, to))
        self.c = self.c[2:]

    def part(self, h, by):
        e = self.net.moved(self.e, by)[self.e]
        return self.at(**{self.a: h if h is None else ("half", h), self.b: None, self.e: e})

    def p3(self):
        for moved in self.c:
            moved.wait_recv()
        self.r0 = self.send(self.part(0, 0), self.e, 1)
        self.l1 = self.send(self.part(1, 0), self.e, 3)
        self.r1 = self.send(self.part(1, 0), self.e, 1)
        self.l0 = self.send(self.part(0, 0), self.e, 3)
        self.core = [self.send(self.part(None, 0), "c", 0)]

    def p3_mid(self):
        self.r0.wait_recv()
        self.f0 = self.send(self.part(0, 3), self.e, 1)
        self.l1.wait_recv()
        self.f1 = self.send(self.part(1, 1), self.e, 3)

    def p3_core(self):
        self.r1.wait_recv()
        self.core.append(self.send(self.part(None, 3), "c", 0))
        self.l0.wait_recv()
        self.core.append(self.send(self.part(None, 1), "c", 0))

    def p3_end(self):
        self.f0.wait_recv()
        self.f1.wait_recv()
        self.core.append(self.send(self.part(None, 2), "c", 0))

    def done(self):
        for moved in self.core:
            moved.wait_recv()


def each(lanes, step):
    for lane in lanes:
        getattr(lane, step)()


def rows_at(base, count):
    return pl.ds(pl.multiple_of(base, TOK // 2), count)


class Window:
    def __init__(self, net, tokens, cotangent, window, cots, local_sem):
        self.net, self.window, self.cots = net, window, cots
        self.tokens, self.cotangent, self.local_sem = tokens, cotangent, local_sem
        self.lo = lax.rem(net.me["y"], 2)

    def pair(self, src, dst, sem):
        local = pltpu.make_async_copy(src.at[self.lo], dst, sem)
        local.start()
        return local, self.net.copy(src.at[1 - self.lo], dst, self.net.pair(1 - self.lo))

    def start(self):
        mine = self.window.at[rows_at(HALO + TOK * self.lo, TOK)]
        self.rows = self.pair(self.tokens, mine, self.local_sem.at[0])

    def start_cots(self):
        mine = self.cots.at[rows_at(TOK * self.lo, TOK)]
        self.cot_rows = self.pair(self.cotangent, mine, self.local_sem.at[1])

    def halo(self):
        local, moved = self.rows
        local.wait()
        moved.wait_recv()
        w, net = self.window, self.net
        self.c = [
            net.copy(w.at[pl.ds(OWN, HALO)], w.at[pl.ds(0, HALO)], net.ring("x", 1)),
            net.copy(w.at[pl.ds(HALO, HALO)], w.at[pl.ds(HALO + OWN, HALO)], net.ring("x", 3)),
        ]

    def done(self):
        for moved in self.c:
            moved.wait_recv()

    def cots_done(self):
        local, moved = self.cot_rows
        local.wait()
        moved.wait_recv()


def place_own(me, mine, peer, full):
    here = chip_index(me)
    c = me["c"]
    first = c == 0

    def both(a, b):
        return jnp.concatenate([jnp.where(first, a, b), jnp.where(first, b, a)], axis=0)

    half = columns(c * 512, 512)
    for j in range(4):
        r = slice(8 * j, 8 * j + 8)
        full[j][here + (slice(None), half)] = both(mine[r, half], peer[r, half])
    for t in range(2):
        r, s = slice(32 + 8 * t, 40 + 8 * t), slice(48 + 8 * t, 56 + 8 * t)
        a = jnp.where(first, mine[r, :], mine[s, :])
        b = jnp.where(first, peer[r, :], peer[s, :])
        full[4][here + (slice(None), columns(c * 2048 + 1024 * t, 1024))] = both(a, b)
    full[5][here + (slice(None), half)] = both(mine[64:96, half], peer[64:96, half])


BLOCKS = ((16, 1024),) * 4 + ((16, 4096), (64, 1024))


SPAN = TOK + 2 * HALO
NT = (((1,), (1,)), ((), ()))
TN = (((0,), (0,)), ((), ()))
NN = (((1,), (0,)), ((), ()))


def mm(a, b, dims=NN):
    return lax.dot_general(a, b, dims, preferred_element_type=F32)


def tile(w, n0, n):
    return w[:, :, :, :, :, columns(n0, n)].reshape(-1, n)


def project(rows, w, out, bias=None, n=512):
    def body(t, carry):
        cols = columns(t * n, n)
        y = mm(rows[...], tile(w, t * n, n))
        if bias is not None:
            y = y + bias[:, cols]
        out[:, cols] = y.astype(BF)
        return carry

    lax.fori_loop(0, out.shape[1] // n, body, 0)


def lane_split(x):
    low = lax.broadcasted_iota(jnp.int32, x.shape, 1) < HEAD
    zero = jnp.zeros_like(x)
    return jnp.concatenate([jnp.where(low, x, zero), jnp.where(low, zero, x)], axis=0)


def lane_join(x):
    n = x.shape[0] // 2
    low = lax.broadcasted_iota(jnp.int32, (n, x.shape[1]), 1) < HEAD
    return jnp.where(low, x[:n], x[n:])


def attention(q, k, v, bias, probs, context, first, last):
    def body(h, carry):
        cols = columns(h * 128, 128)
        for b in range(2):
            mine, near = pl.ds(b * TOK, TOK), pl.ds(b * TOK, SPAN)
            pen = bias[b]
            s = mm(k[near, cols], lane_split(q[mine, cols]), NT) * 0.125 + jnp.concatenate([pen, pen], axis=1)
            e = jnp.exp(s - jnp.max(s, axis=0, keepdims=True))
            p = (e * (1.0 / jnp.sum(e, axis=0, keepdims=True))).astype(BF)
            at = columns((2 * h + b) * OWN, OWN)
            probs[0, :, at], probs[1, :, at] = p[:OWN], p[OWN:]
            y = mm(v[near, cols], p, TN)
            y = jnp.concatenate([y[:HEAD, :TOK], y[HEAD:, TOK:]], axis=0)
            context[mine, cols] = y.T.astype(BF)
        return carry

    lax.fori_loop(first, last, body, 0)


def normalized(a):
    centred = a - jnp.mean(a, axis=-1, keepdims=True)
    inv = lax.rsqrt(jnp.mean(centred * centred, axis=-1, keepdims=True) + 1e-05)
    return centred * inv, inv


def norm_back(dn, n, inv):
    return inv * (dn - jnp.mean(dn, axis=-1, keepdims=True) - n * jnp.mean(dn * n, axis=-1, keepdims=True))


def feed_in(low, wi, bi, act, slope, first, last, n=512):
    def body(t, carry):
        cols = columns(t * n, n)
        u = mm(low[...], tile(wi, t * n, n)) + bi[:, cols]
        phi = 0.5 + 0.5 * lax.erf(u * math.sqrt(0.5))
        act[:, cols] = (u * phi).astype(BF)
        slope[:, cols] = (phi + u * (jnp.exp(-0.5 * (u * u)) * (1.0 / math.sqrt(2 * math.pi)))).astype(BF)
        return carry

    lax.fori_loop(first, last, body, 0)


ROWS = 32


def some_rows(t):
    return pl.ds(pl.multiple_of(t * ROWS, ROWS), ROWS)


def segment_bias(lengths, order, start, lo, bias):
    ends, total = [], 0
    for k in range(16):
        total = total + lengths[lo, order[lo, k]]
        ends.append(total)

    def which(at):
        found = jnp.where(at < 0, -1, 0)
        for e in ends:
            found = found + (at >= e).astype(jnp.int32)
        return found

    keys = which(start + lax.broadcasted_iota(jnp.int32, (WIN, TOK), 0))
    queries = which(start + HALO + lax.broadcasted_iota(jnp.int32, (8, OWN), 1))[:1]
    for b in range(2):
        same = keys[b * TOK : b * TOK + SPAN] == queries[:, b * TOK : b * TOK + TOK]
        bias[b] = jnp.where(same, 0.0, -1e30)


class Vectors:
    def __init__(self, net, small, rows, tiles, vec, inner):
        self.net, self.small, self.rows = net, small, rows
        self.own, self.sib, self.tz, self.ty, self.tx = tiles
        self.vec, self.inner = vec, inner

    def around(self, axis, block):
        return [self.net.copy(block, block, self.net.ring(axis, d)) for d in (1, 3, 2)]

    def start(self):
        sh = lax.axis_index("shard")
        self.rows[...] = jnp.zeros((16, 128), F32)
        for j in range(9):
            n = self.small[j].shape[1]
            self.rows[j : j + 1, :n] = self.small[j][...].astype(F32)
        i = lax.broadcasted_iota(jnp.int32, (128, 128), 0)
        to = lax.broadcasted_iota(jnp.int32, (128, 128), 1)
        value = self.rows[...].astype(BF)
        eight = mm(value, jnp.where((to == 8 * sh + i) & (i < 8), 1.0, 0.0).astype(BF))
        many = mm(value, jnp.where((to == 32 * lax.rem(sh, 4) + i) & (i < 32), 1.0, 0.0).astype(BF))
        r = lax.broadcasted_iota(jnp.int32, (16, 128), 0)
        many = jnp.broadcast_to(many[8:9], (16, 128))
        tile = jnp.where(r < 8, eight, jnp.where(r == 8 + lax.div(sh, 4), many, 0.0))
        self.own[...] = tile.astype(BF)
        self.c = [self.net.copy(self.own, self.sib, self.net.ring("c", 0))]

    def wait(self):
        for moved in self.c:
            moved.wait_recv()

    def along_z(self):
        self.wait()
        z = self.net.me["z"]
        self.tz[z] = self.own[...] + self.sib[...]
        self.c = self.around("z", self.tz.at[z])

    def along_y(self):
        self.wait()
        y = self.net.me["y"]
        self.ty[y] = (self.tz[0] + self.tz[1]) + (self.tz[2] + self.tz[3])
        self.c = self.around("y", self.ty.at[y])

    def along_x(self):
        self.wait()
        x = self.net.me["x"]
        self.tx[x, 0] = self.ty[0] + self.ty[2]
        self.tx[x, 1] = self.ty[1] + self.ty[3]
        self.c = self.around("x", self.tx.at[x])

    def done(self):
        self.wait()
        for dp in range(8):
            got = self.tx[dp // 2, dp % 2].astype(F32)
            self.vec[:, 128 * dp : 128 * dp + 128] = got[:8]
            for t in range(4):
                at = 512 * dp + 128 * t
                self.inner[:, at : at + 128] = got[8 + t : 9 + t]


BQ, BV, BO, G1, S1, BU, G2, S2 = range(8)


class Forward:
    def __init__(self, ins, outs, scratch):
        self.tokens, self.cotangent, self.lengths, self.order = ins[:4]
        self.own, self.small = ins[4:10], ins[10:]
        self.weights_out = outs[:6]
        (self.x_out, self.q_out, self.k_out, self.v_out, self.probs_out, self.context_out, self.low_out) = outs[6:13]
        (self.act_out, self.slope_out, self.n1_out, self.inv1_out, self.d_out, self.encoded_out) = outs[13:19]
        self.vec_out, self.two_out = outs[19:]
        self.mine, self.peer = scratch[:2]
        self.full, scratch = scratch[2:8], scratch[8:]
        (self.window, self.cots, self.q, self.k, self.v, self.probs, self.context, self.low) = scratch[:8]
        (self.act, self.slope, self.bias, self.n1, self.inv1, self.normed, self.total, self.encoded) = scratch[8:16]
        self.vec, self.inner, self.two, self.placed = scratch[16:20]
        tiles, (send_sem, recv_sem, self.local_sem) = scratch[20:25], scratch[25:]
        self.net = Net(send_sem, recv_sem)
        self.me, self.c = self.net.me, self.net.me["c"]
        self.lo = lax.rem(self.me["y"], 2)
        self.stores, self.gets = [], []
        self.vectors = Vectors(self.net, self.small, self.placed, tiles, self.vec, self.inner)
        self.view = Window(self.net, self.tokens, self.cotangent, self.window, self.cots, self.local_sem)
        rows, half = slice(None), columns(self.c * 512, 512)
        wi, wu = self.full[4], self.full[5]

        def inner(base, width, order):
            return Gather(self.net, wi, rows, columns(self.c * 2048 + base, width), ORDER[order])

        self.lanes = {
            "a": [Gather(self.net, self.full[j], rows, half, ORDER[j]) for j in range(3)],
            "b": [Gather(self.net, self.full[3], rows, half, ORDER[2]), inner(0, 1024, 1), inner(1024, 1024, 2)],
            "u": [
                Gather(self.net, wu, pl.ds(0, 32), half, ORDER[0]),
                Gather(self.net, wu, pl.ds(32, 16), half, ORDER[1]),
                Gather(self.net, wu, pl.ds(48, 16), half, ORDER[2]),
            ],
        }

    def store(self, src, dst):
        move = pltpu.make_async_copy(src, dst, self.local_sem.at[2 + len(self.stores)])
        move.start()
        self.stores.append(move)

    def both(self, src, dst):
        self.gets.append(self.net.copy(src, dst.at[self.c], self.net.ring("c", 0)))
        self.store(src, dst.at[self.c])

    def begin(self):
        greeted = self.net.greet()
        for j in range(4):
            self.mine[8 * j : 8 * j + 8, :] = self.own[j][...]
            self.mine[32 + 8 * j : 40 + 8 * j, :] = self.own[4][:, 1024 * j : 1024 * j + 1024]
        self.mine[64:96, :] = self.own[5][...]
        greeted()
        swap = self.net.copy(self.mine, self.peer, self.net.ring("c", 0))
        self.view.start()
        self.vectors.start()
        swap.wait_recv()
        place_own(self.me, self.mine, self.peer, self.full)

    def halo(self):
        self.view.halo()

    def cots_in(self):
        self.view.start_cots()

    def masks(self):
        segment_bias(self.lengths, self.order, self.me["x"] * OWN - HALO, self.lo, self.bias)

    def rows_done(self):
        self.view.done()
        self.both(self.window, self.x_out)

    def query(self):
        project(self.window.at[pl.ds(HALO, OWN)], self.full[0], self.q, self.vec.at[BQ : BQ + 1])

    def key(self):
        project(self.window, self.full[1], self.k)

    def value(self):
        project(self.window, self.full[2], self.v, self.vec.at[BV : BV + 1])

    def keep_heads(self):
        for j in range(3):
            self.store(self.full[j], self.weights_out[j])
        for src, dst in ((self.q, self.q_out), (self.k, self.k_out), (self.v, self.v_out)):
            self.store(src, dst)

    def attend(self, first, last):
        attention(self.q, self.k, self.v, self.bias, self.probs, self.context, first, last)

    def keep_probs(self):
        self.both(self.context, self.context_out)
        self.store(self.probs, self.probs_out)

    def mix(self):
        self.store(self.full[3], self.weights_out[3])
        self.store(self.full[4], self.weights_out[4])

        def body(t, carry):
            cols = columns(t * 512, 512)
            y = mm(self.context[...], tile(self.full[3], t * 512, 512)) + self.vec[BO : BO + 1, cols]
            self.total[:, cols] = y + self.window[pl.ds(HALO, OWN), cols].astype(F32)
            return carry

        lax.fori_loop(0, 2, body, 0)

    def norm_one(self):
        def body(t, carry):
            r = some_rows(t)
            n, inv = normalized(self.total[r, :])
            self.n1[r, :] = n
            self.inv1[r, :] = jnp.broadcast_to(inv, (ROWS, 128))
            y = n * self.vec[G1 : G1 + 1, :] + self.vec[S1 : S1 + 1, :]
            self.normed[r, :] = y
            self.low[r, :] = y.astype(BF)
            return carry

        lax.fori_loop(0, OWN // ROWS, body, 0)
        self.both(self.low, self.low_out)
        self.store(self.n1, self.n1_out)
        self.store(self.inv1, self.inv1_out)

    def feed_in(self, first, last):
        feed_in(self.low, self.full[4], self.inner, self.act, self.slope, first, last)
        if last == FF // 512:
            self.both(self.act, self.act_out)
            self.store(self.slope, self.slope_out)
            self.store(self.vec, self.vec_out)

    def feed_out(self):
        self.store(self.full[5], self.weights_out[5])

        def body(t, carry):
            cols = columns(t * 512, 512)
            y = mm(self.act[...], tile(self.full[5], t * 512, 512)) + self.vec[BU : BU + 1, cols]
            self.total[:, cols] = y + self.normed[:, cols]
            return carry

        lax.fori_loop(0, 2, body, 0)

    def cots_done(self):
        self.view.cots_done()

    def norm_two(self):
        def body(t, carry):
            r = some_rows(t)
            n, inv = normalized(self.total[r, :])
            gain = self.vec[G2 : G2 + 1, :]
            self.encoded[r, :] = (n * gain + self.vec[S2 : S2 + 1, :]).astype(BF)
            d = self.cots[r, :].astype(F32)
            self.normed[r, :] = norm_back(d * gain, n, inv)
            dn = jnp.sum((d * n).reshape(ROWS // 8, 8, D), axis=0)
            return carry[0] + dn, carry[1] + jnp.sum(d.reshape(ROWS // 8, 8, D), axis=0)

        zero = jnp.zeros((8, D), F32)
        gain_sum, shift_sum = lax.fori_loop(0, OWN // ROWS, body, (zero, zero))
        self.two[0:1, :] = jnp.sum(gain_sum, axis=0, keepdims=True)
        self.two[1:2, :] = jnp.sum(shift_sum, axis=0, keepdims=True)
        self.two[2:8, :] = jnp.zeros((6, D), F32)
        self.store(self.normed, self.d_out)
        self.store(self.encoded, self.encoded_out)
        self.store(self.two, self.two_out)

    def finish(self):
        for got in self.gets:
            got.wait_recv()
        for move in self.stores:
            move.wait()
        self.net.finish()


FORE = (
    "begin", "a.p1", "b.p1", "u.p1", "vectors.along_z", "masks", "a.p2", "b.p2", "vectors.along_y", "a.p3",
    "u.p2", "halo", "vectors.along_x", "a.p3_mid", "b.p3", "a.p3_core", "a.p3_end", "vectors.done", "u.p3",
    "cots_in", "a.done", "query", "rows_done", "key", "b.p3_mid", "value", "keep_heads", "attend.0.2",
    "b.p3_core", "attend.2.4", "b.p3_end", "u.p3_mid", "attend.4.6", "u.p3_core", "attend.6.8", "keep_probs",
    "b.done", "mix", "norm_one", "feed_in.0.4", "u.p3_end", "feed_in.4.8", "u.done", "feed_out", "cots_done",
    "norm_two", "finish",
)


def run_steps(work, steps):
    for step in steps:
        name, *rest = step.split(".")
        if name in work.lanes:
            each(work.lanes[name], rest[0])
        elif name == "vectors":
            getattr(work.vectors, rest[0])()
        else:
            getattr(work, name)(*map(int, rest))


def forward_kernel(*refs):
    run_steps(Forward(refs[:19], refs[19:40], refs[40:]), FORE)


def forward_all(tokens, cotangent, lengths, order, own, small):
    any_space = pl.BlockSpec(memory_space=pl.ANY)
    vmem = pl.BlockSpec(memory_space=pltpu.VMEM)
    smem = pl.BlockSpec(memory_space=pltpu.SMEM)
    full = [(CHIPS + s, BF) for s in BLOCKS]
    kept = [
        ((2, WIN, D), BF),
        ((OWN, D), BF),
        ((WIN, D), BF),
        ((WIN, D), BF),
        ((2, OWN, FF), BF),
        ((2, OWN, D), BF),
        ((2, OWN, D), BF),
        ((2, OWN, FF), BF),
        ((OWN, FF), BF),
        ((OWN, D), F32),
        ((OWN, 128), F32),
        ((OWN, D), F32),
        ((OWN, D), BF),
        ((8, D), F32),
        ((8, D), F32),
    ]
    scratch = [((96, 1024), BF)] * 2 + full
    scratch += [((WIN, D), BF), ((OWN, D), BF), ((OWN, D), BF), ((WIN, D), BF), ((WIN, D), BF)]
    scratch += [((2, OWN, FF), BF), ((OWN, D), BF), ((OWN, D), BF), ((OWN, FF), BF), ((OWN, FF), BF)]
    scratch += [((2, SPAN, TOK), F32), ((OWN, D), F32), ((OWN, 128), F32), ((OWN, D), F32), ((OWN, D), F32)]
    scratch += [((OWN, D), BF), ((8, D), F32), ((1, FF), F32), ((8, D), F32), ((16, 128), F32)]
    scratch += [((16, 128), BF)] * 2 + [((4, 16, 128), BF)] * 2 + [((4, 2, 16, 128), BF)]
    return pl.pallas_call(
        forward_kernel,
        name="forward_all",
        out_shape=[jax.ShapeDtypeStruct(s, t) for s, t in full + kept],
        in_specs=[any_space] * 2 + [smem] * 2 + [vmem] * 15,
        out_specs=[any_space] * 21,
        scratch_shapes=[pltpu.VMEM(s, t) for s, t in scratch]
        + [
            pltpu.SemaphoreType.DMA((N_SEM,)),
            pltpu.SemaphoreType.DMA((N_SEM,)),
            pltpu.SemaphoreType.DMA((32,)),
        ],
        compiler_params=pltpu.CompilerParams(collective_id=1, has_side_effects=True, vmem_limit_bytes=62 << 20),
    )(tokens, cotangent, lengths, order, *own, *small)


def add_into(dst, srcs):
    lead = dst.shape[:-2]
    loop = lead[:-1] if len(lead) > 1 else lead
    total = math.prod(loop)

    def body(k, carry):
        index, rest = (), k
        for n in reversed(loop):
            index = (lax.rem(rest, n),) + index
            rest = lax.div(rest, n)
        value = dst[index].astype(F32)
        for s in srcs:
            value = value + s[index].astype(F32)
        dst[index] = value.astype(BF)
        return carry

    lax.fori_loop(0, total, body, 0)


class Reduce:
    def __init__(self, net, ref, rows, cols, order, bufs):
        self.net, self.ref, self.rows, self.cols = net, ref, rows, cols
        self.a, self.b, self.e = order
        self.wide, self.mid, self.low = bufs

    def at(self, **over):
        place = {k: self.net.me[k] for k in AXES}
        place.update(over)
        return self.ref.at[chip_index(place) + (self.rows, self.cols)]

    def quarter(self, by, h):
        b = None if h is None else ("half", h)
        return self.at(**{self.a: self.net.moved(self.a, by)[self.a], self.b: b, self.e: None})

    def buf(self, k, h):
        b = None if h is None else ("half", h)
        return self.wide.at[(k,) + chip_index({self.b: b, self.e: None}, drop=(self.a,))]

    def send(self, by, h, k, to):
        return self.net.copy(self.quarter(by, h), self.buf(k, h), self.net.ring(self.a, to))

    def p1(self):
        self.m0 = self.send(2, 0, 0, 1)
        self.m1 = self.send(2, 1, 0, 3)
        self.l1 = self.send(1, 1, 1, 1)
        self.r0 = self.send(3, 0, 2, 3)

    def p1_mid(self):
        self.m0.wait_recv()
        add_into(self.quarter(1, 0), [self.buf(0, 0)])
        self.l0 = self.send(1, 0, 1, 1)
        self.m1.wait_recv()
        add_into(self.quarter(3, 1), [self.buf(0, 1)])
        self.r1 = self.send(3, 1, 2, 3)

    def p2(self):
        for moved in (self.l1, self.r0, self.l0, self.r1):
            moved.wait_recv()
        add_into(self.quarter(0, None), [self.buf(1, None), self.buf(2, None)])
        self.c = []
        for k, d in enumerate((1, 3, 2)):
            there = self.net.moved(self.b, d)[self.b]
            self.c.append(
                self.net.copy(self.at(**{self.b: there, self.e: None}), self.mid.at[k], self.net.ring(self.b, d))
            )

    def p3(self):
        for moved in self.c:
            moved.wait_recv()
        add_into(self.at(**{self.e: None}), [self.mid.at[k] for k in range(3)])
        self.c = []
        for k, d in enumerate((1, 3, 2)):
            there = self.net.moved(self.e, d)[self.e]
            self.c.append(self.net.copy(self.at(**{self.e: there}), self.low.at[k], self.net.ring(self.e, d)))

    def result(self):
        for moved in self.c:
            moved.wait_recv()
        value = self.at()[...].astype(F32)
        for k in range(3):
            value = value + self.low[k].astype(F32)
        return value


RECTS = (
    (5, (0, 16), (0, 512), 0),
    (5, (16, 16), (0, 512), 1),
    (5, (32, 32), (0, 512), 2),
    (4, (0, 16), (0, 512), 0),
    (4, (0, 16), (512, 512), 1),
    (4, (0, 16), (1024, 1024), 2),
    (3, (0, 16), (0, 512), 1),
    (0, (0, 16), (0, 512), 0),
    (1, (0, 16), (0, 512), 1),
    (2, (0, 16), (0, 512), 2),
)
BIG_FIRST = tuple(tuple(reversed(o)) for o in ORDER)


def reduce_buffers():
    shapes = []
    for _, (_, rows), (_, width), order in RECTS:
        a, b, e = BIG_FIRST[order]
        shapes += [
            (3,) + chip_shape((a,)) + (rows, width),
            (3,) + chip_shape((a, b)) + (rows, width),
            (3, rows, width),
        ]
    return shapes


class VectorSum:
    def __init__(self, net, total, bufs):
        self.net, self.total = net, total
        self.sib, self.whole, self.vx, self.half, self.vy, self.one, self.vz = bufs

    def start(self):
        self.c = [self.net.copy(self.total, self.sib, self.net.ring("c", 0))]

    def wait(self):
        for moved in self.c:
            moved.wait_recv()

    def along_x(self):
        self.wait()
        self.whole[...] = self.total[...] + self.sib[...]
        self.c = []
        for k, d in enumerate((1, 3, 2)):
            x = self.net.moved("x", d)["x"]
            self.c.append(self.net.copy(self.whole.at[:, columns(256 * x, 256)], self.vx.at[k], self.net.ring("x", d)))

    def along_y(self):
        self.wait()
        mine = self.whole[:, columns(256 * self.net.me["x"], 256)]
        for k in range(3):
            mine = mine + self.vx[k]
        self.half[0], self.half[1] = mine[:, :128], mine[:, 128:]
        self.c = []
        for k, d in enumerate((1, 3, 2)):
            lo = lax.rem(self.net.moved("y", d)["y"], 2)
            self.c.append(self.net.copy(self.half.at[lo], self.vy.at[k], self.net.ring("y", d)))

    def along_z(self):
        self.wait()
        mine = self.half[lax.rem(self.net.me["y"], 2)]
        for k in range(3):
            mine = mine + self.vy[k]
        self.one[...] = mine
        self.c = [self.net.copy(self.one, self.vz.at[k], self.net.ring("z", d)) for k, d in enumerate((1, 3, 2))]

    def done(self, out):
        self.wait()
        t = (self.one[...] + self.vz[0]) + (self.vz[1] + self.vz[2])
        sh = lax.axis_index("shard")
        to = lax.broadcasted_iota(jnp.int32, (128, 128), 0)
        i = lax.broadcasted_iota(jnp.int32, (128, 128), 1)
        place = jnp.where(i < 64, 8 * sh + (i & 7), 32 * lax.rem(sh, 4) + i - 64)
        pick = jnp.where((place == to) & (i < 96), 1.0, 0.0).astype(BF)
        high = t.astype(BF)
        rest = t - high.astype(F32)
        mid = rest.astype(BF)
        last = (rest - mid.astype(F32)).astype(BF)
        got = (mm(high, pick) + mm(mid, pick)) + mm(last, pick)
        r = lax.broadcasted_iota(jnp.int32, (16, 128), 0)
        i = lax.broadcasted_iota(jnp.int32, (16, 128), 1)
        keep = ((i < 64) & (lax.shift_right_logical(i, 3) == r)) | ((i >= 64) & (r == 8 + lax.div(sh, 4)))
        out[...] = jnp.broadcast_to(jnp.sum(jnp.where(keep, got, 0.0), axis=0, keepdims=True), (8, 128))


def attention_back(q, k, v, probs, context, d_context, dq, dk, dv, first, last, start):
    def body(i, carry):
        h = lax.rem(i + start, HEADS // 2)
        cols = columns(h * 128, 128)
        dks, dvs = [], []
        for b in range(2):
            mine, near = pl.ds(b * TOK, TOK), pl.ds(b * TOK, SPAN)
            at = columns((2 * h + b) * OWN, OWN)
            p = jnp.concatenate([probs[0, :, at], probs[1, :, at]], axis=0)
            dc = d_context[mine, cols]
            dc2 = lane_split(dc)
            prod = (dc.astype(F32) * context[mine, cols].astype(F32)).T
            dsum = [jnp.sum(prod[s * HEAD : s * HEAD + HEAD], axis=0, keepdims=True) for s in range(2)]
            dp = mm(v[near, cols], dc2, NT)
            dr = (p.astype(F32) * ((dp - jnp.concatenate(dsum, axis=1)) * 0.125)).astype(BF)
            dvs.append(mm(p, dc2))
            dks.append(mm(dr, lane_split(q[mine, cols])))
            g = mm(k[near, cols], dr, TN)
            g = jnp.concatenate([g[:HEAD, :TOK], g[HEAD:, TOK:]], axis=0)
            dq[mine, cols] = g.T.astype(BF)
        for d, o in ((dks, dk), (dvs, dv)):
            o[0:TOK, cols] = d[0][:TOK].astype(BF)
            o[TOK:SPAN, cols] = (d[0][TOK:] + d[1][: SPAN - TOK]).astype(BF)
            o[SPAN:WIN, cols] = d[1][SPAN - TOK :].astype(BF)
        return carry

    lax.fori_loop(first, last, body, 0)


def column_sum(x):
    n, width = x.shape
    return jnp.sum(jnp.sum(x.astype(F32).reshape(n // 8, 8, width), axis=0), axis=0, keepdims=True)


class Return:
    def __init__(self, net, window, encoded, back, out, token_grad, sems):
        self.net, self.window, self.encoded, self.back = net, window, encoded, back
        self.out, self.token_grad, self.sems = out, token_grad, sems
        self.swaps = []
        self.lo = lax.rem(net.me["y"], 2)

    def pair(self, src, dst, sem):
        mine, theirs = rows_at(TOK * self.lo, TOK), rows_at(TOK * (1 - self.lo), TOK)
        local = pltpu.make_async_copy(src.at[mine], dst.at[self.lo], sem)
        local.start()
        return local, self.net.copy(src.at[theirs], dst.at[self.lo], self.net.pair(1 - self.lo))

    def start_encoded(self):
        self.swaps.append(self.pair(self.encoded, self.out, self.sems.at[0]))

    def start(self):
        w, net = self.window, self.net
        self.c = [
            net.copy(w.at[pl.ds(0, HALO)], self.back.at[0], net.ring("x", 3)),
            net.copy(w.at[pl.ds(HALO + OWN, HALO)], self.back.at[1], net.ring("x", 1)),
        ]

    def total(self):
        for moved in self.c:
            moved.wait_recv()
        rest = OWN - HALO
        own = pl.ds(HALO, OWN)
        y = self.window[own, :].astype(F32)
        low = y[:rest] + self.back[1, :rest].astype(F32)
        mid = y[rest:HALO] + self.back[1, rest:].astype(F32) + self.back[0, : HALO - rest].astype(F32)
        high = y[HALO:] + self.back[0, HALO - rest :].astype(F32)
        self.window[own, :] = jnp.concatenate([low, mid, high], axis=0).astype(BF)
        self.swaps.append(self.pair(self.window.at[own], self.token_grad, self.sems.at[1]))

    def done(self):
        for local, moved in self.swaps:
            local.wait()
            moved.wait_recv()


class Stream:
    SLOTS = 4

    def __init__(self, full, ring, sems):
        wq, wk, wv, wo, wi, wu = full
        self.ring = ring
        self.moves = []
        for n in range(12):
            slot = ring.at[n % self.SLOTS]
            if n < 4:
                pairs = [(wu.at[n], slot)]
            elif n < 8:
                pairs = [
                    (wi.at[n - 4, :, :, :, :, pl.ds(1024 * j, 1024)], slot.at[:, :, :, pl.ds(16 * j, 16)])
                    for j in range(4)
                ]
            else:
                w = (wo, wk, wv, wq)[n - 8]
                pairs = [(w.at[x], slot.at[:, :, :, pl.ds(16 * x, 16)]) for x in range(4)]
            self.moves.append([pltpu.make_async_copy(s, d, sems.at[4 * n + j]) for j, (s, d) in enumerate(pairs)])

    def start(self, n):
        for move in self.moves[n]:
            move.start()

    def wait(self, n):
        for move in self.moves[n]:
            move.wait()

    def part(self, n, j):
        return self.ring[n % self.SLOTS, :, :, :, 16 * j : 16 * j + 16].reshape(256, 1024)


class Backward:
    def __init__(self, ins, outs, scratch):
        self.weights = ins[:6]
        (self.x_in, self.q_in, self.k_in, self.v_in, self.probs_in, self.context_in, self.low_in, self.act_in) = ins[6:14]
        (self.slope_in, self.n1_in, self.inv1_in, self.d_in, self.encoded, self.vec, self.two) = ins[14:]
        self.owned, (self.out, self.token_grad, self.small) = outs[:6], outs[6:]
        take = iter(scratch)
        nxt = lambda n: [next(take) for _ in range(n)]
        (self.ring,) = nxt(1)
        self.g = nxt(6)
        self.bufs = nxt(3 * len(RECTS))
        self.x, self.q, self.k, self.v, self.context, self.low, self.act, self.inner, self.n1, self.inv1, self.d = nxt(11)
        self.outer, self.outer_sib, self.inner_sib, self.branch, self.branch_sib, self.d_context = nxt(6)
        self.dq, self.dk, self.dv, self.dq_sib, self.dk_sib, self.dv_sib, self.dx, self.back = nxt(8)
        self.kept, self.low_t = nxt(2)
        self.total, *vector_bufs = nxt(8)
        self.finals, self.ends = nxt(6), nxt(6)
        send_sem, recv_sem, self.local_sem = nxt(3)
        self.net = Net(send_sem, recv_sem)
        self.c = self.net.me["c"]
        self.loads = 0
        self.stream = Stream(self.weights, self.ring, self.local_sem.at[pl.ds(0, 48)])
        self.vectors = VectorSum(self.net, self.total, vector_bufs)
        self.back_rows = Return(
            self.net, self.dx, self.kept, self.back, self.out, self.token_grad, self.local_sem.at[pl.ds(48, 2)]
        )
        lanes = []
        for n, (w, (r0, rows), (base, width), order) in enumerate(RECTS):
            lanes.append(
                Reduce(
                    self.net,
                    self.g[w],
                    pl.ds(r0, rows),
                    pl.ds(base, width),
                    BIG_FIRST[order],
                    self.bufs[3 * n : 3 * n + 3],
                )
            )
        self.lanes = {"u": lanes[:3], "i": lanes[3:6], "o": lanes[6:7], "a": lanes[7:]}

    def load(self, src, dst):
        move = pltpu.make_async_copy(src, dst, self.local_sem.at[50 + self.loads])
        self.loads += 1
        move.start()
        return move

    def half(self, which, width):
        return columns(which * width, width)

    def share(self, src, dst, width):
        return self.net.copy(src.at[:, self.half(1 - self.c, width)], dst, self.net.ring("c", 0))

    def begin(self):
        greeted = self.net.greet()
        at_d = self.load(self.d_in, self.d)
        self.stream.start(0)
        self.total[...] = jnp.zeros((16, D), F32)
        self.total[G2 : G2 + 2, :] = self.two[0:2, :]
        at_d.wait()
        self.at_slope = self.load(self.slope_in, self.inner)
        for n in range(1, 4):
            self.stream.start(n)

        def body(t, carry):
            r = some_rows(t)
            low = self.d[r, :].astype(BF)
            self.outer[r, :] = low
            return carry + jnp.sum(low.astype(F32).reshape(ROWS // 8, 8, D), axis=0)

        s = lax.fori_loop(0, OWN // ROWS, body, jnp.zeros((8, D), F32))
        self.total[BU : BU + 1, :] = jnp.sum(s, axis=0, keepdims=True)
        greeted()
        self.got_outer = self.share(self.outer, self.outer_sib, 512)
        self.at_act = self.load(self.act_in, self.act)
        self.at_low = self.load(self.low_in, self.low)
        self.at_n1 = [self.load(self.n1_in, self.n1), self.load(self.inv1_in, self.inv1)]
        self.at_kept = self.load(self.encoded, self.kept)
        self.at_rest = [
            self.load(self.context_in, self.context),
            self.load(self.x_in, self.x),
            self.load(self.q_in, self.q),
            self.load(self.k_in, self.k),
            self.load(self.v_in, self.v),
        ]

    def d_inner(self):
        self.at_slope.wait()
        for n in range(4):
            self.stream.wait(n)

            def body(lo, carry, n=n):
                at = n * 1024 + lo * 512
                cols = columns(at, 512)
                y = mm(self.outer[...], self.ring[n, lo].reshape(512, 1024), NT)
                y = (y * self.inner[:, cols].astype(F32)).astype(BF)
                self.inner[:, cols] = y
                s = column_sum(y)
                for j in range(4):
                    dp, t = 2 * n + lo, j
                    self.total[8 + t : 9 + t, columns(dp * 128, 128)] = s[:, 128 * j : 128 * j + 128]
                return carry

            lax.fori_loop(0, 2, body, 0)
            self.stream.start(n + 4)
        self.got_inner = self.share(self.inner, self.inner_sib, 2048)

    def grad_outer(self):
        self.at_act.wait()
        self.got_outer.wait_recv()
        c = self.c
        mine = self.outer.at[:, self.half(c, 512)]

        def body(t, carry):
            cols = columns(t * 512, 512)
            y = mm(self.act[c, :, cols], mine[...], TN) + mm(self.act[1 - c, :, cols], self.outer_sib[...], TN)
            self.g[5][lax.div(t, 2), lax.rem(t, 2)] = y.astype(BF).reshape(2, 4, 64, 512)
            return carry

        lax.fori_loop(0, 8, body, 0)
        self.at_probs = self.load(self.probs_in, self.act)

    def d_normed(self):
        for n in range(4):
            self.stream.wait(4 + n)
            cols = slice(256 * n, 256 * n + 256)
            y = self.d[:, cols]
            for j in range(4):
                y = y + mm(self.inner[:, 1024 * j : 1024 * j + 1024], self.stream.part(4 + n, j), NT)
            self.d[:, cols] = y
            self.stream.start(8 + n)

    def turn_low(self):
        self.at_low.wait()
        for j, which in enumerate((self.c, 1 - self.c)):
            for x in range(4):
                part = self.low[which, :, 256 * x : 256 * x + 256]
                self.low_t[256 * x : 256 * x + 256, OWN * j : OWN * j + OWN] = part.T

    def grad_inner(self):
        self.got_inner.wait_recv()
        c = self.c

        def body(t, carry):
            x, j = lax.div(t, 4), lax.rem(t, 4)
            rows, cols = pl.ds(pl.multiple_of(x * 256, 256), 256), columns(j * 512, 512)
            y = mm(self.low_t[rows, :OWN], self.inner[:, columns(c * 2048 + j * 512, 512)])
            y = y + mm(self.low_t[rows, OWN:], self.inner_sib[:, cols])
            self.g[4][x, :, :, :, :, cols] = y.astype(BF).reshape(2, 2, 4, 16, 512)
            return carry

        lax.fori_loop(0, 16, body, 0)

    def norm_one(self):
        for move in self.at_n1:
            move.wait()

        def body(t, carry):
            r = some_rows(t)
            d, n = self.d[r, :], self.n1[r, :]
            da = norm_back(d * self.vec[G1 : G1 + 1, :], n, self.inv1[r, :1])
            low = da.astype(BF)
            self.d[r, :] = da
            self.branch[r, :] = low
            new = (d * n, d, low.astype(F32))
            return tuple(a + jnp.sum(b.reshape(ROWS // 8, 8, D), axis=0) for a, b in zip(carry, new))

        zero = jnp.zeros((8, D), F32)
        sums = lax.fori_loop(0, OWN // ROWS, body, (zero, zero, zero))
        for row, s in zip((G1, S1, BO), sums):
            self.total[row : row + 1, :] = jnp.sum(s, axis=0, keepdims=True)
        self.got_branch = self.share(self.branch, self.branch_sib, 512)

    def d_mixed(self):
        self.stream.wait(8)
        for x in range(4):
            self.d_context[:, 256 * x : 256 * x + 256] = mm(self.branch[...], self.stream.part(8, x), NT).astype(BF)

    def grad_rows(self, left, right, sib, out):
        mine = right.at[:, self.half(self.c, 512)]

        def body(x, carry):
            rows = columns(x * 256, 256)
            y = mm(left[0][:, rows], mine[...], TN) + mm(left[1][:, rows], sib[...], TN)
            out[x] = y.astype(BF).reshape(2, 2, 4, 16, 512)
            return carry

        lax.fori_loop(0, 4, body, 0)

    def pair(self, ref):
        return ref.at[self.c], ref.at[1 - self.c]

    def grad_output(self):
        self.got_branch.wait_recv()
        for move in self.at_rest:
            move.wait()
        self.grad_rows(self.pair(self.context), self.branch, self.branch_sib, self.g[3])

    def attend(self, first, last):
        if first == 0:
            self.at_probs.wait()
        attention_back(
            self.q,
            self.k,
            self.v,
            self.act,
            self.context.at[self.c],
            self.d_context,
            self.dq,
            self.dk,
            self.dv,
            first,
            last,
            HEADS // 4 * (1 - self.c),
        )

    def share_heads(self):
        self.got_heads = [
            self.share(self.dk, self.dk_sib, 512),
            self.share(self.dv, self.dv_sib, 512),
            self.share(self.dq, self.dq_sib, 512),
        ]

    def head_sums(self):
        self.total[BQ : BQ + 1, :] = column_sum(self.dq[...])
        self.total[BV : BV + 1, :] = column_sum(self.dv[...])
        self.vectors.start()

    def grad_key(self):
        self.got_heads[0].wait_recv()
        self.grad_rows(self.pair(self.x), self.dk, self.dk_sib, self.g[1])

    def grad_value(self):
        self.got_heads[1].wait_recv()
        self.grad_rows(self.pair(self.x), self.dv, self.dv_sib, self.g[2])

    def grad_query(self):
        self.got_heads[2].wait_recv()
        own = pl.ds(HALO, OWN)
        rows = (self.x.at[self.c, own], self.x.at[1 - self.c, own])
        self.grad_rows(rows, self.dq, self.dq_sib, self.g[0])

    def d_halo(self):
        for n in (9, 10):
            self.stream.wait(n)

        def sides(ref):
            return jnp.concatenate([ref[:HALO, :], ref[HALO + OWN :, :]], axis=0)

        for x in range(4):
            cols = slice(256 * x, 256 * x + 256)
            y = mm(sides(self.dk), self.stream.part(9, x), NT) + mm(sides(self.dv), self.stream.part(10, x), NT)
            self.dx[:HALO, cols] = y[:HALO].astype(BF)
            self.dx[HALO + OWN :, cols] = y[HALO:].astype(BF)
        self.back_rows.start()

    def d_own(self):
        self.stream.wait(11)
        own = slice(HALO, HALO + OWN)
        for x in range(4):
            cols = slice(256 * x, 256 * x + 256)
            y = mm(self.dk[own, :], self.stream.part(9, x), NT) + mm(self.dv[own, :], self.stream.part(10, x), NT)
            y = y + self.d[:, cols] + mm(self.dq[...], self.stream.part(11, x), NT)
            self.dx[own, cols] = y.astype(BF)

    def encoded_out(self):
        self.at_kept.wait()
        self.back_rows.start_encoded()

    def rows_back(self):
        self.back_rows.total()

    def finish(self):
        c, net = self.c, self.net
        done = [lane for group in ("u", "i", "o", "a") for lane in self.lanes[group]]
        swaps = []
        rects = list(zip(done, RECTS))
        for w in (5, 4, 3, 0, 1, 2):
            final, end = self.finals[w], self.ends[w]
            for lane, (of, (r0, rows), (base, width), _) in rects:
                if of == w:
                    final[pl.ds(r0, rows), pl.ds(base, width)] = lane.result()
            n, width = final.shape[0] // 2, final.shape[1]
            kept = final.at[pl.ds(pl.multiple_of(n * c, 8), n)]
            given = final.at[pl.ds(pl.multiple_of(n * (1 - c), 8), n)]
            swaps.append((w, net.copy(given, end.at[:, columns(c * width, width)], net.ring("c", 0))))
            end[:, columns(c * width, width)] = kept[...]
        self.vectors.done(self.small)
        stores = []
        for w, swap in swaps:
            swap.wait_recv()
            stores.append(self.load(self.ends[w], self.owned[w]))
        for store in stores:
            store.wait()
        self.back_rows.done()
        net.finish()


BACK = (
    "begin", "grad_outer", "u.p1", "encoded_out", "d_inner", "d_normed", "u.p1_mid", "norm_one", "turn_low",
    "d_mixed", "grad_output", "o.p1", "grad_inner", "i.p1", "attend.0.4", "share_heads", "u.p2", "attend.4.8",
    "o.p1_mid", "i.p1_mid", "head_sums", "d_halo", "grad_key", "grad_value", "grad_query", "a.p1", "d_own",
    "u.p3", "vectors.along_x", "i.p2", "a.p1_mid", "vectors.along_y", "o.p2", "rows_back", "i.p3",
    "vectors.along_z", "a.p2", "o.p3", "a.p3", "finish",
)


def backward_kernel(*refs):
    run_steps(Backward(refs[:21], refs[21:30], refs[30:]), BACK)


def backward_all(kept):
    any_space = pl.BlockSpec(memory_space=pl.ANY)
    vmem = pl.BlockSpec(memory_space=pltpu.VMEM)
    owned = [(r // 2, n) for r, n in BLOCKS]
    scratch = [((4, 2, 2, 4, 64, 1024), BF)]
    scratch += [(CHIPS + (r, n // 2), BF) for r, n in BLOCKS]
    scratch += [(s, BF) for s in reduce_buffers()]
    scratch += [((2, WIN, D), BF), ((OWN, D), BF), ((WIN, D), BF), ((WIN, D), BF), ((2, OWN, D), BF), ((2, OWN, D), BF)]
    scratch += [((2, OWN, FF), BF), ((OWN, FF), BF), ((OWN, D), F32), ((OWN, 128), F32), ((OWN, D), F32)]
    scratch += [((OWN, D), BF), ((OWN, 512), BF), ((OWN, 2048), BF), ((OWN, D), BF), ((OWN, 512), BF), ((OWN, D), BF)]
    scratch += [((OWN, D), BF), ((WIN, D), BF), ((WIN, D), BF), ((OWN, 512), BF), ((WIN, 512), BF), ((WIN, 512), BF)]
    scratch += [((WIN, D), BF), ((2, HALO, D), BF), ((OWN, D), BF), ((D, 2 * OWN), BF)]
    scratch += [((16, D), F32), ((16, D), F32), ((16, D), F32), ((3, 16, 256), F32), ((2, 16, 128), F32), ((3, 16, 128), F32)]
    scratch += [((16, 128), F32), ((3, 16, 128), F32)]
    scratch += [((r, n // 2), F32) for r, n in BLOCKS] + [(s, F32) for s in owned]
    return pl.pallas_call(
        backward_kernel,
        name="backward_all",
        out_shape=[jax.ShapeDtypeStruct(s, F32) for s in owned]
        + [jax.ShapeDtypeStruct((2, TOK, D), BF)] * 2
        + [jax.ShapeDtypeStruct((8, 128), F32)],
        in_specs=[any_space] * 19 + [vmem] * 2,
        out_specs=[any_space] * 8 + [vmem],
        scratch_shapes=[pltpu.VMEM(s, t) for s, t in scratch]
        + [
            pltpu.SemaphoreType.DMA((N_SEM,)),
            pltpu.SemaphoreType.DMA((N_SEM,)),
            pltpu.SemaphoreType.DMA((80,)),
        ],
        compiler_params=pltpu.CompilerParams(collective_id=2, has_side_effects=True, vmem_limit_bytes=63 << 20),
    )(*kept)


def keep_kernel(*refs):
    for src, dst in zip(refs[:8], refs[8:]):
        dst[...] = src[...]


def keep(*arrays):
    return pl.pallas_call(
        keep_kernel,
        name="keep",
        out_shape=[jax.ShapeDtypeStruct(a.shape, a.dtype) for a in arrays],
        in_specs=[pl.BlockSpec(memory_space=pltpu.VMEM)] * 8,
        out_specs=[pl.BlockSpec(memory_space=pltpu.VMEM)] * 8,
    )(*arrays)


def local(
    tokens, cotangent, seq_lengths, block_offsets, deal_order, wq, wk, wv, wo, bq, bv, bo, g1, s1, wi, bi, wu, bu, g2, s2
):
    small = [v[None] for v in (bq, bv, bo, g1, s1, bu, g2, s2, bi)]
    kept = forward_all(
        tokens[:, 0], cotangent[:, 0], seq_lengths[:, 0], deal_order[:, 0], (wq, wk, wv, wo, wi, wu), small
    )
    *owned, out, token_grad, sums = backward_all(kept)
    *owned, out, token_grad = keep(*owned, out, token_grad)
    mine = sums[0]
    sbq, sbv, sbo, sg1, ss1, sbu, sg2, ss2 = [mine[8 * j : 8 * j + 8] for j in range(8)]
    return (
        out[:, None],
        token_grad[:, None],
        *owned[:4],
        sbq,
        sbv,
        sbo,
        sg1,
        ss1,
        owned[4],
        mine[64:96],
        owned[5],
        sbu,
        sg2,
        ss2,
    )


def solution(mesh):
    rows = P(None, "shard", "dp", None)
    table = P(None, "shard", None)
    matrix, vector = P(("dp", "shard"), None), P(("dp", "shard"))
    in_specs = (rows, rows) + (table,) * 3 + (matrix,) * 4 + (vector,) * 5 + (matrix, vector, matrix) + (vector,) * 3
    out_specs = (rows, rows) + (matrix,) * 4 + (vector,) * 5 + (matrix, vector, matrix) + (vector,) * 3
    return jax.shard_map(local, mesh=mesh, in_specs=in_specs, out_specs=out_specs, check_vma=False)
```

```python
import math

import jax
import jax.numpy as jnp
from jax import lax
from jax.experimental import pallas as pl
from jax.experimental.pallas import tpu as pltpu
from jax.sharding import PartitionSpec as P

MESH = pl.DeviceIdType.MESH
BF = jnp.bfloat16
F32 = jnp.float32
D = 1024
FF = 4096
HEADS = 16
HEAD = 64
TOK = 128
OWN = 2 * TOK
HALO = 192
WIN = OWN + 2 * HALO
AXES = ("x", "y", "z")
ORDER = (("z", "y", "x"), ("x", "z", "y"), ("y", "x", "z"))
CHIPS = (4, 2, 2, 4)


def position():
    dp, sh = lax.axis_index("dp"), lax.axis_index("shard")
    return {
        "x": lax.div(dp, 2),
        "y": lax.div(sh, 8) * 2 + lax.rem(dp, 2),
        "z": lax.div(lax.rem(sh, 8), 2),
        "c": lax.rem(sh, 2),
    }


def device_at(at):
    return (
        at["x"] * 2 + lax.rem(at["y"], 2),
        lax.div(at["y"], 2) * 8 + at["z"] * 2 + at["c"],
    )


class Batch:
    def __init__(self, net, whole):
        self.net, self.whole = net, whole
        self.k = net.used
        net.used += 1
        net.batches.append(self)

    def send(self, src, dst, device):
        pltpu.make_async_remote_copy(
            src_ref=src,
            dst_ref=dst,
            send_sem=self.net.send_sem.at[self.k],
            recv_sem=self.net.recv_sem.at[self.k],
            device_id=device,
            device_id_type=MESH,
        ).start()

    def wait_recv(self):
        pltpu.make_async_copy(self.whole, self.whole, self.net.recv_sem.at[self.k]).wait()

    def wait_send(self):
        pltpu.make_async_copy(self.whole, self.whole, self.net.send_sem.at[self.k]).wait()


class Net:
    def __init__(self, send_sem, recv_sem):
        self.me = position()
        self.send_sem, self.recv_sem = send_sem, recv_sem
        self.used = 0
        self.batches = []

    def moved(self, axis, by):
        at = dict(self.me)
        if axis == "c":
            at["c"] = 1 - at["c"]
        else:
            at[axis] = lax.rem(at[axis] + by, 4)
        return at

    def ring(self, axis, by):
        return device_at(self.moved(axis, by))

    def pair(self, lo):
        at = dict(self.me)
        at["y"] = lax.div(at["y"], 2) * 2 + lo
        return device_at(at)

    def copy(self, src, dst, device):
        batch = Batch(self, dst)
        batch.send(src, dst, device)
        return batch

    def greet(self):
        bar = pltpu.get_barrier_semaphore()
        peers = [self.ring("c", 0)] + [self.ring(a, b) for a in AXES for b in (1, 2, 3)]
        for p in peers:
            pl.semaphore_signal(bar, inc=1, device_id=p, device_id_type=MESH)
        return lambda: pl.semaphore_wait(bar, len(peers))

    def finish(self):
        for batch in self.batches:
            batch.wait_send()
        assert self.used <= self.send_sem.shape[0], self.used


def chip_index(at, drop=()):
    out = []
    for axis in AXES:
        if axis in drop:
            continue
        v = at[axis]
        if axis == "y":
            if v is None:
                out += [slice(None), slice(None)]
            elif isinstance(v, tuple):
                out += [v[1], slice(None)]
            else:
                out += [lax.rem(v, 2), lax.div(v, 2)]
        elif v is None:
            out.append(slice(None))
        elif isinstance(v, tuple):
            out.append(pl.ds(2 * v[1], 2))
        else:
            out.append(v)
    return tuple(out)


def chip_shape(drop):
    shape = ()
    for axis in AXES:
        if axis not in drop:
            shape += (2, 2) if axis == "y" else (4,)
    return shape


def columns(base, width):
    return pl.ds(pl.multiple_of(base, 128), width)


class Gather:
    def __init__(self, net, ref, rows, cols, order):
        self.net, self.ref, self.rows, self.cols = net, ref, rows, cols
        self.a, self.b, self.e = order

    def at(self, **over):
        place = {k: self.net.me[k] for k in AXES}
        place.update(over)
        return self.ref.at[chip_index(place) + (self.rows, self.cols)]

    def send(self, batch, region, axis, by):
        batch.send(region, region, self.net.ring(axis, by))

    def blocks(self, *chips):
        return Batch(self.net, self.ref.at[chips + (self.rows, self.cols)])

    def p1(self):
        self.c = self.blocks(pl.ds(0, 3), 0, 0, 0)
        for d in (1, 3, 2):
            self.send(self.c, self.at(), self.a, d)

    def p2(self):
        self.c.wait_recv()
        self.c = self.blocks(pl.ds(0, 3), 0, 0, slice(None))
        for d in (1, 3, 2):
            self.send(self.c, self.at(**{self.a: None}), self.b, d)

    def p2_ring(self):
        self.c.wait_recv()
        self.c = self.blocks(pl.ds(0, 2), 0, 0, slice(None))
        for d in (1, 3):
            self.send(self.c, self.at(**{self.a: None}), self.b, d)

    def p2_mid(self):
        self.c.wait_recv()
        self.c = self.blocks(0, 0, 0, slice(None))
        for h, to in enumerate((1, 3)):
            b = self.net.moved(self.b, 4 - to)[self.b]
            self.send(self.c, self.at(**{self.a: ("half", h), self.b: b}), self.b, to)

    def part(self, h, by):
        e = self.net.moved(self.e, by)[self.e]
        return self.at(**{self.a: h if h is None else ("half", h), self.b: None, self.e: e})

    def quarter(self):
        return Batch(self.net, self.part(None, 0))

    def p3(self):
        self.c.wait_recv()
        self.near, self.far = self.quarter(), self.quarter()
        self.send(self.near, self.part(0, 0), self.e, 1)
        self.send(self.near, self.part(1, 0), self.e, 3)
        self.send(self.far, self.part(1, 0), self.e, 1)
        self.send(self.far, self.part(0, 0), self.e, 3)
        self.core = self.blocks(*(slice(None),) * 4)
        self.send(self.core, self.part(None, 0), "c", 0)

    def p3_mid(self):
        self.near.wait_recv()
        self.last = self.quarter()
        self.send(self.last, self.part(0, 3), self.e, 1)
        self.send(self.last, self.part(1, 1), self.e, 3)

    def p3_core(self):
        self.far.wait_recv()
        self.send(self.core, self.part(None, 3), "c", 0)
        self.send(self.core, self.part(None, 1), "c", 0)

    def p3_end(self):
        self.last.wait_recv()
        self.send(self.core, self.part(None, 2), "c", 0)

    def done(self):
        self.core.wait_recv()


def each(lanes, step):
    for lane in lanes:
        getattr(lane, step)()


def rows_at(base, count):
    return pl.ds(pl.multiple_of(base, TOK // 2), count)


class Window:
    def __init__(self, net, tokens, cotangent, window, cots, local_sem):
        self.net, self.window, self.cots = net, window, cots
        self.tokens, self.cotangent, self.local_sem = tokens, cotangent, local_sem
        self.lo = lax.rem(net.me["y"], 2)

    def pair(self, src, dst, sem):
        local = pltpu.make_async_copy(src.at[self.lo], dst, sem)
        local.start()
        return local, self.net.copy(src.at[1 - self.lo], dst, self.net.pair(1 - self.lo))

    def start(self):
        mine = self.window.at[rows_at(HALO + TOK * self.lo, TOK)]
        self.rows = self.pair(self.tokens, mine, self.local_sem.at[0])

    def start_cots(self):
        mine = self.cots.at[rows_at(TOK * self.lo, TOK)]
        self.cot_rows = self.pair(self.cotangent, mine, self.local_sem.at[1])

    def halo(self):
        local, moved = self.rows
        local.wait()
        moved.wait_recv()
        w, net = self.window, self.net
        self.c = Batch(net, w.at[pl.ds(0, 2 * HALO)])
        self.c.send(w.at[pl.ds(OWN, HALO)], w.at[pl.ds(0, HALO)], net.ring("x", 1))
        self.c.send(w.at[pl.ds(HALO, HALO)], w.at[pl.ds(HALO + OWN, HALO)], net.ring("x", 3))

    def done(self):
        self.c.wait_recv()

    def cots_done(self):
        local, moved = self.cot_rows
        local.wait()
        moved.wait_recv()


def place_own(me, mine, peer, full):
    here = chip_index(me)
    c = me["c"]
    first = c == 0

    def both(a, b):
        return jnp.concatenate([jnp.where(first, a, b), jnp.where(first, b, a)], axis=0)

    half = columns(c * 512, 512)
    for j in range(4):
        r = slice(8 * j, 8 * j + 8)
        full[j][here + (slice(None), half)] = both(mine[r, half], peer[r, half])
    for t in range(2):
        r, s = slice(32 + 8 * t, 40 + 8 * t), slice(48 + 8 * t, 56 + 8 * t)
        a = jnp.where(first, mine[r, :], mine[s, :])
        b = jnp.where(first, peer[r, :], peer[s, :])
        full[4][here + (slice(None), columns(c * 2048 + 1024 * t, 1024))] = both(a, b)
    full[5][here + (slice(None), half)] = both(mine[64:96, half], peer[64:96, half])


BLOCKS = ((16, 1024),) * 4 + ((16, 4096), (64, 1024))


SPAN = TOK + 2 * HALO
NT = (((1,), (1,)), ((), ()))
TN = (((0,), (0,)), ((), ()))
NN = (((1,), (0,)), ((), ()))


def mm(a, b, dims=NN):
    return lax.dot_general(a, b, dims, preferred_element_type=F32)


def tile(w, n0, n):
    return w[:, :, :, :, :, columns(n0, n)].reshape(-1, n)


def project(rows, w, out, bias=None, n=1024):
    def body(t, carry):
        cols = columns(t * n, n)
        y = mm(rows[...], tile(w, t * n, n))
        if bias is not None:
            y = y + bias[:, cols]
        out[:, cols] = y.astype(BF)
        return carry

    lax.fori_loop(0, out.shape[1] // n, body, 0)


def lane_split(x):
    low = lax.broadcasted_iota(jnp.int32, x.shape, 1) < HEAD
    zero = jnp.zeros_like(x)
    return jnp.concatenate([jnp.where(low, x, zero), jnp.where(low, zero, x)], axis=0)


def lane_join(x):
    n = x.shape[0] // 2
    low = lax.broadcasted_iota(jnp.int32, (n, x.shape[1]), 1) < HEAD
    return jnp.where(low, x[:n], x[n:])


def attention(q, k, v, bias, probs, context, first, last):
    def body(h, carry):
        cols = columns(h * 128, 128)
        for b in range(2):
            mine, near = pl.ds(b * TOK, TOK), pl.ds(b * TOK, SPAN)
            some, two = k[near, cols], lane_split(q[mine, cols]) * jnp.asarray(0.125, BF)
            p = []
            for s in range(2):
                e = mm(some, two[s * TOK : s * TOK + TOK], NT) + bias[b]
                e = jnp.exp(e - jnp.max(e, axis=0, keepdims=True))
                p.append((e * (1.0 / jnp.sum(e, axis=0, keepdims=True))).astype(BF))
            p = jnp.concatenate(p, axis=1)
            at = columns((2 * h + b) * OWN, OWN)
            probs[0, :, at], probs[1, :, at] = p[:OWN], p[OWN:]
            y = mm(v[near, cols], p, TN)
            y = jnp.concatenate([y[:HEAD, :TOK], y[HEAD:, TOK:]], axis=0)
            context[mine, cols] = y.T.astype(BF)
        return carry

    lax.fori_loop(first, last, body, 0, unroll=2)


def normalized(a):
    centred = a - jnp.mean(a, axis=-1, keepdims=True)
    inv = lax.rsqrt(jnp.mean(centred * centred, axis=-1, keepdims=True) + 1e-05)
    return centred * inv, inv


def norm_back(dn, n, inv):
    return inv * (dn - jnp.mean(dn, axis=-1, keepdims=True) - n * jnp.mean(dn * n, axis=-1, keepdims=True))


def feed_in(low, wi, bi, act, slope, first, last, n=512):
    def body(t, carry):
        cols = columns(t * n, n)
        u = mm(low[...], tile(wi, t * n, n)) + bi[:, cols]
        phi = 0.5 + 0.5 * lax.erf(u * math.sqrt(0.5))
        act[:, cols] = (u * phi).astype(BF)
        slope[:, cols] = (phi + u * (jnp.exp(-0.5 * (u * u)) * (1.0 / math.sqrt(2 * math.pi)))).astype(BF)
        return carry

    lax.fori_loop(first, last, body, 0, unroll=2)


ROWS = 32


def some_rows(t):
    return pl.ds(pl.multiple_of(t * ROWS, ROWS), ROWS)


def segment_bias(lengths, order, start, lo, bias):
    ends, total = [], 0
    for k in range(16):
        total = total + lengths[lo, order[lo, k]]
        ends.append(total)

    def which(at):
        found = jnp.where(at < 0, -1, 0)
        for e in ends:
            found = found + (at >= e).astype(jnp.int32)
        return found

    keys = which(start + lax.broadcasted_iota(jnp.int32, (WIN, TOK), 0))
    queries = which(start + HALO + lax.broadcasted_iota(jnp.int32, (8, OWN), 1))[:1]
    for b in range(2):
        same = keys[b * TOK : b * TOK + SPAN] == queries[:, b * TOK : b * TOK + TOK]
        bias[b] = jnp.where(same, 0.0, -1e30)


class Vectors:
    def __init__(self, net, small, rows, tiles, vec, inner):
        self.net, self.small, self.rows = net, small, rows
        self.own, self.sib, self.tz, self.ty, self.tx = tiles
        self.vec, self.inner = vec, inner

    def around(self, axis, tiles, mine):
        self.c = Batch(self.net, tiles.at[pl.ds(0, 3)])
        for d in (1, 3, 2):
            self.c.send(tiles.at[mine], tiles.at[mine], self.net.ring(axis, d))

    def place(self):
        sh = lax.axis_index("shard")
        self.rows[...] = jnp.zeros((16, 128), F32)
        for j in range(9):
            n = self.small[j].shape[1]
            self.rows[j : j + 1, :n] = self.small[j][...].astype(F32)
        i = lax.broadcasted_iota(jnp.int32, (128, 128), 0)
        to = lax.broadcasted_iota(jnp.int32, (128, 128), 1)
        value = self.rows[...].astype(BF)
        eight = mm(value, jnp.where((to == 8 * sh + i) & (i < 8), 1.0, 0.0).astype(BF))
        many = mm(value, jnp.where((to == 32 * lax.rem(sh, 4) + i) & (i < 32), 1.0, 0.0).astype(BF))
        r = lax.broadcasted_iota(jnp.int32, (16, 128), 0)
        many = jnp.broadcast_to(many[8:9], (16, 128))
        tile = jnp.where(r < 8, eight, jnp.where(r == 8 + lax.div(sh, 4), many, 0.0))
        self.own[...] = tile.astype(BF)

    def start(self):
        self.c = self.net.copy(self.own, self.sib, self.net.ring("c", 0))

    def wait(self):
        self.c.wait_recv()

    def along_z(self):
        self.wait()
        z = self.net.me["z"]
        self.tz[z] = self.own[...] + self.sib[...]
        self.around("z", self.tz, z)

    def along_y(self):
        self.wait()
        y = self.net.me["y"]
        self.ty[y] = (self.tz[0] + self.tz[1]) + (self.tz[2] + self.tz[3])
        self.around("y", self.ty, y)

    def along_x(self):
        self.wait()
        x = self.net.me["x"]
        self.tx[x, 0] = self.ty[0] + self.ty[2]
        self.tx[x, 1] = self.ty[1] + self.ty[3]
        self.around("x", self.tx, x)

    def done(self):
        self.wait()
        for dp in range(8):
            got = self.tx[dp // 2, dp % 2].astype(F32)
            self.vec[:, 128 * dp : 128 * dp + 128] = got[:8]
            for t in range(4):
                at = 512 * dp + 128 * t
                self.inner[:, at : at + 128] = got[8 + t : 9 + t]


BQ, BV, BO, G1, S1, BU, G2, S2 = range(8)


class Forward:
    def __init__(self, ins, outs, scratch):
        self.tokens, self.cotangent, self.lengths, self.order = ins[:4]
        self.own, self.small = ins[4:10], ins[10:]
        self.weights_out = outs[:6]
        (self.x_out, self.q_out, self.k_out, self.v_out, self.probs_out, self.context_out, self.low_out) = outs[6:13]
        (self.act_out, self.slope_out, self.n1_out, self.inv1_out, self.d_out, self.encoded_out) = outs[13:19]
        self.vec_out, self.two_out = outs[19:]
        self.mine, self.peer = scratch[:2]
        self.full, scratch = scratch[2:8], scratch[8:]
        (self.window, self.cots, self.q, self.k, self.v, self.probs, self.context, self.low) = scratch[:8]
        (self.act, self.slope, self.bias, self.n1, self.inv1, self.normed, self.total, self.encoded) = scratch[8:16]
        self.vec, self.inner, self.two, self.placed = scratch[16:20]
        tiles, (send_sem, recv_sem, self.local_sem) = scratch[20:25], scratch[25:]
        self.net = Net(send_sem, recv_sem)
        self.me, self.c = self.net.me, self.net.me["c"]
        self.lo = lax.rem(self.me["y"], 2)
        self.stores, self.gets = [], []
        self.vectors = Vectors(self.net, self.small, self.placed, tiles, self.vec, self.inner)
        self.view = Window(self.net, self.tokens, self.cotangent, self.window, self.cots, self.local_sem)
        rows, half = slice(None), columns(self.c * 512, 512)
        wi, wu = self.full[4], self.full[5]

        def inner(base, width, order):
            return Gather(self.net, wi, rows, columns(self.c * 2048 + base, width), ORDER[order])

        self.lanes = {
            "a": [Gather(self.net, self.full[j], rows, half, ORDER[j]) for j in range(3)],
            "b": [Gather(self.net, self.full[3], rows, half, ORDER[2]), inner(0, 1024, 1), inner(1024, 1024, 2)],
            "u": [
                Gather(self.net, wu, pl.ds(0, 32), half, ORDER[0]),
                Gather(self.net, wu, pl.ds(32, 16), half, ORDER[1]),
                Gather(self.net, wu, pl.ds(48, 16), half, ORDER[2]),
            ],
        }

    def store(self, src, dst):
        move = pltpu.make_async_copy(src, dst, self.local_sem.at[2 + len(self.stores)])
        move.start()
        self.stores.append(move)

    def both(self, src, dst):
        self.gets.append(self.net.copy(src, dst.at[self.c], self.net.ring("c", 0)))
        self.store(src, dst.at[self.c])

    def begin(self):
        greeted = self.net.greet()
        for j in range(4):
            self.mine[8 * j : 8 * j + 8, :] = self.own[j][...]
            self.mine[32 + 8 * j : 40 + 8 * j, :] = self.own[4][:, 1024 * j : 1024 * j + 1024]
        self.mine[64:96, :] = self.own[5][...]
        self.vectors.place()
        segment_bias(self.lengths, self.order, self.me["x"] * OWN - HALO, self.lo, self.bias)
        greeted()
        swap = self.net.copy(self.mine, self.peer, self.net.ring("c", 0))
        self.view.start()
        self.vectors.start()
        swap.wait_recv()
        place_own(self.me, self.mine, self.peer, self.full)

    def halo(self):
        self.view.halo()

    def cots_in(self):
        self.view.start_cots()

    def rows_done(self):
        self.view.done()
        self.both(self.window, self.x_out)

    def query(self):
        project(self.window.at[pl.ds(HALO, OWN)], self.full[0], self.q, self.vec.at[BQ : BQ + 1])

    def key(self):
        project(self.window, self.full[1], self.k)

    def value(self):
        project(self.window, self.full[2], self.v, self.vec.at[BV : BV + 1])

    def keep_heads(self):
        for j in range(3):
            self.store(self.full[j], self.weights_out[j])
        for src, dst in ((self.q, self.q_out), (self.k, self.k_out), (self.v, self.v_out)):
            self.store(src, dst)

    def attend(self, first, last):
        attention(self.q, self.k, self.v, self.bias, self.probs, self.context, first, last)

    def keep_probs(self):
        self.both(self.context, self.context_out)
        self.store(self.probs, self.probs_out)

    def mix(self):
        self.store(self.full[3], self.weights_out[3])
        self.store(self.full[4], self.weights_out[4])

        def body(t, carry):
            cols = columns(t * 512, 512)
            y = mm(self.context[...], tile(self.full[3], t * 512, 512)) + self.vec[BO : BO + 1, cols]
            self.total[:, cols] = y + self.window[pl.ds(HALO, OWN), cols].astype(F32)
            return carry

        lax.fori_loop(0, 2, body, 0, unroll=2)

    def norm_one(self):
        def body(t, carry):
            r = some_rows(t)
            n, inv = normalized(self.total[r, :])
            self.n1[r, :] = n
            self.inv1[r, :] = jnp.broadcast_to(inv, (ROWS, 128))
            y = n * self.vec[G1 : G1 + 1, :] + self.vec[S1 : S1 + 1, :]
            self.normed[r, :] = y
            self.low[r, :] = y.astype(BF)
            return carry

        lax.fori_loop(0, OWN // ROWS, body, 0)
        self.both(self.low, self.low_out)
        self.store(self.n1, self.n1_out)
        self.store(self.inv1, self.inv1_out)

    def feed_in(self, first, last):
        feed_in(self.low, self.full[4], self.inner, self.act, self.slope, first, last)
        if last == FF // 512:
            self.both(self.act, self.act_out)
            self.store(self.slope, self.slope_out)
            self.store(self.vec, self.vec_out)

    def feed_out(self):
        self.store(self.full[5], self.weights_out[5])

        def body(t, carry):
            cols = columns(t * 512, 512)
            y = mm(self.act[...], tile(self.full[5], t * 512, 512)) + self.vec[BU : BU + 1, cols]
            self.total[:, cols] = y + self.normed[:, cols]
            return carry

        lax.fori_loop(0, 2, body, 0, unroll=2)

    def cots_done(self):
        self.view.cots_done()

    def norm_two(self):
        def body(t, carry):
            r = some_rows(t)
            n, inv = normalized(self.total[r, :])
            gain = self.vec[G2 : G2 + 1, :]
            self.encoded[r, :] = (n * gain + self.vec[S2 : S2 + 1, :]).astype(BF)
            d = self.cots[r, :].astype(F32)
            self.normed[r, :] = norm_back(d * gain, n, inv)
            dn = jnp.sum((d * n).reshape(ROWS // 8, 8, D), axis=0)
            return carry[0] + dn, carry[1] + jnp.sum(d.reshape(ROWS // 8, 8, D), axis=0)

        zero = jnp.zeros((8, D), F32)
        gain_sum, shift_sum = lax.fori_loop(0, OWN // ROWS, body, (zero, zero))
        self.two[0:1, :] = jnp.sum(gain_sum, axis=0, keepdims=True)
        self.two[1:2, :] = jnp.sum(shift_sum, axis=0, keepdims=True)
        self.two[2:8, :] = jnp.zeros((6, D), F32)
        self.store(self.normed, self.d_out)
        self.store(self.encoded, self.encoded_out)
        self.store(self.two, self.two_out)

    def finish(self):
        for got in self.gets:
            got.wait_recv()
        for move in self.stores:
            move.wait()
        self.net.finish()


FORE = (
    "begin", "a.p1", "b.p1", "u.p1", "vectors.along_z", "a.p2", "b.p2_ring", "u.p2_ring", "vectors.along_y", "a.p3",
    "b.p2_mid", "u.p2_mid", "halo", "vectors.along_x", "a.p3_mid", "b.p3", "a.p3_core", "a.p3_end", "vectors.done",
    "a.done", "query", "rows_done", "b.p3_mid", "u.p3", "key", "value", "attend.0.2", "cots_in", "b.p3_core",
    "attend.2.4", "b.p3_end", "keep_heads", "attend.4.6", "u.p3_mid", "attend.6.8", "keep_probs", "b.done", "mix",
    "norm_one", "u.p3_core", "feed_in.0.2", "feed_in.2.4", "u.p3_end", "feed_in.4.6", "feed_in.6.8", "u.done",
    "feed_out", "cots_done", "norm_two", "finish",
)


def run_steps(work, steps):
    for step in steps:
        name, *rest = step.split(".")
        if name in work.lanes:
            each(work.lanes[name], rest[0])
        elif name == "vectors":
            getattr(work.vectors, rest[0])()
        else:
            getattr(work, name)(*map(int, rest))


def forward_kernel(*refs):
    run_steps(Forward(refs[:19], refs[19:40], refs[40:]), FORE)


def forward_all(tokens, cotangent, lengths, order, own, small):
    any_space = pl.BlockSpec(memory_space=pl.ANY)
    vmem = pl.BlockSpec(memory_space=pltpu.VMEM)
    smem = pl.BlockSpec(memory_space=pltpu.SMEM)
    full = [(CHIPS + s, BF) for s in BLOCKS]
    kept = [
        ((2, WIN, D), BF),
        ((OWN, D), BF),
        ((WIN, D), BF),
        ((WIN, D), BF),
        ((2, OWN, FF), BF),
        ((2, OWN, D), BF),
        ((2, OWN, D), BF),
        ((2, OWN, FF), BF),
        ((OWN, FF), BF),
        ((OWN, D), F32),
        ((OWN, 128), F32),
        ((OWN, D), F32),
        ((OWN, D), BF),
        ((8, D), F32),
        ((8, D), F32),
    ]
    scratch = [((96, 1024), BF)] * 2 + full
    scratch += [((WIN, D), BF), ((OWN, D), BF), ((OWN, D), BF), ((WIN, D), BF), ((WIN, D), BF)]
    scratch += [((2, OWN, FF), BF), ((OWN, D), BF), ((OWN, D), BF), ((OWN, FF), BF), ((OWN, FF), BF)]
    scratch += [((2, SPAN, TOK), F32), ((OWN, D), F32), ((OWN, 128), F32), ((OWN, D), F32), ((OWN, D), F32)]
    scratch += [((OWN, D), BF), ((8, D), F32), ((1, FF), F32), ((8, D), F32), ((16, 128), F32)]
    scratch += [((16, 128), BF)] * 2 + [((4, 16, 128), BF)] * 2 + [((4, 2, 16, 128), BF)]
    return pl.pallas_call(
        forward_kernel,
        name="forward_all",
        out_shape=[jax.ShapeDtypeStruct(s, t) for s, t in full + kept],
        in_specs=[any_space] * 2 + [smem] * 2 + [vmem] * 15,
        out_specs=[any_space] * 21,
        scratch_shapes=[pltpu.VMEM(s, t) for s, t in scratch]
        + [
            pltpu.SemaphoreType.DMA((80,)),
            pltpu.SemaphoreType.DMA((80,)),
            pltpu.SemaphoreType.DMA((24,)),
        ],
        compiler_params=pltpu.CompilerParams(collective_id=1, has_side_effects=True, vmem_limit_bytes=62 << 20),
    )(tokens, cotangent, lengths, order, *own, *small)


def add_into(dst, srcs):
    lead = dst.shape[:-2]
    loop = lead[:-1] if len(lead) > 1 else lead
    total = math.prod(loop)

    def body(k, carry):
        index, rest = (), k
        for n in reversed(loop):
            index = (lax.rem(rest, n),) + index
            rest = lax.div(rest, n)
        value = dst[index].astype(F32)
        for s in srcs:
            value = value + s[index].astype(F32)
        dst[index] = value.astype(BF)
        return carry

    lax.fori_loop(0, total, body, 0)


class Reduce:
    def __init__(self, net, ref, rows, cols, order, bufs):
        self.net, self.ref, self.rows, self.cols = net, ref, rows, cols
        self.a, self.b, self.e = order
        self.wide, self.mid, self.low = bufs

    def at(self, **over):
        place = {k: self.net.me[k] for k in AXES}
        place.update(over)
        return self.ref.at[chip_index(place) + (self.rows, self.cols)]

    def quarter(self, by, h):
        b = None if h is None else ("half", h)
        return self.at(**{self.a: self.net.moved(self.a, by)[self.a], self.b: b, self.e: None})

    def buf(self, k, h):
        b = None if h is None else ("half", h)
        return self.wide.at[(k,) + chip_index({self.b: b, self.e: None}, drop=(self.a,))]

    def send(self, batch, by, h, k, to):
        batch.send(self.quarter(by, h), self.buf(k, h), self.net.ring(self.a, to))

    def p1(self):
        self.near = Batch(self.net, self.buf(0, None))
        self.send(self.near, 2, 0, 0, 1)
        self.send(self.near, 2, 1, 0, 3)
        self.far = Batch(self.net, self.wide.at[pl.ds(1, 2)])
        self.send(self.far, 1, 1, 1, 1)
        self.send(self.far, 3, 0, 2, 3)

    def p1_mid(self):
        self.near.wait_recv()
        add_into(self.quarter(1, 0), [self.buf(0, 0)])
        self.send(self.far, 1, 0, 1, 1)
        add_into(self.quarter(3, 1), [self.buf(0, 1)])
        self.send(self.far, 3, 1, 2, 3)

    def p2(self):
        self.far.wait_recv()
        add_into(self.quarter(0, None), [self.buf(1, None), self.buf(2, None)])
        self.c = Batch(self.net, self.mid)
        for k, d in enumerate((1, 3, 2)):
            there = self.net.moved(self.b, d)[self.b]
            self.c.send(self.at(**{self.b: there, self.e: None}), self.mid.at[k], self.net.ring(self.b, d))

    def p3(self):
        self.c.wait_recv()
        add_into(self.at(**{self.e: None}), [self.mid.at[k] for k in range(3)])
        self.c = Batch(self.net, self.low)
        for k, d in enumerate((1, 3, 2)):
            there = self.net.moved(self.e, d)[self.e]
            self.c.send(self.at(**{self.e: there}), self.low.at[k], self.net.ring(self.e, d))

    def result(self):
        self.c.wait_recv()
        value = self.at()[...].astype(F32)
        for k in range(3):
            value = value + self.low[k].astype(F32)
        return value


RECTS = (
    (5, (0, 16), (0, 512), 0),
    (5, (16, 16), (0, 512), 1),
    (5, (32, 32), (0, 512), 2),
    (4, (0, 16), (0, 512), 0),
    (4, (0, 16), (512, 512), 1),
    (4, (0, 16), (1024, 1024), 2),
    (3, (0, 16), (0, 512), 1),
    (0, (0, 16), (0, 512), 0),
    (1, (0, 16), (0, 512), 1),
    (2, (0, 16), (0, 512), 2),
)
BIG_FIRST = tuple(tuple(reversed(o)) for o in ORDER)


def reduce_buffers():
    shapes = []
    for _, (_, rows), (_, width), order in RECTS:
        a, b, e = BIG_FIRST[order]
        shapes += [
            (3,) + chip_shape((a,)) + (rows, width),
            (3,) + chip_shape((a, b)) + (rows, width),
            (3, rows, width),
        ]
    return shapes


class VectorSum:
    def __init__(self, net, total, bufs):
        self.net, self.total = net, total
        self.sib, self.whole, self.vx, self.half, self.vy, self.one, self.vz = bufs

    def start(self):
        self.c = self.net.copy(self.total, self.sib, self.net.ring("c", 0))

    def around(self, axis, bufs, part):
        self.c = Batch(self.net, bufs)
        for k, d in enumerate((1, 3, 2)):
            self.c.send(part(self.net.moved(axis, d)[axis]), bufs.at[k], self.net.ring(axis, d))

    def along_x(self):
        self.c.wait_recv()
        self.whole[...] = self.total[...] + self.sib[...]
        self.around("x", self.vx, lambda x: self.whole.at[:, columns(256 * x, 256)])

    def along_y(self):
        self.c.wait_recv()
        mine = self.whole[:, columns(256 * self.net.me["x"], 256)]
        for k in range(3):
            mine = mine + self.vx[k]
        self.half[0], self.half[1] = mine[:, :128], mine[:, 128:]
        self.around("y", self.vy, lambda y: self.half.at[lax.rem(y, 2)])

    def along_z(self):
        self.c.wait_recv()
        mine = self.half[lax.rem(self.net.me["y"], 2)]
        for k in range(3):
            mine = mine + self.vy[k]
        self.one[...] = mine
        self.around("z", self.vz, lambda z: self.one)

    def done(self, out):
        self.c.wait_recv()
        t = (self.one[...] + self.vz[0]) + (self.vz[1] + self.vz[2])
        sh = lax.axis_index("shard")
        to = lax.broadcasted_iota(jnp.int32, (128, 128), 0)
        i = lax.broadcasted_iota(jnp.int32, (128, 128), 1)
        place = jnp.where(i < 64, 8 * sh + (i & 7), 32 * lax.rem(sh, 4) + i - 64)
        pick = jnp.where((place == to) & (i < 96), 1.0, 0.0).astype(BF)
        high = t.astype(BF)
        rest = t - high.astype(F32)
        mid = rest.astype(BF)
        last = (rest - mid.astype(F32)).astype(BF)
        got = (mm(high, pick) + mm(mid, pick)) + mm(last, pick)
        r = lax.broadcasted_iota(jnp.int32, (16, 128), 0)
        i = lax.broadcasted_iota(jnp.int32, (16, 128), 1)
        keep = ((i < 64) & (lax.shift_right_logical(i, 3) == r)) | ((i >= 64) & (r == 8 + lax.div(sh, 4)))
        out[...] = jnp.broadcast_to(jnp.sum(jnp.where(keep, got, 0.0), axis=0, keepdims=True), (8, 128))


def attention_back(q, k, v, probs, context, d_context, dq, dk, dv, first, last, start):
    def body(i, carry):
        h = lax.rem(i + start, HEADS // 2)
        cols = columns(h * 128, 128)
        dks, dvs = [], []
        for b in range(2):
            mine, near = pl.ds(b * TOK, TOK), pl.ds(b * TOK, SPAN)
            at = columns((2 * h + b) * OWN, OWN)
            p = jnp.concatenate([probs[0, :, at], probs[1, :, at]], axis=0)
            dc = d_context[mine, cols]
            dc2 = lane_split(dc)
            prod = (dc.astype(F32) * context[mine, cols].astype(F32)).T
            dr = []
            for s in range(2):
                own = slice(s * TOK, s * TOK + TOK)
                dsum = jnp.sum(prod[s * HEAD : s * HEAD + HEAD], axis=0, keepdims=True)
                dp = mm(v[near, cols], dc2[own], NT)
                dr.append((p[:, own].astype(F32) * ((dp - dsum) * 0.125)).astype(BF))
            dr = jnp.concatenate(dr, axis=1)
            dvs.append(mm(p, dc2))
            dks.append(mm(dr, lane_split(q[mine, cols])))
            g = mm(k[near, cols], dr, TN)
            g = jnp.concatenate([g[:HEAD, :TOK], g[HEAD:, TOK:]], axis=0)
            dq[mine, cols] = g.T.astype(BF)
        for d, o in ((dks, dk), (dvs, dv)):
            o[0:TOK, cols] = d[0][:TOK].astype(BF)
            o[TOK:SPAN, cols] = (d[0][TOK:] + d[1][: SPAN - TOK]).astype(BF)
            o[SPAN:WIN, cols] = d[1][SPAN - TOK :].astype(BF)
        return carry

    lax.fori_loop(first, last, body, 0, unroll=2)


def column_sum(x):
    n, width = x.shape
    return jnp.sum(jnp.sum(x.astype(F32).reshape(n // 8, 8, width), axis=0), axis=0, keepdims=True)


class Return:
    def __init__(self, net, window, encoded, back, out, token_grad, sems):
        self.net, self.window, self.encoded, self.back = net, window, encoded, back
        self.out, self.token_grad, self.sems = out, token_grad, sems
        self.swaps = []
        self.lo = lax.rem(net.me["y"], 2)

    def pair(self, src, dst, sem):
        mine, theirs = rows_at(TOK * self.lo, TOK), rows_at(TOK * (1 - self.lo), TOK)
        local = pltpu.make_async_copy(src.at[mine], dst.at[self.lo], sem)
        local.start()
        return local, self.net.copy(src.at[theirs], dst.at[self.lo], self.net.pair(1 - self.lo))

    def start_encoded(self):
        self.swaps.append(self.pair(self.encoded, self.out, self.sems.at[0]))

    def start(self):
        w, net = self.window, self.net
        self.c = Batch(net, self.back)
        self.c.send(w.at[pl.ds(0, HALO)], self.back.at[0], net.ring("x", 3))
        self.c.send(w.at[pl.ds(HALO + OWN, HALO)], self.back.at[1], net.ring("x", 1))

    def total(self):
        self.c.wait_recv()
        rest = OWN - HALO
        own = pl.ds(HALO, OWN)
        y = self.window[own, :].astype(F32)
        low = y[:rest] + self.back[1, :rest].astype(F32)
        mid = y[rest:HALO] + self.back[1, rest:].astype(F32) + self.back[0, : HALO - rest].astype(F32)
        high = y[HALO:] + self.back[0, HALO - rest :].astype(F32)
        self.window[own, :] = jnp.concatenate([low, mid, high], axis=0).astype(BF)
        self.swaps.append(self.pair(self.window.at[own], self.token_grad, self.sems.at[1]))

    def done(self):
        for local, moved in self.swaps:
            local.wait()
            moved.wait_recv()


class Stream:
    SLOTS = 4

    def __init__(self, full, ring, sems):
        wq, wk, wv, wo, wi, wu = full
        self.ring = ring
        self.moves = []
        for n in range(12):
            slot = ring.at[n % self.SLOTS]
            if n < 4:
                pairs = [(wu.at[n], slot)]
            elif n < 8:
                pairs = [
                    (wi.at[n - 4, :, :, :, :, pl.ds(1024 * j, 1024)], slot.at[:, :, :, pl.ds(16 * j, 16)])
                    for j in range(4)
                ]
            else:
                w = (wo, wk, wv, wq)[n - 8]
                pairs = [(w.at[x], slot.at[:, :, :, pl.ds(16 * x, 16)]) for x in range(4)]
            self.moves.append([pltpu.make_async_copy(s, d, sems.at[4 * (n % self.SLOTS) + j]) for j, (s, d) in enumerate(pairs)])

    def start(self, n):
        for move in self.moves[n]:
            move.start()

    def wait(self, n):
        for move in self.moves[n]:
            move.wait()

    def part(self, n, j):
        return self.ring[n % self.SLOTS, :, :, :, 16 * j : 16 * j + 16].reshape(256, 1024)


class Backward:
    def __init__(self, ins, outs, scratch):
        self.weights = ins[:6]
        (self.x_in, self.q_in, self.k_in, self.v_in, self.probs_in, self.context_in, self.low_in, self.act_in) = ins[6:14]
        (self.slope_in, self.n1_in, self.inv1_in, self.d_in, self.encoded, self.vec, self.two) = ins[14:]
        self.owned, (self.out, self.token_grad, self.small) = outs[:6], outs[6:]
        take = iter(scratch)
        nxt = lambda n: [next(take) for _ in range(n)]
        (self.ring,) = nxt(1)
        self.g = nxt(6)
        self.bufs = nxt(3 * len(RECTS))
        self.x, self.q, self.k, self.v, self.context, self.act, self.inner, self.n1, self.inv1, self.d = nxt(10)
        self.outer, self.outer_sib, self.inner_sib, self.branch, self.branch_sib, self.d_context = nxt(6)
        self.dq, self.dk, self.dv, self.dq_sib, self.dk_sib, self.dv_sib, self.dx, self.back = nxt(8)
        self.kept, self.low_t = nxt(2)
        self.total, *vector_bufs = nxt(8)
        self.finals, self.ends = nxt(6), nxt(6)
        send_sem, recv_sem, self.local_sem = nxt(3)
        self.net = Net(send_sem, recv_sem)
        self.c = self.net.me["c"]
        self.loads = 0
        self.stream = Stream(self.weights, self.ring, self.local_sem.at[pl.ds(0, 16)])
        self.vectors = VectorSum(self.net, self.total, vector_bufs)
        self.back_rows = Return(
            self.net, self.dx, self.kept, self.back, self.out, self.token_grad, self.local_sem.at[pl.ds(16, 2)]
        )
        lanes = []
        for n, (w, (r0, rows), (base, width), order) in enumerate(RECTS):
            lanes.append(
                Reduce(
                    self.net,
                    self.g[w],
                    pl.ds(r0, rows),
                    pl.ds(base, width),
                    BIG_FIRST[order],
                    self.bufs[3 * n : 3 * n + 3],
                )
            )
        self.lanes = {"u": lanes[:3], "i": lanes[3:6], "o": lanes[6:7], "q": lanes[7:8], "k": lanes[8:9], "v": lanes[9:]}

    def load(self, src, dst):
        move = pltpu.make_async_copy(src, dst, self.local_sem.at[18 + self.loads])
        self.loads += 1
        move.start()
        return move

    def half(self, which, width):
        return columns(which * width, width)

    def share(self, src, dst, width):
        return self.net.copy(src.at[:, self.half(1 - self.c, width)], dst, self.net.ring("c", 0))

    def begin(self):
        self.greeted = self.net.greet()
        at_d = self.load(self.d_in, self.d)
        self.stream.start(0)
        self.total[...] = jnp.zeros((16, D), F32)
        self.total[G2 : G2 + 2, :] = self.two[0:2, :]
        at_d.wait()
        self.at_slope = self.load(self.slope_in, self.inner)
        for n in range(1, 4):
            self.stream.start(n)

        def body(t, carry):
            r = some_rows(t)
            low = self.d[r, :].astype(BF)
            self.outer[r, :] = low
            return carry + jnp.sum(low.astype(F32).reshape(ROWS // 8, 8, D), axis=0)

        s = lax.fori_loop(0, OWN // ROWS, body, jnp.zeros((8, D), F32))
        self.total[BU : BU + 1, :] = jnp.sum(s, axis=0, keepdims=True)
        self.at_act = self.load(self.act_in, self.act)
        self.at_low = [self.load(self.low_in.at[n], self.dx.at[pl.ds(OWN * n, OWN)]) for n in range(2)]
        self.at_n1 = [self.load(self.n1_in, self.n1), self.load(self.inv1_in, self.inv1)]
        self.at_kept = self.load(self.encoded, self.kept)
        self.at_rest = [
            self.load(self.context_in, self.context),
            self.load(self.x_in, self.x),
            self.load(self.q_in, self.q),
            self.load(self.k_in, self.k),
            self.load(self.v_in, self.v),
        ]

    def meet(self):
        self.greeted()
        self.got_outer = self.share(self.outer, self.outer_sib, 512)

    def d_inner(self):
        self.at_slope.wait()
        for n in range(4):
            self.stream.wait(n)

            cols = slice(1024 * n, 1024 * n + 1024)
            y = mm(self.outer[...], self.ring[n].reshape(1024, 1024), NT)
            y = (y * self.inner[:, cols].astype(F32)).astype(BF)
            self.inner[:, cols] = y
            s = column_sum(y)
            for dp in (2 * n, 2 * n + 1):
                for t in range(4):
                    at = 512 * (dp - 2 * n) + 128 * t
                    self.total[8 + t : 9 + t, 128 * dp : 128 * dp + 128] = s[:, at : at + 128]
            self.stream.start(n + 4)

    def share_inner(self):
        self.got_inner = self.share(self.inner, self.inner_sib, 2048)

    def grad_outer(self):
        self.at_act.wait()
        self.got_outer.wait_recv()
        c = self.c
        mine = self.outer.at[:, self.half(c, 512)]

        def body(t, carry):
            cols = columns(t * 1024, 1024)
            y = mm(self.act[c, :, cols], mine[...], TN) + mm(self.act[1 - c, :, cols], self.outer_sib[...], TN)
            self.g[5][t] = y.astype(BF).reshape(2, 2, 4, 64, 512)
            return carry

        lax.fori_loop(0, 4, body, 0, unroll=2)
        self.at_probs = self.load(self.probs_in, self.act)

    def d_normed(self):
        for n in range(4):
            self.stream.wait(4 + n)
            cols = slice(256 * n, 256 * n + 256)
            y = self.d[:, cols]
            for j in range(4):
                y = y + mm(self.inner[:, 1024 * j : 1024 * j + 1024], self.stream.part(4 + n, j), NT)
            self.d[:, cols] = y
            self.stream.start(8 + n)

    def turn_low(self):
        for move in self.at_low:
            move.wait()
        for j, which in enumerate((self.c, 1 - self.c)):
            rows = pl.ds(pl.multiple_of(OWN * which, OWN), OWN)
            for x in range(4):
                part = self.dx[rows, 256 * x : 256 * x + 256]
                self.low_t[256 * x : 256 * x + 256, OWN * j : OWN * j + OWN] = part.T

    def grad_inner(self):
        self.got_inner.wait_recv()
        c = self.c

        def body(t, carry):
            x, j = lax.div(t, 2), lax.rem(t, 2)
            rows, cols = pl.ds(pl.multiple_of(x * 256, 256), 256), columns(j * 1024, 1024)
            y = mm(self.low_t[rows, :OWN], self.inner[:, columns(c * 2048 + j * 1024, 1024)])
            y = y + mm(self.low_t[rows, OWN:], self.inner_sib[:, cols])
            self.g[4][x, :, :, :, :, cols] = y.astype(BF).reshape(2, 2, 4, 16, 1024)
            return carry

        lax.fori_loop(0, 8, body, 0, unroll=2)

    def norm_one(self):
        for move in self.at_n1:
            move.wait()

        def body(t, carry):
            r = some_rows(t)
            d, n = self.d[r, :], self.n1[r, :]
            da = norm_back(d * self.vec[G1 : G1 + 1, :], n, self.inv1[r, :1])
            low = da.astype(BF)
            self.d[r, :] = da
            self.branch[r, :] = low
            new = (d * n, d, low.astype(F32))
            return tuple(a + jnp.sum(b.reshape(ROWS // 8, 8, D), axis=0) for a, b in zip(carry, new))

        zero = jnp.zeros((8, D), F32)
        sums = lax.fori_loop(0, OWN // ROWS, body, (zero, zero, zero))
        for row, s in zip((G1, S1, BO), sums):
            self.total[row : row + 1, :] = jnp.sum(s, axis=0, keepdims=True)
        self.got_branch = self.share(self.branch, self.branch_sib, 512)

    def d_mixed(self):
        self.stream.wait(8)
        for x in range(4):
            self.d_context[:, 256 * x : 256 * x + 256] = mm(self.branch[...], self.stream.part(8, x), NT).astype(BF)

    def grad_rows(self, left, right, sib, out):
        mine = right.at[:, self.half(self.c, 512)]

        def body(x, carry):
            rows = columns(x * 256, 256)
            y = mm(left[0][:, rows], mine[...], TN) + mm(left[1][:, rows], sib[...], TN)
            out[x] = y.astype(BF).reshape(2, 2, 4, 16, 512)
            return carry

        lax.fori_loop(0, 4, body, 0, unroll=2)

    def pair(self, ref):
        return ref.at[self.c], ref.at[1 - self.c]

    def grad_output(self):
        self.got_branch.wait_recv()
        for move in self.at_rest:
            move.wait()
        self.grad_rows(self.pair(self.context), self.branch, self.branch_sib, self.g[3])

    def attend(self, first, last):
        if first == 0:
            self.at_probs.wait()
        attention_back(
            self.q,
            self.k,
            self.v,
            self.act,
            self.context.at[self.c],
            self.d_context,
            self.dq,
            self.dk,
            self.dv,
            first,
            last,
            HEADS // 4 * (1 - self.c),
        )

    def share_heads(self):
        self.got_heads = [
            self.share(self.dk, self.dk_sib, 512),
            self.share(self.dv, self.dv_sib, 512),
            self.share(self.dq, self.dq_sib, 512),
        ]

    def head_sums(self):
        self.total[BQ : BQ + 1, :] = column_sum(self.dq[...])
        self.total[BV : BV + 1, :] = column_sum(self.dv[...])
        self.vectors.start()

    def grad_key(self):
        self.got_heads[0].wait_recv()
        self.grad_rows(self.pair(self.x), self.dk, self.dk_sib, self.g[1])

    def grad_value(self):
        self.got_heads[1].wait_recv()
        self.grad_rows(self.pair(self.x), self.dv, self.dv_sib, self.g[2])

    def grad_query(self):
        self.got_heads[2].wait_recv()
        own = pl.ds(HALO, OWN)
        rows = (self.x.at[self.c, own], self.x.at[1 - self.c, own])
        self.grad_rows(rows, self.dq, self.dq_sib, self.g[0])

    def d_halo(self):
        for n in (9, 10):
            self.stream.wait(n)

        def sides(ref):
            return jnp.concatenate([ref[:HALO, :], ref[HALO + OWN :, :]], axis=0)

        for x in range(4):
            cols = slice(256 * x, 256 * x + 256)
            y = mm(sides(self.dk), self.stream.part(9, x), NT) + mm(sides(self.dv), self.stream.part(10, x), NT)
            self.dx[:HALO, cols] = y[:HALO].astype(BF)
            self.dx[HALO + OWN :, cols] = y[HALO:].astype(BF)
        self.back_rows.start()

    def d_own(self):
        self.stream.wait(11)
        own = slice(HALO, HALO + OWN)
        for x in range(4):
            cols = slice(256 * x, 256 * x + 256)
            y = mm(self.dk[own, :], self.stream.part(9, x), NT) + mm(self.dv[own, :], self.stream.part(10, x), NT)
            y = y + self.d[:, cols] + mm(self.dq[...], self.stream.part(11, x), NT)
            self.dx[own, cols] = y.astype(BF)

    def encoded_out(self):
        self.at_kept.wait()
        self.back_rows.start_encoded()

    def rows_back(self):
        self.back_rows.total()

    def finish(self):
        c, net = self.c, self.net
        done = [lane for group in ("u", "i", "o", "q", "k", "v") for lane in self.lanes[group]]
        swaps = []
        rects = list(zip(done, RECTS))
        for w in (5, 4, 3, 0, 1, 2):
            final, end = self.finals[w], self.ends[w]
            for lane, (of, (r0, rows), (base, width), _) in rects:
                if of == w:
                    final[pl.ds(r0, rows), pl.ds(base, width)] = lane.result()
            n, width = final.shape[0] // 2, final.shape[1]
            kept = final.at[pl.ds(pl.multiple_of(n * c, 8), n)]
            given = final.at[pl.ds(pl.multiple_of(n * (1 - c), 8), n)]
            swaps.append((w, net.copy(given, end.at[:, columns(c * width, width)], net.ring("c", 0))))
            end[:, columns(c * width, width)] = kept[...]
        self.vectors.done(self.small)
        stores = []
        for w, swap in swaps:
            swap.wait_recv()
            stores.append(self.load(self.ends[w], self.owned[w]))
        for store in stores:
            store.wait()
        self.back_rows.done()
        net.finish()


BACK = (
    "begin", "d_inner", "meet", "share_inner", "grad_outer", "u.p1", "encoded_out", "d_normed", "u.p1_mid", "norm_one",
    "turn_low", "d_mixed", "grad_output", "o.p1", "grad_inner", "i.p1", "attend.0.2", "attend.2.4", "share_heads",
    "attend.4.6", "u.p2", "attend.6.8", "o.p1_mid", "i.p1_mid", "head_sums", "d_halo", "grad_key", "k.p1",
    "grad_value", "v.p1", "grad_query", "q.p1", "d_own", "vectors.along_x", "i.p2", "k.p1_mid", "v.p1_mid",
    "q.p1_mid", "u.p3", "vectors.along_y", "o.p2", "rows_back", "i.p3", "vectors.along_z", "k.p2", "v.p2", "q.p2",
    "o.p3", "k.p3", "v.p3", "q.p3", "finish",
)


def backward_kernel(*refs):
    run_steps(Backward(refs[:21], refs[21:30], refs[30:]), BACK)


def backward_all(kept):
    any_space = pl.BlockSpec(memory_space=pl.ANY)
    vmem = pl.BlockSpec(memory_space=pltpu.VMEM)
    owned = [(r // 2, n) for r, n in BLOCKS]
    scratch = [((4, 2, 2, 4, 64, 1024), BF)]
    scratch += [(CHIPS + (r, n // 2), BF) for r, n in BLOCKS]
    scratch += [(s, BF) for s in reduce_buffers()]
    scratch += [((2, WIN, D), BF), ((OWN, D), BF), ((WIN, D), BF), ((WIN, D), BF), ((2, OWN, D), BF)]
    scratch += [((2, OWN, FF), BF), ((OWN, FF), BF), ((OWN, D), F32), ((OWN, 128), F32), ((OWN, D), F32)]
    scratch += [((OWN, D), BF), ((OWN, 512), BF), ((OWN, 2048), BF), ((OWN, D), BF), ((OWN, 512), BF), ((OWN, D), BF)]
    scratch += [((OWN, D), BF), ((WIN, D), BF), ((WIN, D), BF), ((OWN, 512), BF), ((WIN, 512), BF), ((WIN, 512), BF)]
    scratch += [((WIN, D), BF), ((2, HALO, D), BF), ((OWN, D), BF), ((D, 2 * OWN), BF)]
    scratch += [((16, D), F32), ((16, D), F32), ((16, D), F32), ((3, 16, 256), F32), ((2, 16, 128), F32), ((3, 16, 128), F32)]
    scratch += [((16, 128), F32), ((3, 16, 128), F32)]
    scratch += [((r, n // 2), F32) for r, n in BLOCKS] + [(s, F32) for s in owned]
    return pl.pallas_call(
        backward_kernel,
        name="backward_all",
        out_shape=[jax.ShapeDtypeStruct(s, F32) for s in owned]
        + [jax.ShapeDtypeStruct((2, TOK, D), BF)] * 2
        + [jax.ShapeDtypeStruct((8, 128), F32)],
        in_specs=[any_space] * 19 + [vmem] * 2,
        out_specs=[any_space] * 8 + [vmem],
        scratch_shapes=[pltpu.VMEM(s, t) for s, t in scratch]
        + [
            pltpu.SemaphoreType.DMA((68,)),
            pltpu.SemaphoreType.DMA((68,)),
            pltpu.SemaphoreType.DMA((40,)),
        ],
        compiler_params=pltpu.CompilerParams(collective_id=2, has_side_effects=True, vmem_limit_bytes=63 << 20),
    )(*kept)


def keep_kernel(*refs):
    (sums, *ins), outs = refs[:9], refs[9:]
    for src, dst in zip(ins, outs):
        dst[...] = src[...]
    for j, dst in enumerate(outs[8:]):
        dst[...] = sums[0:1, 8 * j : 8 * j + dst.shape[1]]


def keep(sums, *arrays):
    shapes = [(a.shape, a.dtype) for a in arrays] + [((1, 8), F32)] * 8 + [((1, 32), F32)]
    return pl.pallas_call(
        keep_kernel,
        name="keep",
        out_shape=[jax.ShapeDtypeStruct(s, t) for s, t in shapes],
        in_specs=[pl.BlockSpec(memory_space=pltpu.VMEM)] * 9,
        out_specs=[pl.BlockSpec(memory_space=pltpu.VMEM)] * 17,
    )(sums, *arrays)


def local(
    tokens, cotangent, seq_lengths, block_offsets, deal_order, wq, wk, wv, wo, bq, bv, bo, g1, s1, wi, bi, wu, bu, g2, s2
):
    small = [v[None] for v in (bq, bv, bo, g1, s1, bu, g2, s2, bi)]
    kept = forward_all(
        tokens[:, 0], cotangent[:, 0], seq_lengths[:, 0], deal_order[:, 0], (wq, wk, wv, wo, wi, wu), small
    )
    *owned, out, token_grad, sums = backward_all(kept)
    results = keep(sums, *owned, out, token_grad)
    owned, (out, token_grad), vectors = results[:6], results[6:8], results[8:]
    sbq, sbv, sbo, sg1, ss1, sbu, sg2, ss2, sbi = [v[0] for v in vectors]
    return (
        out[:, None],
        token_grad[:, None],
        *owned[:4],
        sbq,
        sbv,
        sbo,
        sg1,
        ss1,
        owned[4],
        sbi,
        owned[5],
        sbu,
        sg2,
        ss2,
    )


def solution(mesh):
    rows = P(None, "shard", "dp", None)
    table = P(None, "shard", None)
    matrix, vector = P(("dp", "shard"), None), P(("dp", "shard"))
    in_specs = (rows, rows) + (table,) * 3 + (matrix,) * 4 + (vector,) * 5 + (matrix, vector, matrix) + (vector,) * 3
    out_specs = (rows, rows) + (matrix,) * 4 + (vector,) * 5 + (matrix, vector, matrix) + (vector,) * 3
    return jax.shard_map(local, mesh=mesh, in_specs=in_specs, out_specs=out_specs, check_vma=False)
```

```python
import math

import jax
import jax.numpy as jnp
from jax import lax
from jax.experimental import pallas as pl
from jax.experimental.pallas import tpu as pltpu
from jax.sharding import PartitionSpec as P

MESH = pl.DeviceIdType.MESH
BF = jnp.bfloat16
F32 = jnp.float32
D = 1024
FF = 4096
HEADS = 16
HEAD = 64
TOK = 128
OWN = 2 * TOK
HALO = 192
WIN = OWN + 2 * HALO
AXES = ("x", "y", "z")
ORDER = (("z", "y", "x"), ("x", "z", "y"), ("y", "x", "z"))
CHIPS = (4, 2, 2, 4)


def position():
    dp, sh = lax.axis_index("dp"), lax.axis_index("shard")
    return {
        "x": lax.div(dp, 2),
        "y": lax.div(sh, 8) * 2 + lax.rem(dp, 2),
        "z": lax.div(lax.rem(sh, 8), 2),
        "c": lax.rem(sh, 2),
    }


def device_at(at):
    return (
        at["x"] * 2 + lax.rem(at["y"], 2),
        lax.div(at["y"], 2) * 8 + at["z"] * 2 + at["c"],
    )


class Batch:
    def __init__(self, net, whole):
        self.net, self.whole = net, whole
        self.k = net.used
        net.used += 1
        net.batches.append(self)

    def send(self, src, dst, device):
        pltpu.make_async_remote_copy(
            src_ref=src,
            dst_ref=dst,
            send_sem=self.net.send_sem.at[self.k],
            recv_sem=self.net.recv_sem.at[self.k],
            device_id=device,
            device_id_type=MESH,
        ).start()

    def wait_recv(self):
        pltpu.make_async_copy(self.whole, self.whole, self.net.recv_sem.at[self.k]).wait()

    def wait_send(self):
        pltpu.make_async_copy(self.whole, self.whole, self.net.send_sem.at[self.k]).wait()


class Net:
    def __init__(self, send_sem, recv_sem):
        self.me = position()
        self.send_sem, self.recv_sem = send_sem, recv_sem
        self.used = 0
        self.batches = []

    def moved(self, axis, by):
        at = dict(self.me)
        if axis == "c":
            at["c"] = 1 - at["c"]
        else:
            at[axis] = lax.rem(at[axis] + by, 4)
        return at

    def ring(self, axis, by):
        return device_at(self.moved(axis, by))

    def pair(self, lo):
        at = dict(self.me)
        at["y"] = lax.div(at["y"], 2) * 2 + lo
        return device_at(at)

    def copy(self, src, dst, device):
        batch = Batch(self, dst)
        batch.send(src, dst, device)
        return batch

    def greet(self):
        bar = pltpu.get_barrier_semaphore()
        peers = [self.ring("c", 0)] + [self.ring(a, b) for a in AXES for b in (1, 2, 3)]
        for p in peers:
            pl.semaphore_signal(bar, inc=1, device_id=p, device_id_type=MESH)
        return lambda: pl.semaphore_wait(bar, len(peers))

    def finish(self):
        for batch in self.batches:
            batch.wait_send()
        assert self.used <= self.send_sem.shape[0], self.used


def chip_index(at, drop=()):
    out = []
    for axis in AXES:
        if axis in drop:
            continue
        v = at[axis]
        if axis == "y":
            if v is None:
                out += [slice(None), slice(None)]
            elif isinstance(v, tuple):
                out += [v[1], slice(None)]
            else:
                out += [lax.rem(v, 2), lax.div(v, 2)]
        elif v is None:
            out.append(slice(None))
        elif isinstance(v, tuple):
            out.append(pl.ds(2 * v[1], 2))
        else:
            out.append(v)
    return tuple(out)


def chip_shape(drop):
    shape = ()
    for axis in AXES:
        if axis not in drop:
            shape += (2, 2) if axis == "y" else (4,)
    return shape


def columns(base, width):
    return pl.ds(pl.multiple_of(base, 128), width)


class Gather:
    def __init__(self, net, ref, rows, cols, order):
        self.net, self.ref, self.rows, self.cols = net, ref, rows, cols
        self.a, self.b, self.e = order

    def at(self, **over):
        place = {k: self.net.me[k] for k in AXES}
        place.update(over)
        return self.ref.at[chip_index(place) + (self.rows, self.cols)]

    def send(self, batch, region, axis, by):
        batch.send(region, region, self.net.ring(axis, by))

    def blocks(self, *chips):
        return Batch(self.net, self.ref.at[chips + (self.rows, self.cols)])

    def p1(self):
        self.c = self.blocks(pl.ds(0, 3), 0, 0, 0)
        for d in (1, 3, 2):
            self.send(self.c, self.at(), self.a, d)

    def p2(self):
        self.c.wait_recv()
        self.c = self.blocks(pl.ds(0, 3), 0, 0, slice(None))
        for d in (1, 3, 2):
            self.send(self.c, self.at(**{self.a: None}), self.b, d)

    def p2_ring(self):
        self.c.wait_recv()
        self.c = self.blocks(pl.ds(0, 2), 0, 0, slice(None))
        for d in (1, 3):
            self.send(self.c, self.at(**{self.a: None}), self.b, d)

    def p2_mid(self):
        self.c.wait_recv()
        self.c = self.blocks(0, 0, 0, slice(None))
        for h, to in enumerate((1, 3)):
            b = self.net.moved(self.b, 4 - to)[self.b]
            self.send(self.c, self.at(**{self.a: ("half", h), self.b: b}), self.b, to)

    def part(self, h, by):
        e = self.net.moved(self.e, by)[self.e]
        return self.at(**{self.a: h if h is None else ("half", h), self.b: None, self.e: e})

    def quarter(self):
        return Batch(self.net, self.part(None, 0))

    def p3(self):
        self.c.wait_recv()
        self.near, self.far = self.quarter(), self.quarter()
        self.send(self.near, self.part(0, 0), self.e, 1)
        self.send(self.near, self.part(1, 0), self.e, 3)
        self.send(self.far, self.part(1, 0), self.e, 1)
        self.send(self.far, self.part(0, 0), self.e, 3)
        self.core = self.blocks(*(slice(None),) * 4)
        self.send(self.core, self.part(None, 0), "c", 0)

    def p3_mid(self):
        self.near.wait_recv()
        self.last = self.quarter()
        self.send(self.last, self.part(0, 3), self.e, 1)
        self.send(self.last, self.part(1, 1), self.e, 3)

    def p3_core(self):
        self.far.wait_recv()
        self.send(self.core, self.part(None, 3), "c", 0)
        self.send(self.core, self.part(None, 1), "c", 0)

    def p3_end(self):
        self.last.wait_recv()
        self.send(self.core, self.part(None, 2), "c", 0)

    def done(self):
        self.core.wait_recv()


def each(lanes, step):
    for lane in lanes:
        getattr(lane, step)()


def rows_at(base, count):
    return pl.ds(pl.multiple_of(base, TOK // 2), count)


class Window:
    def __init__(self, net, tokens, cotangent, window, cots, local_sem):
        self.net, self.window, self.cots = net, window, cots
        self.tokens, self.cotangent, self.local_sem = tokens, cotangent, local_sem
        self.lo = lax.rem(net.me["y"], 2)

    def pair(self, src, dst, sem):
        local = pltpu.make_async_copy(src.at[self.lo], dst, sem)
        local.start()
        return local, self.net.copy(src.at[1 - self.lo], dst, self.net.pair(1 - self.lo))

    def start(self):
        mine = self.window.at[rows_at(HALO + TOK * self.lo, TOK)]
        self.rows = self.pair(self.tokens, mine, self.local_sem.at[0])

    def start_cots(self):
        mine = self.cots.at[rows_at(TOK * self.lo, TOK)]
        self.cot_rows = self.pair(self.cotangent, mine, self.local_sem.at[1])

    def halo(self):
        local, moved = self.rows
        local.wait()
        moved.wait_recv()
        w, net = self.window, self.net
        self.c = Batch(net, w.at[pl.ds(0, 2 * HALO)])
        self.c.send(w.at[pl.ds(OWN, HALO)], w.at[pl.ds(0, HALO)], net.ring("x", 1))
        self.c.send(w.at[pl.ds(HALO, HALO)], w.at[pl.ds(HALO + OWN, HALO)], net.ring("x", 3))

    def done(self):
        self.c.wait_recv()

    def cots_done(self):
        local, moved = self.cot_rows
        local.wait()
        moved.wait_recv()


def place_own(me, mine, peer, full):
    here = chip_index(me)
    c = me["c"]
    first = c == 0

    def both(a, b):
        return jnp.concatenate([jnp.where(first, a, b), jnp.where(first, b, a)], axis=0)

    half = columns(c * 512, 512)
    for j in range(4):
        r = slice(8 * j, 8 * j + 8)
        full[j][here + (slice(None), half)] = both(mine[r, half], peer[r, half])
    for t in range(2):
        r, s = slice(32 + 8 * t, 40 + 8 * t), slice(48 + 8 * t, 56 + 8 * t)
        a = jnp.where(first, mine[r, :], mine[s, :])
        b = jnp.where(first, peer[r, :], peer[s, :])
        full[4][here + (slice(None), columns(c * 2048 + 1024 * t, 1024))] = both(a, b)
    full[5][here + (slice(None), half)] = both(mine[64:96, half], peer[64:96, half])


BLOCKS = ((16, 1024),) * 4 + ((16, 4096), (64, 1024))


SPAN = TOK + 2 * HALO
NT = (((1,), (1,)), ((), ()))
TN = (((0,), (0,)), ((), ()))
NN = (((1,), (0,)), ((), ()))


def mm(a, b, dims=NN):
    return lax.dot_general(a, b, dims, preferred_element_type=F32)


def tile(w, n0, n):
    return w[:, :, :, :, :, columns(n0, n)].reshape(-1, n)


def project(rows, w, out, bias=None, n=1024):
    def body(t, carry):
        cols = columns(t * n, n)
        y = mm(rows[...], tile(w, t * n, n))
        if bias is not None:
            y = y + bias[:, cols]
        out[:, cols] = y.astype(BF)
        return carry

    lax.fori_loop(0, out.shape[1] // n, body, 0)


def lane_split(x):
    low = lax.broadcasted_iota(jnp.int32, x.shape, 1) < HEAD
    zero = jnp.zeros_like(x)
    return jnp.concatenate([jnp.where(low, x, zero), jnp.where(low, zero, x)], axis=0)


def lane_join(x):
    n = x.shape[0] // 2
    low = lax.broadcasted_iota(jnp.int32, (n, x.shape[1]), 1) < HEAD
    return jnp.where(low, x[:n], x[n:])


def attention(q, k, v, bias, probs, context, first, last):
    def body(h, carry):
        cols = columns(h * 128, 128)
        for b in range(2):
            mine, near = pl.ds(b * TOK, TOK), pl.ds(b * TOK, SPAN)
            some, two = k[near, cols], lane_split(q[mine, cols]) * jnp.asarray(0.125, BF)
            p = []
            for s in range(2):
                e = mm(some, two[s * TOK : s * TOK + TOK], NT) + bias[b]
                e = jnp.exp(e - jnp.max(e, axis=0, keepdims=True))
                p.append((e * (1.0 / jnp.sum(e, axis=0, keepdims=True))).astype(BF))
            p = jnp.concatenate(p, axis=1)
            at = columns((2 * h + b) * OWN, OWN)
            probs[0, :, at], probs[1, :, at] = p[:OWN], p[OWN:]
            y = mm(v[near, cols], p, TN)
            y = jnp.concatenate([y[:HEAD, :TOK], y[HEAD:, TOK:]], axis=0)
            context[mine, cols] = y.T.astype(BF)
        return carry

    lax.fori_loop(first, last, body, 0, unroll=2)


def normalized(a):
    centred = a - jnp.mean(a, axis=-1, keepdims=True)
    inv = lax.rsqrt(jnp.mean(centred * centred, axis=-1, keepdims=True) + 1e-05)
    return centred * inv, inv


def norm_back(dn, n, inv):
    return inv * (dn - jnp.mean(dn, axis=-1, keepdims=True) - n * jnp.mean(dn * n, axis=-1, keepdims=True))


def feed_in(low, wi, bi, act, slope, first, last, n=512):
    def body(t, carry):
        cols = columns(t * n, n)
        u = mm(low[...], tile(wi, t * n, n)) + bi[:, cols]
        phi = 0.5 + 0.5 * lax.erf(u * math.sqrt(0.5))
        act[:, cols] = (u * phi).astype(BF)
        slope[:, cols] = (phi + u * (jnp.exp(-0.5 * (u * u)) * (1.0 / math.sqrt(2 * math.pi)))).astype(BF)
        return carry

    lax.fori_loop(first, last, body, 0, unroll=2)


ROWS = 32


def some_rows(t):
    return pl.ds(pl.multiple_of(t * ROWS, ROWS), ROWS)


def segment_bias(lengths, order, start, lo, bias):
    ends, total = [], 0
    for k in range(16):
        total = total + lengths[lo, order[lo, k]]
        ends.append(total)

    def which(at):
        found = jnp.where(at < 0, -1, 0)
        for e in ends:
            found = found + (at >= e).astype(jnp.int32)
        return found

    keys = which(start + lax.broadcasted_iota(jnp.int32, (WIN, TOK), 0))
    queries = which(start + HALO + lax.broadcasted_iota(jnp.int32, (8, OWN), 1))[:1]
    for b in range(2):
        same = keys[b * TOK : b * TOK + SPAN] == queries[:, b * TOK : b * TOK + TOK]
        bias[b] = jnp.where(same, 0.0, -1e30)


class Vectors:
    def __init__(self, net, small, rows, tiles, vec, inner):
        self.net, self.small, self.rows = net, small, rows
        self.own, self.sib, self.tz, self.ty, self.tx = tiles
        self.vec, self.inner = vec, inner

    def around(self, axis, tiles, mine):
        self.c = Batch(self.net, tiles.at[pl.ds(0, 3)])
        for d in (1, 3, 2):
            self.c.send(tiles.at[mine], tiles.at[mine], self.net.ring(axis, d))

    def place(self):
        sh = lax.axis_index("shard")
        self.rows[...] = jnp.zeros((16, 128), F32)
        for j in range(9):
            n = self.small[j].shape[1]
            self.rows[j : j + 1, :n] = self.small[j][...].astype(F32)
        i = lax.broadcasted_iota(jnp.int32, (128, 128), 0)
        to = lax.broadcasted_iota(jnp.int32, (128, 128), 1)
        value = self.rows[...].astype(BF)
        eight = mm(value, jnp.where((to == 8 * sh + i) & (i < 8), 1.0, 0.0).astype(BF))
        many = mm(value, jnp.where((to == 32 * lax.rem(sh, 4) + i) & (i < 32), 1.0, 0.0).astype(BF))
        r = lax.broadcasted_iota(jnp.int32, (16, 128), 0)
        many = jnp.broadcast_to(many[8:9], (16, 128))
        tile = jnp.where(r < 8, eight, jnp.where(r == 8 + lax.div(sh, 4), many, 0.0))
        self.own[...] = tile.astype(BF)

    def start(self):
        self.c = self.net.copy(self.own, self.sib, self.net.ring("c", 0))

    def wait(self):
        self.c.wait_recv()

    def along_z(self):
        self.wait()
        z = self.net.me["z"]
        self.tz[z] = self.own[...] + self.sib[...]
        self.around("z", self.tz, z)

    def along_y(self):
        self.wait()
        y = self.net.me["y"]
        self.ty[y] = (self.tz[0] + self.tz[1]) + (self.tz[2] + self.tz[3])
        self.around("y", self.ty, y)

    def along_x(self):
        self.wait()
        x = self.net.me["x"]
        self.tx[x, 0] = self.ty[0] + self.ty[2]
        self.tx[x, 1] = self.ty[1] + self.ty[3]
        self.around("x", self.tx, x)

    def done(self):
        self.wait()
        for dp in range(8):
            got = self.tx[dp // 2, dp % 2].astype(F32)
            self.vec[:, 128 * dp : 128 * dp + 128] = got[:8]
            for t in range(4):
                at = 512 * dp + 128 * t
                self.inner[:, at : at + 128] = got[8 + t : 9 + t]


BQ, BV, BO, G1, S1, BU, G2, S2 = range(8)


class Forward:
    def __init__(self, ins, outs, scratch):
        self.tokens, self.cotangent, self.lengths, self.order = ins[:4]
        self.own, self.small = ins[4:10], ins[10:]
        self.weights_out = outs[:6]
        (self.x_out, self.q_out, self.k_out, self.v_out, self.probs_out, self.context_out, self.low_out) = outs[6:13]
        (self.act_out, self.slope_out, self.n1_out, self.inv1_out, self.d_out, self.encoded_out) = outs[13:19]
        self.vec_out, self.two_out = outs[19:]
        self.mine, self.peer = scratch[:2]
        self.full, scratch = scratch[2:8], scratch[8:]
        (self.window, self.cots, self.q, self.k, self.v, self.probs, self.context, self.low) = scratch[:8]
        (self.act, self.slope, self.bias, self.n1, self.inv1, self.normed, self.total, self.encoded) = scratch[8:16]
        self.vec, self.inner, self.two, self.placed = scratch[16:20]
        tiles, (send_sem, recv_sem, self.local_sem) = scratch[20:25], scratch[25:]
        self.net = Net(send_sem, recv_sem)
        self.me, self.c = self.net.me, self.net.me["c"]
        self.lo = lax.rem(self.me["y"], 2)
        self.stores, self.gets = [], []
        self.vectors = Vectors(self.net, self.small, self.placed, tiles, self.vec, self.inner)
        self.view = Window(self.net, self.tokens, self.cotangent, self.window, self.cots, self.local_sem)
        rows, half = slice(None), columns(self.c * 512, 512)
        wi, wu = self.full[4], self.full[5]

        def inner(base, width, order):
            return Gather(self.net, wi, rows, columns(self.c * 2048 + base, width), ORDER[order])

        self.lanes = {
            "a": [Gather(self.net, self.full[j], rows, half, ORDER[j]) for j in range(3)],
            "b": [Gather(self.net, self.full[3], rows, half, ORDER[2]), inner(0, 1024, 1), inner(1024, 1024, 2)],
            "u": [
                Gather(self.net, wu, pl.ds(0, 32), half, ORDER[0]),
                Gather(self.net, wu, pl.ds(32, 16), half, ORDER[1]),
                Gather(self.net, wu, pl.ds(48, 16), half, ORDER[2]),
            ],
        }

    def store(self, src, dst):
        move = pltpu.make_async_copy(src, dst, self.local_sem.at[2 + len(self.stores)])
        move.start()
        self.stores.append(move)

    def both(self, src, dst):
        self.gets.append(self.net.copy(src, dst.at[self.c], self.net.ring("c", 0)))
        self.store(src, dst.at[self.c])

    def begin(self):
        greeted = self.net.greet()
        for j in range(4):
            self.mine[8 * j : 8 * j + 8, :] = self.own[j][...]
            self.mine[32 + 8 * j : 40 + 8 * j, :] = self.own[4][:, 1024 * j : 1024 * j + 1024]
        self.mine[64:96, :] = self.own[5][...]
        self.vectors.place()
        segment_bias(self.lengths, self.order, self.me["x"] * OWN - HALO, self.lo, self.bias)
        greeted()
        swap = self.net.copy(self.mine, self.peer, self.net.ring("c", 0))
        self.view.start()
        self.vectors.start()
        swap.wait_recv()
        place_own(self.me, self.mine, self.peer, self.full)

    def halo(self):
        self.view.halo()

    def cots_in(self):
        self.view.start_cots()

    def rows_done(self):
        self.view.done()
        self.both(self.window, self.x_out)

    def query(self):
        project(self.window.at[pl.ds(HALO, OWN)], self.full[0], self.q, self.vec.at[BQ : BQ + 1])

    def key(self):
        project(self.window, self.full[1], self.k)

    def value(self):
        project(self.window, self.full[2], self.v, self.vec.at[BV : BV + 1])

    def keep_heads(self):
        for j in range(3):
            self.store(self.full[j], self.weights_out[j])
        for src, dst in ((self.q, self.q_out), (self.k, self.k_out), (self.v, self.v_out)):
            self.store(src, dst)

    def attend(self, first, last):
        attention(self.q, self.k, self.v, self.bias, self.probs, self.context, first, last)

    def keep_probs(self):
        self.both(self.context, self.context_out)
        self.store(self.probs, self.probs_out)

    def mix(self):
        self.store(self.full[3], self.weights_out[3])
        self.store(self.full[4], self.weights_out[4])

        def body(t, carry):
            cols = columns(t * 512, 512)
            y = mm(self.context[...], tile(self.full[3], t * 512, 512)) + self.vec[BO : BO + 1, cols]
            self.total[:, cols] = y + self.window[pl.ds(HALO, OWN), cols].astype(F32)
            return carry

        lax.fori_loop(0, 2, body, 0, unroll=2)

    def norm_one(self):
        def body(t, carry):
            r = some_rows(t)
            n, inv = normalized(self.total[r, :])
            self.n1[r, :] = n
            self.inv1[r, :] = jnp.broadcast_to(inv, (ROWS, 128))
            y = n * self.vec[G1 : G1 + 1, :] + self.vec[S1 : S1 + 1, :]
            self.normed[r, :] = y
            self.low[r, :] = y.astype(BF)
            return carry

        lax.fori_loop(0, OWN // ROWS, body, 0)
        self.both(self.low, self.low_out)
        self.store(self.n1, self.n1_out)
        self.store(self.inv1, self.inv1_out)

    def feed_in(self, first, last):
        feed_in(self.low, self.full[4], self.inner, self.act, self.slope, first, last)
        if last == FF // 512:
            self.both(self.act, self.act_out)
            self.store(self.slope, self.slope_out)
            self.store(self.vec, self.vec_out)

    def feed_out(self):
        self.store(self.full[5], self.weights_out[5])

        def body(t, carry):
            cols = columns(t * 512, 512)
            y = mm(self.act[...], tile(self.full[5], t * 512, 512)) + self.vec[BU : BU + 1, cols]
            self.total[:, cols] = y + self.normed[:, cols]
            return carry

        lax.fori_loop(0, 2, body, 0, unroll=2)

    def cots_done(self):
        self.view.cots_done()

    def norm_two(self):
        def body(t, carry):
            r = some_rows(t)
            n, inv = normalized(self.total[r, :])
            gain = self.vec[G2 : G2 + 1, :]
            self.encoded[r, :] = (n * gain + self.vec[S2 : S2 + 1, :]).astype(BF)
            d = self.cots[r, :].astype(F32)
            self.normed[r, :] = norm_back(d * gain, n, inv)
            dn = jnp.sum((d * n).reshape(ROWS // 8, 8, D), axis=0)
            return carry[0] + dn, carry[1] + jnp.sum(d.reshape(ROWS // 8, 8, D), axis=0)

        zero = jnp.zeros((8, D), F32)
        gain_sum, shift_sum = lax.fori_loop(0, OWN // ROWS, body, (zero, zero))
        self.two[0:1, :] = jnp.sum(gain_sum, axis=0, keepdims=True)
        self.two[1:2, :] = jnp.sum(shift_sum, axis=0, keepdims=True)
        self.two[2:8, :] = jnp.zeros((6, D), F32)
        self.store(self.normed, self.d_out)
        self.store(self.encoded, self.encoded_out)
        self.store(self.two, self.two_out)

    def finish(self):
        for got in self.gets:
            got.wait_recv()
        for move in self.stores:
            move.wait()
        self.net.finish()


FORE = (
    "begin", "a.p1", "b.p1", "u.p1", "vectors.along_z", "a.p2", "b.p2_ring", "u.p2_ring", "vectors.along_y",
    "a.p3", "b.p2_mid", "u.p2_mid", "halo", "vectors.along_x", "a.p3_mid", "b.p3", "cots_in", "a.p3_core",
    "a.p3_end", "vectors.done", "a.done", "b.p3_mid", "u.p3", "query", "rows_done", "key", "value",
    "attend.0.2", "b.p3_core", "attend.2.4", "b.p3_end", "attend.4.6", "u.p3_mid", "attend.6.8", "keep_heads",
    "u.p3_core", "keep_probs", "b.done", "mix", "norm_one", "feed_in.0.2", "feed_in.2.4", "u.p3_end",
    "feed_in.4.6", "feed_in.6.8", "u.done", "feed_out", "cots_done", "norm_two", "finish",
)


def run_steps(work, steps):
    for step in steps:
        name, *rest = step.split(".")
        if name in work.lanes:
            each(work.lanes[name], rest[0])
        elif name == "vectors":
            getattr(work.vectors, rest[0])()
        else:
            getattr(work, name)(*map(int, rest))


def forward_kernel(*refs):
    run_steps(Forward(refs[:19], refs[19:40], refs[40:]), FORE)


def forward_all(tokens, cotangent, lengths, order, own, small):
    any_space = pl.BlockSpec(memory_space=pl.ANY)
    vmem = pl.BlockSpec(memory_space=pltpu.VMEM)
    smem = pl.BlockSpec(memory_space=pltpu.SMEM)
    full = [(CHIPS + s, BF) for s in BLOCKS]
    kept = [
        ((2, WIN, D), BF),
        ((OWN, D), BF),
        ((WIN, D), BF),
        ((WIN, D), BF),
        ((2, OWN, FF), BF),
        ((2, OWN, D), BF),
        ((2, OWN, D), BF),
        ((2, OWN, FF), BF),
        ((OWN, FF), BF),
        ((OWN, D), F32),
        ((OWN, 128), F32),
        ((OWN, D), F32),
        ((OWN, D), BF),
        ((8, D), F32),
        ((8, D), F32),
    ]
    scratch = [((96, 1024), BF)] * 2 + full
    scratch += [((WIN, D), BF), ((OWN, D), BF), ((OWN, D), BF), ((WIN, D), BF), ((WIN, D), BF)]
    scratch += [((2, OWN, FF), BF), ((OWN, D), BF), ((OWN, D), BF), ((OWN, FF), BF), ((OWN, FF), BF)]
    scratch += [((2, SPAN, TOK), F32), ((OWN, D), F32), ((OWN, 128), F32), ((OWN, D), F32), ((OWN, D), F32)]
    scratch += [((OWN, D), BF), ((8, D), F32), ((1, FF), F32), ((8, D), F32), ((16, 128), F32)]
    scratch += [((16, 128), BF)] * 2 + [((4, 16, 128), BF)] * 2 + [((4, 2, 16, 128), BF)]
    return pl.pallas_call(
        forward_kernel,
        name="forward_all",
        out_shape=[jax.ShapeDtypeStruct(s, t) for s, t in full + kept],
        in_specs=[any_space] * 2 + [smem] * 2 + [vmem] * 15,
        out_specs=[any_space] * 21,
        scratch_shapes=[pltpu.VMEM(s, t) for s, t in scratch]
        + [
            pltpu.SemaphoreType.DMA((80,)),
            pltpu.SemaphoreType.DMA((80,)),
            pltpu.SemaphoreType.DMA((24,)),
        ],
        compiler_params=pltpu.CompilerParams(collective_id=1, has_side_effects=True, vmem_limit_bytes=62 << 20),
    )(tokens, cotangent, lengths, order, *own, *small)


def add_into(dst, srcs):
    lead = dst.shape[:-2]
    loop = lead[:-1] if len(lead) > 1 else lead
    total = math.prod(loop)

    def body(k, carry):
        index, rest = (), k
        for n in reversed(loop):
            index = (lax.rem(rest, n),) + index
            rest = lax.div(rest, n)
        value = dst[index].astype(F32)
        for s in srcs:
            value = value + s[index].astype(F32)
        dst[index] = value.astype(BF)
        return carry

    lax.fori_loop(0, total, body, 0)


class Reduce:
    def __init__(self, net, ref, rows, cols, order, bufs):
        self.net, self.ref, self.rows, self.cols = net, ref, rows, cols
        self.a, self.b, self.e = order
        self.wide, self.mid, self.low = bufs
        self.ringed = False

    def at(self, **over):
        place = {k: self.net.me[k] for k in AXES}
        place.update(over)
        return self.ref.at[chip_index(place) + (self.rows, self.cols)]

    def quarter(self, by, h):
        b = None if h is None else ("half", h)
        return self.at(**{self.a: self.net.moved(self.a, by)[self.a], self.b: b, self.e: None})

    def buf(self, k, h):
        b = None if h is None else ("half", h)
        return self.wide.at[(k,) + chip_index({self.b: b, self.e: None}, drop=(self.a,))]

    def send(self, batch, by, h, k, to):
        batch.send(self.quarter(by, h), self.buf(k, h), self.net.ring(self.a, to))

    def p1(self):
        self.near = Batch(self.net, self.buf(0, None))
        self.send(self.near, 2, 0, 0, 1)
        self.send(self.near, 2, 1, 0, 3)
        self.far = Batch(self.net, self.wide.at[pl.ds(1, 2)])
        self.send(self.far, 1, 1, 1, 1)
        self.send(self.far, 3, 0, 2, 3)

    def p1_mid(self):
        self.near.wait_recv()
        add_into(self.quarter(1, 0), [self.buf(0, 0)])
        self.send(self.far, 1, 0, 1, 1)
        add_into(self.quarter(3, 1), [self.buf(0, 1)])
        self.send(self.far, 3, 1, 2, 3)

    def p2(self):
        self.far.wait_recv()
        add_into(self.quarter(0, None), [self.buf(1, None), self.buf(2, None)])
        self.c = Batch(self.net, self.mid)
        for k, d in enumerate((1, 3, 2)):
            there = self.net.moved(self.b, d)[self.b]
            self.c.send(self.at(**{self.b: there, self.e: None}), self.mid.at[k], self.net.ring(self.b, d))

    def line(self, by, h):
        e = None if h is None else ("half", h)
        return self.at(**{self.b: self.net.moved(self.b, by)[self.b], self.e: e})

    def line_buf(self, k, h):
        e = None if h is None else ("half", h)
        return self.mid.at[(k,) + chip_index({self.e: e}, drop=(self.a, self.b))]

    def send_line(self, batch, by, h, k, to):
        batch.send(self.line(by, h), self.line_buf(k, h), self.net.ring(self.b, to))

    def p2_ring(self):
        self.far.wait_recv()
        add_into(self.quarter(0, None), [self.buf(1, None), self.buf(2, None)])
        self.near = Batch(self.net, self.line_buf(0, None))
        self.send_line(self.near, 2, 0, 0, 1)
        self.send_line(self.near, 2, 1, 0, 3)
        self.c = Batch(self.net, self.mid.at[pl.ds(1, 2)])
        self.send_line(self.c, 1, 1, 1, 1)
        self.send_line(self.c, 3, 0, 2, 3)

    def p2_mid(self):
        self.near.wait_recv()
        add_into(self.line(1, 0), [self.line_buf(0, 0)])
        self.send_line(self.c, 1, 0, 1, 1)
        add_into(self.line(3, 1), [self.line_buf(0, 1)])
        self.send_line(self.c, 3, 1, 2, 3)
        self.ringed = True

    def p3(self):
        self.c.wait_recv()
        add_into(self.at(**{self.e: None}), [self.mid.at[k] for k in range(1 if self.ringed else 0, 3)])
        self.c = Batch(self.net, self.low)
        for k, d in enumerate((1, 3, 2)):
            there = self.net.moved(self.e, d)[self.e]
            self.c.send(self.at(**{self.e: there}), self.low.at[k], self.net.ring(self.e, d))

    def result(self):
        self.c.wait_recv()
        value = self.at()[...].astype(F32)
        for k in range(3):
            value = value + self.low[k].astype(F32)
        return value


RECTS = (
    (5, (0, 16), (0, 512), 0),
    (5, (16, 16), (0, 512), 1),
    (5, (32, 32), (0, 512), 2),
    (4, (0, 16), (0, 768), 0),
    (4, (0, 16), (768, 512), 1),
    (4, (0, 16), (1280, 768), 2),
    (3, (0, 16), (0, 512), 1),
    (0, (0, 16), (0, 512), 0),
    (1, (0, 16), (0, 512), 1),
    (2, (0, 16), (0, 512), 2),
)
LANES = ("u0", "u1", "u2", "i0", "i1", "i2", "o", "q", "k", "v")
BIG_FIRST = tuple(tuple(reversed(o)) for o in ORDER)


def reduce_buffers():
    shapes = []
    for _, (_, rows), (_, width), order in RECTS:
        a, b, e = BIG_FIRST[order]
        shapes += [
            (3,) + chip_shape((a,)) + (rows, width),
            (3,) + chip_shape((a, b)) + (rows, width),
            (3, rows, width),
        ]
    return shapes


class VectorSum:
    def __init__(self, net, total, bufs):
        self.net, self.total = net, total
        self.sib, self.whole, self.vx, self.half, self.vy, self.one, self.vz = bufs

    def start(self):
        self.c = self.net.copy(self.total, self.sib, self.net.ring("c", 0))

    def around(self, axis, bufs, part):
        self.c = Batch(self.net, bufs)
        for k, d in enumerate((1, 3, 2)):
            self.c.send(part(self.net.moved(axis, d)[axis]), bufs.at[k], self.net.ring(axis, d))

    def along_x(self):
        self.c.wait_recv()
        self.whole[...] = self.total[...] + self.sib[...]
        self.around("x", self.vx, lambda x: self.whole.at[:, columns(256 * x, 256)])

    def along_y(self):
        self.c.wait_recv()
        mine = self.whole[:, columns(256 * self.net.me["x"], 256)]
        for k in range(3):
            mine = mine + self.vx[k]
        self.half[0], self.half[1] = mine[:, :128], mine[:, 128:]
        self.around("y", self.vy, lambda y: self.half.at[lax.rem(y, 2)])

    def along_z(self):
        self.c.wait_recv()
        mine = self.half[lax.rem(self.net.me["y"], 2)]
        for k in range(3):
            mine = mine + self.vy[k]
        self.one[...] = mine
        self.around("z", self.vz, lambda z: self.one)

    def done(self, out):
        self.c.wait_recv()
        t = (self.one[...] + self.vz[0]) + (self.vz[1] + self.vz[2])
        sh = lax.axis_index("shard")
        to = lax.broadcasted_iota(jnp.int32, (128, 128), 0)
        i = lax.broadcasted_iota(jnp.int32, (128, 128), 1)
        place = jnp.where(i < 64, 8 * sh + (i & 7), 32 * lax.rem(sh, 4) + i - 64)
        pick = jnp.where((place == to) & (i < 96), 1.0, 0.0).astype(BF)
        high = t.astype(BF)
        rest = t - high.astype(F32)
        mid = rest.astype(BF)
        last = (rest - mid.astype(F32)).astype(BF)
        got = (mm(high, pick) + mm(mid, pick)) + mm(last, pick)
        r = lax.broadcasted_iota(jnp.int32, (16, 128), 0)
        i = lax.broadcasted_iota(jnp.int32, (16, 128), 1)
        keep = ((i < 64) & (lax.shift_right_logical(i, 3) == r)) | ((i >= 64) & (r == 8 + lax.div(sh, 4)))
        out[...] = jnp.broadcast_to(jnp.sum(jnp.where(keep, got, 0.0), axis=0, keepdims=True), (8, 128))


def attention_back(q, k, v, probs, context, d_context, dq, dk, dv, first, last, start):
    def body(i, carry):
        h = lax.rem(i + start, HEADS // 2)
        cols = columns(h * 128, 128)
        dks, dvs = [], []
        for b in range(2):
            mine, near = pl.ds(b * TOK, TOK), pl.ds(b * TOK, SPAN)
            at = columns((2 * h + b) * OWN, OWN)
            p = jnp.concatenate([probs[0, :, at], probs[1, :, at]], axis=0)
            dc = d_context[mine, cols]
            dc2 = lane_split(dc)
            prod = (dc.astype(F32) * context[mine, cols].astype(F32)).T
            dr = []
            for s in range(2):
                own = slice(s * TOK, s * TOK + TOK)
                dsum = jnp.sum(prod[s * HEAD : s * HEAD + HEAD], axis=0, keepdims=True)
                dp = mm(v[near, cols], dc2[own], NT)
                dr.append((p[:, own].astype(F32) * ((dp - dsum) * 0.125)).astype(BF))
            dr = jnp.concatenate(dr, axis=1)
            dvs.append(mm(p, dc2))
            dks.append(mm(dr, lane_split(q[mine, cols])))
            g = mm(k[near, cols], dr, TN)
            g = jnp.concatenate([g[:HEAD, :TOK], g[HEAD:, TOK:]], axis=0)
            dq[mine, cols] = g.T.astype(BF)
        for d, o in ((dks, dk), (dvs, dv)):
            o[0:TOK, cols] = d[0][:TOK].astype(BF)
            o[TOK:SPAN, cols] = (d[0][TOK:] + d[1][: SPAN - TOK]).astype(BF)
            o[SPAN:WIN, cols] = d[1][SPAN - TOK :].astype(BF)
        return carry

    lax.fori_loop(first, last, body, 0, unroll=2)


def column_sum(x):
    n, width = x.shape
    return jnp.sum(jnp.sum(x.astype(F32).reshape(n // 8, 8, width), axis=0), axis=0, keepdims=True)


class Return:
    def __init__(self, net, window, encoded, back, out, token_grad, sems):
        self.net, self.window, self.encoded, self.back = net, window, encoded, back
        self.out, self.token_grad, self.sems = out, token_grad, sems
        self.swaps = []
        self.lo = lax.rem(net.me["y"], 2)

    def pair(self, src, dst, sem):
        mine, theirs = rows_at(TOK * self.lo, TOK), rows_at(TOK * (1 - self.lo), TOK)
        local = pltpu.make_async_copy(src.at[mine], dst.at[self.lo], sem)
        local.start()
        return local, self.net.copy(src.at[theirs], dst.at[self.lo], self.net.pair(1 - self.lo))

    def start_encoded(self):
        self.swaps.append(self.pair(self.encoded, self.out, self.sems.at[0]))

    def start(self):
        w, net = self.window, self.net
        self.c = Batch(net, self.back)
        self.c.send(w.at[pl.ds(0, HALO)], self.back.at[0], net.ring("x", 3))
        self.c.send(w.at[pl.ds(HALO + OWN, HALO)], self.back.at[1], net.ring("x", 1))

    def total(self):
        self.c.wait_recv()
        rest = OWN - HALO
        own = pl.ds(HALO, OWN)
        y = self.window[own, :].astype(F32)
        low = y[:rest] + self.back[1, :rest].astype(F32)
        mid = y[rest:HALO] + self.back[1, rest:].astype(F32) + self.back[0, : HALO - rest].astype(F32)
        high = y[HALO:] + self.back[0, HALO - rest :].astype(F32)
        self.window[own, :] = jnp.concatenate([low, mid, high], axis=0).astype(BF)
        self.swaps.append(self.pair(self.window.at[own], self.token_grad, self.sems.at[1]))

    def done(self):
        for local, moved in self.swaps:
            local.wait()
            moved.wait_recv()


class Stream:
    SLOTS = 4

    def __init__(self, full, ring, sems):
        wq, wk, wv, wo, wi, wu = full
        self.ring = ring
        self.moves = []
        for n in range(12):
            slot = ring.at[n % self.SLOTS]
            if n < 4:
                pairs = [(wu.at[n], slot)]
            elif n < 8:
                pairs = [
                    (wi.at[n - 4, :, :, :, :, pl.ds(1024 * j, 1024)], slot.at[:, :, :, pl.ds(16 * j, 16)])
                    for j in range(4)
                ]
            else:
                w = (wo, wk, wv, wq)[n - 8]
                pairs = [(w.at[x], slot.at[:, :, :, pl.ds(16 * x, 16)]) for x in range(4)]
            self.moves.append([pltpu.make_async_copy(s, d, sems.at[4 * (n % self.SLOTS) + j]) for j, (s, d) in enumerate(pairs)])

    def start(self, n):
        for move in self.moves[n]:
            move.start()

    def wait(self, n):
        for move in self.moves[n]:
            move.wait()

    def part(self, n, j):
        return self.ring[n % self.SLOTS, :, :, :, 16 * j : 16 * j + 16].reshape(256, 1024)


class Backward:
    def __init__(self, ins, outs, scratch):
        self.weights = ins[:6]
        (self.x_in, self.q_in, self.k_in, self.v_in, self.probs_in, self.context_in, self.low_in, self.act_in) = ins[6:14]
        (self.slope_in, self.n1_in, self.inv1_in, self.d_in, self.encoded, self.vec, self.two) = ins[14:]
        self.owned, (self.out, self.token_grad, self.small) = outs[:6], outs[6:]
        take = iter(scratch)
        nxt = lambda n: [next(take) for _ in range(n)]
        (self.ring,) = nxt(1)
        self.g = nxt(6)
        self.bufs = nxt(3 * len(RECTS))
        self.x, self.q, self.k, self.v, self.context, self.act, self.inner, self.n1, self.inv1, self.d = nxt(10)
        self.outer, self.outer_sib, self.inner_sib, self.branch, self.branch_sib, self.d_context = nxt(6)
        self.dq, self.dk, self.dv, self.dq_sib, self.dk_sib, self.dv_sib, self.dx, self.back = nxt(8)
        self.kept, self.low_t = nxt(2)
        self.total, *vector_bufs = nxt(8)
        self.finals, self.ends = nxt(6), nxt(6)
        send_sem, recv_sem, self.local_sem = nxt(3)
        self.net = Net(send_sem, recv_sem)
        self.c = self.net.me["c"]
        self.loads = 0
        self.swaps = []
        self.stream = Stream(self.weights, self.ring, self.local_sem.at[pl.ds(0, 16)])
        self.vectors = VectorSum(self.net, self.total, vector_bufs)
        self.back_rows = Return(
            self.net, self.dx, self.kept, self.back, self.out, self.token_grad, self.local_sem.at[pl.ds(16, 2)]
        )
        lanes = []
        for n, (w, (r0, rows), (base, width), order) in enumerate(RECTS):
            lanes.append(
                Reduce(
                    self.net,
                    self.g[w],
                    pl.ds(r0, rows),
                    pl.ds(base, width),
                    BIG_FIRST[order],
                    self.bufs[3 * n : 3 * n + 3],
                )
            )
        self.lanes = dict(zip(LANES, ([lane] for lane in lanes)))

    def load(self, src, dst):
        move = pltpu.make_async_copy(src, dst, self.local_sem.at[18 + self.loads])
        self.loads += 1
        move.start()
        return move

    def half(self, which, width):
        return columns(which * width, width)

    def share(self, src, dst, width):
        return self.net.copy(src.at[:, self.half(1 - self.c, width)], dst, self.net.ring("c", 0))

    def begin(self):
        self.greeted = self.net.greet()
        at_d = self.load(self.d_in, self.d)
        self.at_act = self.load(self.act_in, self.act)
        self.total[...] = jnp.zeros((16, D), F32)
        self.total[G2 : G2 + 2, :] = self.two[0:2, :]
        at_d.wait()

        def body(t, carry):
            r = some_rows(t)
            low = self.d[r, :].astype(BF)
            self.outer[r, :] = low
            return carry + jnp.sum(low.astype(F32).reshape(ROWS // 8, 8, D), axis=0)

        s = lax.fori_loop(0, OWN // ROWS, body, jnp.zeros((8, D), F32), unroll=2)
        self.total[BU : BU + 1, :] = jnp.sum(s, axis=0, keepdims=True)

    def load_all(self):
        self.at_slope = self.load(self.slope_in, self.inner)
        for n in range(4):
            self.stream.start(n)
        self.at_low = [self.load(self.low_in.at[n], self.dx.at[pl.ds(OWN * n, OWN)]) for n in range(2)]
        self.at_n1 = [self.load(self.n1_in, self.n1), self.load(self.inv1_in, self.inv1)]
        self.at_kept = self.load(self.encoded, self.kept)
        self.at_rest = [
            self.load(self.context_in, self.context),
            self.load(self.x_in, self.x),
            self.load(self.q_in, self.q),
            self.load(self.k_in, self.k),
            self.load(self.v_in, self.v),
        ]

    def meet(self):
        self.greeted()
        self.got_outer = self.share(self.outer, self.outer_sib, 512)

    def d_inner(self):
        self.at_slope.wait()
        for n in range(4):
            self.stream.wait(n)

            cols = slice(1024 * n, 1024 * n + 1024)
            y = mm(self.outer[...], self.ring[n].reshape(1024, 1024), NT)
            y = (y * self.inner[:, cols].astype(F32)).astype(BF)
            self.inner[:, cols] = y
            s = column_sum(y)
            for dp in (2 * n, 2 * n + 1):
                for t in range(4):
                    at = 512 * (dp - 2 * n) + 128 * t
                    self.total[8 + t : 9 + t, 128 * dp : 128 * dp + 128] = s[:, at : at + 128]
            self.stream.start(n + 4)

    def share_inner(self):
        self.got_inner = self.share(self.inner, self.inner_sib, 2048)

    def grad_outer(self):
        self.at_act.wait()
        self.got_outer.wait_recv()
        c = self.c
        mine = self.outer.at[:, self.half(c, 512)]

        def body(t, carry):
            cols = columns(t * 1024, 1024)
            y = mm(self.act[c, :, cols], mine[...], TN) + mm(self.act[1 - c, :, cols], self.outer_sib[...], TN)
            self.g[5][t] = y.astype(BF).reshape(2, 2, 4, 64, 512)
            return carry

        lax.fori_loop(0, 4, body, 0, unroll=2)
        self.at_probs = self.load(self.probs_in, self.act)

    def d_normed(self):
        for n in range(4):
            self.stream.wait(4 + n)
            cols = slice(256 * n, 256 * n + 256)
            y = self.d[:, cols]
            for j in range(4):
                y = y + mm(self.inner[:, 1024 * j : 1024 * j + 1024], self.stream.part(4 + n, j), NT)
            self.d[:, cols] = y
            self.stream.start(8 + n)

    def turn_low(self):
        for move in self.at_low:
            move.wait()
        for j, which in enumerate((self.c, 1 - self.c)):
            rows = pl.ds(pl.multiple_of(OWN * which, OWN), OWN)
            for x in range(4):
                part = self.dx[rows, 256 * x : 256 * x + 256]
                self.low_t[256 * x : 256 * x + 256, OWN * j : OWN * j + OWN] = part.T

    def grad_inner(self):
        self.got_inner.wait_recv()
        c = self.c

        def body(t, carry):
            x, j = lax.div(t, 2), lax.rem(t, 2)
            rows, cols = pl.ds(pl.multiple_of(x * 256, 256), 256), columns(j * 1024, 1024)
            y = mm(self.low_t[rows, :OWN], self.inner[:, columns(c * 2048 + j * 1024, 1024)])
            y = y + mm(self.low_t[rows, OWN:], self.inner_sib[:, cols])
            self.g[4][x, :, :, :, :, cols] = y.astype(BF).reshape(2, 2, 4, 16, 1024)
            return carry

        lax.fori_loop(0, 8, body, 0, unroll=2)

    def norm_one(self):
        for move in self.at_n1:
            move.wait()

        def body(t, carry):
            r = some_rows(t)
            d, n = self.d[r, :], self.n1[r, :]
            da = norm_back(d * self.vec[G1 : G1 + 1, :], n, self.inv1[r, :1])
            low = da.astype(BF)
            self.d[r, :] = da
            self.branch[r, :] = low
            new = (d * n, d, low.astype(F32))
            return tuple(a + jnp.sum(b.reshape(ROWS // 8, 8, D), axis=0) for a, b in zip(carry, new))

        zero = jnp.zeros((8, D), F32)
        sums = lax.fori_loop(0, OWN // ROWS, body, (zero, zero, zero))
        for row, s in zip((G1, S1, BO), sums):
            self.total[row : row + 1, :] = jnp.sum(s, axis=0, keepdims=True)
        self.got_branch = self.share(self.branch, self.branch_sib, 512)

    def d_mixed(self):
        self.stream.wait(8)
        for x in range(4):
            self.d_context[:, 256 * x : 256 * x + 256] = mm(self.branch[...], self.stream.part(8, x), NT).astype(BF)

    def grad_rows(self, left, right, sib, out):
        mine = right.at[:, self.half(self.c, 512)]

        def body(x, carry):
            rows = columns(x * 256, 256)
            y = mm(left[0][:, rows], mine[...], TN) + mm(left[1][:, rows], sib[...], TN)
            out[x] = y.astype(BF).reshape(2, 2, 4, 16, 512)
            return carry

        lax.fori_loop(0, 4, body, 0, unroll=2)

    def pair(self, ref):
        return ref.at[self.c], ref.at[1 - self.c]

    def grad_output(self):
        self.got_branch.wait_recv()
        for move in self.at_rest:
            move.wait()
        self.grad_rows(self.pair(self.context), self.branch, self.branch_sib, self.g[3])

    def attend(self, first, last):
        if first == 0:
            self.at_probs.wait()
        attention_back(
            self.q,
            self.k,
            self.v,
            self.act,
            self.context.at[self.c],
            self.d_context,
            self.dq,
            self.dk,
            self.dv,
            first,
            last,
            HEADS // 4 * (1 - self.c),
        )

    def share_heads(self):
        self.got_heads = [
            self.share(self.dk, self.dk_sib, 512),
            self.share(self.dv, self.dv_sib, 512),
            self.share(self.dq, self.dq_sib, 512),
        ]

    def head_sums(self):
        self.total[BQ : BQ + 1, :] = column_sum(self.dq[...])
        self.total[BV : BV + 1, :] = column_sum(self.dv[...])
        self.vectors.start()

    def grad_key(self):
        self.got_heads[0].wait_recv()
        self.grad_rows(self.pair(self.x), self.dk, self.dk_sib, self.g[1])

    def grad_value(self):
        self.got_heads[1].wait_recv()
        self.grad_rows(self.pair(self.x), self.dv, self.dv_sib, self.g[2])

    def grad_query(self):
        self.got_heads[2].wait_recv()
        own = pl.ds(HALO, OWN)
        rows = (self.x.at[self.c, own], self.x.at[1 - self.c, own])
        self.grad_rows(rows, self.dq, self.dq_sib, self.g[0])

    def d_halo(self):
        for n in (9, 10):
            self.stream.wait(n)

        def sides(ref):
            return jnp.concatenate([ref[:HALO, :], ref[HALO + OWN :, :]], axis=0)

        for x in range(4):
            cols = slice(256 * x, 256 * x + 256)
            y = mm(sides(self.dk), self.stream.part(9, x), NT) + mm(sides(self.dv), self.stream.part(10, x), NT)
            self.dx[:HALO, cols] = y[:HALO].astype(BF)
            self.dx[HALO + OWN :, cols] = y[HALO:].astype(BF)
        self.back_rows.start()

    def d_own(self):
        self.stream.wait(11)
        own = slice(HALO, HALO + OWN)
        for x in range(4):
            cols = slice(256 * x, 256 * x + 256)
            y = mm(self.dk[own, :], self.stream.part(9, x), NT) + mm(self.dv[own, :], self.stream.part(10, x), NT)
            y = y + self.d[:, cols] + mm(self.dq[...], self.stream.part(11, x), NT)
            self.dx[own, cols] = y.astype(BF)

    def encoded_out(self):
        self.at_kept.wait()
        self.back_rows.start_encoded()

    def rows_back(self):
        self.back_rows.total()

    def final(self, *weights):
        c, net = self.c, self.net
        lanes = [lane for name in LANES for lane in self.lanes[name]]
        for w in weights:
            final, end = self.finals[w], self.ends[w]
            for lane, (of, (r0, rows), (base, width), _) in zip(lanes, RECTS):
                if of == w:
                    final[pl.ds(r0, rows), pl.ds(base, width)] = lane.result()
            n, width = final.shape[0] // 2, final.shape[1]
            kept = final.at[pl.ds(pl.multiple_of(n * c, 8), n)]
            given = final.at[pl.ds(pl.multiple_of(n * (1 - c), 8), n)]
            self.swaps.append((w, net.copy(given, end.at[:, columns(c * width, width)], net.ring("c", 0))))
            end[:, columns(c * width, width)] = kept[...]

    def finish(self):
        self.vectors.done(self.small)
        stores = []
        for w, swap in self.swaps:
            swap.wait_recv()
            stores.append(self.load(self.ends[w], self.owned[w]))
        for store in stores:
            store.wait()
        self.back_rows.done()
        self.net.finish()


BACK = (
    "begin", "meet", "load_all", "grad_outer", "u0.p1", "u1.p1", "u2.p1", "d_inner", "share_inner",
    "encoded_out", "d_normed", "u0.p1_mid", "u1.p1_mid", "u2.p1_mid", "norm_one", "turn_low", "d_mixed",
    "grad_inner", "i0.p1", "i1.p1", "i2.p1", "grad_output", "o.p1", "attend.0.2", "attend.2.4", "i0.p1_mid",
    "i1.p1_mid", "i2.p1_mid", "share_heads", "attend.4.6", "o.p1_mid", "u0.p2_ring", "u1.p2_ring",
    "u2.p2_ring", "attend.6.8", "head_sums", "d_halo", "u0.p2_mid", "u1.p2_mid", "u2.p2_mid", "grad_key",
    "k.p1", "grad_value", "v.p1", "grad_query", "q.p1", "d_own", "vectors.along_x", "i0.p2", "i1.p2", "i2.p2",
    "k.p1_mid", "v.p1_mid", "q.p1_mid", "u0.p3", "u1.p3", "u2.p3", "vectors.along_y", "o.p2", "rows_back",
    "i0.p3", "i1.p3", "i2.p3", "vectors.along_z", "k.p2", "v.p2", "q.p2", "final.5", "o.p3", "final.4",
    "k.p3", "v.p3", "q.p3", "final.3.1.2.0", "finish",
)


def backward_kernel(*refs):
    run_steps(Backward(refs[:21], refs[21:30], refs[30:]), BACK)


def backward_all(kept):
    any_space = pl.BlockSpec(memory_space=pl.ANY)
    vmem = pl.BlockSpec(memory_space=pltpu.VMEM)
    owned = [(r // 2, n) for r, n in BLOCKS]
    scratch = [((4, 2, 2, 4, 64, 1024), BF)]
    scratch += [(CHIPS + (r, n // 2), BF) for r, n in BLOCKS]
    scratch += [(s, BF) for s in reduce_buffers()]
    scratch += [((2, WIN, D), BF), ((OWN, D), BF), ((WIN, D), BF), ((WIN, D), BF), ((2, OWN, D), BF)]
    scratch += [((2, OWN, FF), BF), ((OWN, FF), BF), ((OWN, D), F32), ((OWN, 128), F32), ((OWN, D), F32)]
    scratch += [((OWN, D), BF), ((OWN, 512), BF), ((OWN, 2048), BF), ((OWN, D), BF), ((OWN, 512), BF), ((OWN, D), BF)]
    scratch += [((OWN, D), BF), ((WIN, D), BF), ((WIN, D), BF), ((OWN, 512), BF), ((WIN, 512), BF), ((WIN, 512), BF)]
    scratch += [((WIN, D), BF), ((2, HALO, D), BF), ((OWN, D), BF), ((D, 2 * OWN), BF)]
    scratch += [((16, D), F32), ((16, D), F32), ((16, D), F32), ((3, 16, 256), F32), ((2, 16, 128), F32), ((3, 16, 128), F32)]
    scratch += [((16, 128), F32), ((3, 16, 128), F32)]
    scratch += [((r, n // 2), F32) for r, n in BLOCKS] + [(s, F32) for s in owned]
    return pl.pallas_call(
        backward_kernel,
        name="backward_all",
        out_shape=[jax.ShapeDtypeStruct(s, F32) for s in owned]
        + [jax.ShapeDtypeStruct((2, TOK, D), BF)] * 2
        + [jax.ShapeDtypeStruct((8, 128), F32)],
        in_specs=[any_space] * 19 + [vmem] * 2,
        out_specs=[any_space] * 8 + [vmem],
        scratch_shapes=[pltpu.VMEM(s, t) for s, t in scratch]
        + [
            pltpu.SemaphoreType.DMA((72,)),
            pltpu.SemaphoreType.DMA((72,)),
            pltpu.SemaphoreType.DMA((40,)),
        ],
        compiler_params=pltpu.CompilerParams(collective_id=2, has_side_effects=True, vmem_limit_bytes=63 << 20),
    )(*kept)


def keep_kernel(*refs):
    (sums, *ins), outs = refs[:9], refs[9:]
    for src, dst in zip(ins, outs):
        dst[...] = src[...]
    for j, dst in enumerate(outs[8:]):
        dst[...] = sums[0:1, 8 * j : 8 * j + dst.shape[1]]


def keep(sums, *arrays):
    shapes = [(a.shape, a.dtype) for a in arrays] + [((1, 8), F32)] * 8 + [((1, 32), F32)]
    return pl.pallas_call(
        keep_kernel,
        name="keep",
        out_shape=[jax.ShapeDtypeStruct(s, t) for s, t in shapes],
        in_specs=[pl.BlockSpec(memory_space=pltpu.VMEM)] * 9,
        out_specs=[pl.BlockSpec(memory_space=pltpu.VMEM)] * 17,
    )(sums, *arrays)


def local(
    tokens, cotangent, seq_lengths, block_offsets, deal_order, wq, wk, wv, wo, bq, bv, bo, g1, s1, wi, bi, wu, bu, g2, s2
):
    small = [v[None] for v in (bq, bv, bo, g1, s1, bu, g2, s2, bi)]
    kept = forward_all(
        tokens[:, 0], cotangent[:, 0], seq_lengths[:, 0], deal_order[:, 0], (wq, wk, wv, wo, wi, wu), small
    )
    *owned, out, token_grad, sums = backward_all(kept)
    results = keep(sums, *owned, out, token_grad)
    owned, (out, token_grad), vectors = results[:6], results[6:8], results[8:]
    sbq, sbv, sbo, sg1, ss1, sbu, sg2, ss2, sbi = [v[0] for v in vectors]
    return (
        out[:, None],
        token_grad[:, None],
        *owned[:4],
        sbq,
        sbv,
        sbo,
        sg1,
        ss1,
        owned[4],
        sbi,
        owned[5],
        sbu,
        sg2,
        ss2,
    )


def solution(mesh):
    rows = P(None, "shard", "dp", None)
    table = P(None, "shard", None)
    matrix, vector = P(("dp", "shard"), None), P(("dp", "shard"))
    in_specs = (rows, rows) + (table,) * 3 + (matrix,) * 4 + (vector,) * 5 + (matrix, vector, matrix) + (vector,) * 3
    out_specs = (rows, rows) + (matrix,) * 4 + (vector,) * 5 + (matrix, vector, matrix) + (vector,) * 3
    return jax.shard_map(local, mesh=mesh, in_specs=in_specs, out_specs=out_specs, check_vma=False)
```

```python
import math

import jax
import jax.numpy as jnp
from jax import lax
from jax.experimental import pallas as pl
from jax.experimental.pallas import tpu as pltpu
from jax.sharding import PartitionSpec as P

MESH = pl.DeviceIdType.MESH
BF = jnp.bfloat16
F32 = jnp.float32
D = 1024
FF = 4096
HEADS = 16
HEAD = 64
TOK = 128
OWN = 2 * TOK
HALO = 192
WIN = OWN + 2 * HALO
AXES = ("x", "y", "z")
ORDER = (("z", "y", "x"), ("x", "z", "y"), ("y", "x", "z"))
CHIPS = (4, 2, 2, 4)


def position():
    dp, sh = lax.axis_index("dp"), lax.axis_index("shard")
    return {
        "x": lax.div(dp, 2),
        "y": lax.div(sh, 8) * 2 + lax.rem(dp, 2),
        "z": lax.div(lax.rem(sh, 8), 2),
        "c": lax.rem(sh, 2),
    }


def device_at(at):
    return (
        at["x"] * 2 + lax.rem(at["y"], 2),
        lax.div(at["y"], 2) * 8 + at["z"] * 2 + at["c"],
    )


class Batch:
    def __init__(self, net, whole):
        self.net, self.whole = net, whole
        self.k = net.used
        net.used += 1
        net.batches.append(self)

    def send(self, src, dst, device):
        pltpu.make_async_remote_copy(
            src_ref=src,
            dst_ref=dst,
            send_sem=self.net.send_sem.at[self.k],
            recv_sem=self.net.recv_sem.at[self.k],
            device_id=device,
            device_id_type=MESH,
        ).start()

    def wait_recv(self):
        pltpu.make_async_copy(self.whole, self.whole, self.net.recv_sem.at[self.k]).wait()

    def wait_send(self):
        pltpu.make_async_copy(self.whole, self.whole, self.net.send_sem.at[self.k]).wait()


class Net:
    def __init__(self, send_sem, recv_sem):
        self.me = position()
        self.send_sem, self.recv_sem = send_sem, recv_sem
        self.used = 0
        self.batches = []

    def moved(self, axis, by):
        at = dict(self.me)
        if axis == "c":
            at["c"] = 1 - at["c"]
        else:
            at[axis] = lax.rem(at[axis] + by, 4)
        return at

    def ring(self, axis, by):
        return device_at(self.moved(axis, by))

    def pair(self, lo):
        at = dict(self.me)
        at["y"] = lax.div(at["y"], 2) * 2 + lo
        return device_at(at)

    def copy(self, src, dst, device):
        batch = Batch(self, dst)
        batch.send(src, dst, device)
        return batch

    def greet(self):
        bar = pltpu.get_barrier_semaphore()
        peers = [self.ring("c", 0)] + [self.ring(a, b) for a in AXES for b in (1, 2, 3)]
        for p in peers:
            pl.semaphore_signal(bar, inc=1, device_id=p, device_id_type=MESH)
        return lambda: pl.semaphore_wait(bar, len(peers))

    def finish(self):
        for batch in self.batches:
            batch.wait_send()
        assert self.used <= self.send_sem.shape[0], self.used


def chip_index(at, drop=()):
    out = []
    for axis in AXES:
        if axis in drop:
            continue
        v = at[axis]
        if axis == "y":
            if v is None:
                out += [slice(None), slice(None)]
            elif isinstance(v, tuple):
                out += [v[1], slice(None)]
            else:
                out += [lax.rem(v, 2), lax.div(v, 2)]
        elif v is None:
            out.append(slice(None))
        elif isinstance(v, tuple):
            out.append(pl.ds(2 * v[1], 2))
        else:
            out.append(v)
    return tuple(out)


def chip_shape(drop):
    shape = ()
    for axis in AXES:
        if axis not in drop:
            shape += (2, 2) if axis == "y" else (4,)
    return shape


def columns(base, width):
    return pl.ds(pl.multiple_of(base, 128), width)


class Gather:
    def __init__(self, net, ref, rows, cols, order):
        self.net, self.ref, self.rows, self.cols = net, ref, rows, cols
        self.a, self.b, self.e = order

    def at(self, **over):
        place = {k: self.net.me[k] for k in AXES}
        place.update(over)
        return self.ref.at[chip_index(place) + (self.rows, self.cols)]

    def send(self, batch, region, axis, by):
        batch.send(region, region, self.net.ring(axis, by))

    def blocks(self, *chips):
        return Batch(self.net, self.ref.at[chips + (self.rows, self.cols)])

    def p1(self):
        self.c = self.blocks(pl.ds(0, 3), 0, 0, 0)
        for d in (1, 3, 2):
            self.send(self.c, self.at(), self.a, d)

    def p2(self):
        self.c.wait_recv()
        self.c = self.blocks(pl.ds(0, 3), 0, 0, slice(None))
        for d in (1, 3, 2):
            self.send(self.c, self.at(**{self.a: None}), self.b, d)

    def p2_ring(self):
        self.c.wait_recv()
        self.c = self.blocks(pl.ds(0, 2), 0, 0, slice(None))
        for d in (1, 3):
            self.send(self.c, self.at(**{self.a: None}), self.b, d)

    def p2_mid(self):
        self.c.wait_recv()
        self.c = self.blocks(0, 0, 0, slice(None))
        for h, to in enumerate((1, 3)):
            b = self.net.moved(self.b, 4 - to)[self.b]
            self.send(self.c, self.at(**{self.a: ("half", h), self.b: b}), self.b, to)

    def part(self, h, by):
        e = self.net.moved(self.e, by)[self.e]
        return self.at(**{self.a: h if h is None else ("half", h), self.b: None, self.e: e})

    def quarter(self):
        return Batch(self.net, self.part(None, 0))

    def p3(self):
        self.c.wait_recv()
        self.near, self.far = self.quarter(), self.quarter()
        self.send(self.near, self.part(0, 0), self.e, 1)
        self.send(self.near, self.part(1, 0), self.e, 3)
        self.send(self.far, self.part(1, 0), self.e, 1)
        self.send(self.far, self.part(0, 0), self.e, 3)
        self.core = self.blocks(*(slice(None),) * 4)
        self.send(self.core, self.part(None, 0), "c", 0)

    def p3_mid(self):
        self.near.wait_recv()
        self.last = self.quarter()
        self.send(self.last, self.part(0, 3), self.e, 1)
        self.send(self.last, self.part(1, 1), self.e, 3)

    def p3_core(self):
        self.far.wait_recv()
        self.send(self.core, self.part(None, 3), "c", 0)
        self.send(self.core, self.part(None, 1), "c", 0)

    def p3_end(self):
        self.last.wait_recv()
        self.send(self.core, self.part(None, 2), "c", 0)

    def done(self):
        self.core.wait_recv()


def each(lanes, step):
    for lane in lanes:
        step(lane)


def rows_at(base, count):
    return pl.ds(pl.multiple_of(base, TOK // 2), count)


class Window:
    def __init__(self, net, tokens, cotangent, window, cots, local_sem):
        self.net, self.window, self.cots = net, window, cots
        self.tokens, self.cotangent, self.local_sem = tokens, cotangent, local_sem
        self.lo = lax.rem(net.me["y"], 2)

    def pair(self, src, dst, sem):
        local = pltpu.make_async_copy(src.at[self.lo], dst, sem)
        local.start()
        return local, self.net.copy(src.at[1 - self.lo], dst, self.net.pair(1 - self.lo))

    def start(self):
        mine = self.window.at[rows_at(HALO + TOK * self.lo, TOK)]
        self.rows = self.pair(self.tokens, mine, self.local_sem.at[0])

    def start_cots(self):
        mine = self.cots.at[rows_at(TOK * self.lo, TOK)]
        self.cot_rows = self.pair(self.cotangent, mine, self.local_sem.at[1])

    def halo(self):
        local, moved = self.rows
        local.wait()
        moved.wait_recv()
        w, net = self.window, self.net
        self.c = Batch(net, w.at[pl.ds(0, 2 * HALO)])
        self.c.send(w.at[pl.ds(OWN, HALO)], w.at[pl.ds(0, HALO)], net.ring("x", 1))
        self.c.send(w.at[pl.ds(HALO, HALO)], w.at[pl.ds(HALO + OWN, HALO)], net.ring("x", 3))

    def done(self):
        self.c.wait_recv()

    def cots_done(self):
        local, moved = self.cot_rows
        local.wait()
        moved.wait_recv()


def place_own(me, mine, peer, full):
    here = chip_index(me)
    c = me["c"]
    first = c == 0

    def both(a, b):
        return jnp.concatenate([jnp.where(first, a, b), jnp.where(first, b, a)], axis=0)

    half = columns(c * 512, 512)
    for j in range(4):
        r = slice(8 * j, 8 * j + 8)
        full[j][here + (slice(None), half)] = both(mine[r, half], peer[r, half])
    for t in range(2):
        r, s = slice(32 + 8 * t, 40 + 8 * t), slice(48 + 8 * t, 56 + 8 * t)
        a = jnp.where(first, mine[r, :], mine[s, :])
        b = jnp.where(first, peer[r, :], peer[s, :])
        full[4][here + (slice(None), columns(c * 2048 + 1024 * t, 1024))] = both(a, b)
    full[5][here + (slice(None), half)] = both(mine[64:96, half], peer[64:96, half])


BLOCKS = ((16, 1024),) * 4 + ((16, 4096), (64, 1024))


SPAN = TOK + 2 * HALO
NT = (((1,), (1,)), ((), ()))
TN = (((0,), (0,)), ((), ()))
NN = (((1,), (0,)), ((), ()))


def mm(a, b, dims=NN):
    return lax.dot_general(a, b, dims, preferred_element_type=F32)


def tile(w, n0, n):
    return w[:, :, :, :, :, columns(n0, n)].reshape(-1, n)


def project(rows, w, out, bias=None, n=1024):
    def body(t, carry):
        cols = columns(t * n, n)
        y = mm(rows[...], tile(w, t * n, n))
        if bias is not None:
            y = y + bias[:, cols]
        out[:, cols] = y.astype(BF)
        return carry

    lax.fori_loop(0, out.shape[1] // n, body, 0)


def lane_split(x):
    low = lax.broadcasted_iota(jnp.int32, x.shape, 1) < HEAD
    zero = jnp.zeros_like(x)
    return jnp.concatenate([jnp.where(low, x, zero), jnp.where(low, zero, x)], axis=0)


def lane_join(x):
    n = x.shape[0] // 2
    low = lax.broadcasted_iota(jnp.int32, (n, x.shape[1]), 1) < HEAD
    return jnp.where(low, x[:n], x[n:])


def attention(q, k, v, bias, probs, context, first, last):
    def body(h, carry):
        cols = columns(h * 128, 128)
        for b in range(2):
            mine, near = pl.ds(b * TOK, TOK), pl.ds(b * TOK, SPAN)
            some, two = k[near, cols], lane_split(q[mine, cols]) * jnp.asarray(0.125, BF)
            p = []
            for s in range(2):
                e = mm(some, two[s * TOK : s * TOK + TOK], NT) + bias[b]
                e = jnp.exp(e - jnp.max(e, axis=0, keepdims=True))
                p.append((e * (1.0 / jnp.sum(e, axis=0, keepdims=True))).astype(BF))
            p = jnp.concatenate(p, axis=1)
            at = columns((2 * h + b) * OWN, OWN)
            probs[0, :, at], probs[1, :, at] = p[:OWN], p[OWN:]
            y = mm(v[near, cols], p, TN)
            y = jnp.concatenate([y[:HEAD, :TOK], y[HEAD:, TOK:]], axis=0)
            context[mine, cols] = y.T.astype(BF)
        return carry

    lax.fori_loop(first, last, body, 0, unroll=2)


def normalized(a):
    centred = a - jnp.mean(a, axis=-1, keepdims=True)
    inv = lax.rsqrt(jnp.mean(centred * centred, axis=-1, keepdims=True) + 1e-05)
    return centred * inv, inv


def norm_back(dn, n, inv):
    return inv * (dn - jnp.mean(dn, axis=-1, keepdims=True) - n * jnp.mean(dn * n, axis=-1, keepdims=True))


def feed_in(low, wi, bi, act, slope, first, last, n=512):
    def body(t, carry):
        cols = columns(t * n, n)
        u = mm(low[...], tile(wi, t * n, n)) + bi[:, cols]
        phi = 0.5 + 0.5 * lax.erf(u * math.sqrt(0.5))
        act[:, cols] = (u * phi).astype(BF)
        slope[:, cols] = (phi + u * (jnp.exp(-0.5 * (u * u)) * (1.0 / math.sqrt(2 * math.pi)))).astype(BF)
        return carry

    lax.fori_loop(first, last, body, 0, unroll=2)


ROWS = 32


def some_rows(t):
    return pl.ds(pl.multiple_of(t * ROWS, ROWS), ROWS)


def segment_bias(lengths, order, start, lo, bias):
    ends, total = [], 0
    for k in range(16):
        total = total + lengths[lo, order[lo, k]]
        ends.append(total)

    def which(at):
        found = jnp.where(at < 0, -1, 0)
        for e in ends:
            found = found + (at >= e).astype(jnp.int32)
        return found

    keys = which(start + lax.broadcasted_iota(jnp.int32, (WIN, TOK), 0))
    queries = which(start + HALO + lax.broadcasted_iota(jnp.int32, (8, OWN), 1))[:1]
    for b in range(2):
        same = keys[b * TOK : b * TOK + SPAN] == queries[:, b * TOK : b * TOK + TOK]
        bias[b] = jnp.where(same, 0.0, -1e30)


class Vectors:
    def __init__(self, net, small, rows, tiles, vec, inner):
        self.net, self.small, self.rows = net, small, rows
        self.own, self.sib, self.tz, self.ty, self.tx = tiles
        self.vec, self.inner = vec, inner

    def around(self, axis, tiles, mine):
        self.c = Batch(self.net, tiles.at[pl.ds(0, 3)])
        for d in (1, 3, 2):
            self.c.send(tiles.at[mine], tiles.at[mine], self.net.ring(axis, d))

    def place(self):
        sh = lax.axis_index("shard")
        self.rows[...] = jnp.zeros((16, 128), F32)
        for j in range(9):
            n = self.small[j].shape[1]
            self.rows[j : j + 1, :n] = self.small[j][...].astype(F32)
        i = lax.broadcasted_iota(jnp.int32, (128, 128), 0)
        to = lax.broadcasted_iota(jnp.int32, (128, 128), 1)
        value = self.rows[...].astype(BF)
        eight = mm(value, jnp.where((to == 8 * sh + i) & (i < 8), 1.0, 0.0).astype(BF))
        many = mm(value, jnp.where((to == 32 * lax.rem(sh, 4) + i) & (i < 32), 1.0, 0.0).astype(BF))
        r = lax.broadcasted_iota(jnp.int32, (16, 128), 0)
        many = jnp.broadcast_to(many[8:9], (16, 128))
        tile = jnp.where(r < 8, eight, jnp.where(r == 8 + lax.div(sh, 4), many, 0.0))
        self.own[...] = tile.astype(BF)

    def start(self):
        self.c = self.net.copy(self.own, self.sib, self.net.ring("c", 0))

    def wait(self):
        self.c.wait_recv()

    def along_z(self):
        self.wait()
        z = self.net.me["z"]
        self.tz[z] = self.own[...] + self.sib[...]
        self.around("z", self.tz, z)

    def along_y(self):
        self.wait()
        y = self.net.me["y"]
        self.ty[y] = (self.tz[0] + self.tz[1]) + (self.tz[2] + self.tz[3])
        self.around("y", self.ty, y)

    def along_x(self):
        self.wait()
        x = self.net.me["x"]
        self.tx[x, 0] = self.ty[0] + self.ty[2]
        self.tx[x, 1] = self.ty[1] + self.ty[3]
        self.around("x", self.tx, x)

    def done(self):
        self.wait()
        for dp in range(8):
            got = self.tx[dp // 2, dp % 2].astype(F32)
            self.vec[:, 128 * dp : 128 * dp + 128] = got[:8]
            for t in range(4):
                at = 512 * dp + 128 * t
                self.inner[:, at : at + 128] = got[8 + t : 9 + t]


BQ, BV, BO, G1, S1, BU, G2, S2 = range(8)


class Forward:
    def __init__(self, ins, outs, scratch):
        self.tokens, self.cotangent, self.lengths, self.order = ins[:4]
        self.own, self.small = ins[4:10], ins[10:]
        self.weights_out = outs[:6]
        (self.x_out, self.q_out, self.k_out, self.v_out, self.probs_out, self.context_out, self.low_out) = outs[6:13]
        (self.act_out, self.slope_out, self.n1_out, self.inv1_out, self.d_out, self.encoded_out) = outs[13:19]
        self.vec_out, self.two_out = outs[19:]
        self.mine, self.peer = scratch[:2]
        self.full, scratch = scratch[2:8], scratch[8:]
        (self.window, self.cots, self.q, self.k, self.v, self.probs, self.context, self.low) = scratch[:8]
        (self.act, self.slope, self.bias, self.n1, self.inv1, self.normed, self.total, self.encoded) = scratch[8:16]
        self.vec, self.inner, self.two, self.placed = scratch[16:20]
        tiles, (send_sem, recv_sem, self.local_sem) = scratch[20:25], scratch[25:]
        self.net = Net(send_sem, recv_sem)
        self.me, self.c = self.net.me, self.net.me["c"]
        self.lo = lax.rem(self.me["y"], 2)
        self.stores, self.gets = [], []
        self.vectors = Vectors(self.net, self.small, self.placed, tiles, self.vec, self.inner)
        self.view = Window(self.net, self.tokens, self.cotangent, self.window, self.cots, self.local_sem)
        rows, half = slice(None), columns(self.c * 512, 512)
        wi, wu = self.full[4], self.full[5]

        def inner(base, width, order):
            return Gather(self.net, wi, rows, columns(self.c * 2048 + base, width), ORDER[order])

        self.lanes = (
            [Gather(self.net, self.full[j], rows, half, ORDER[j]) for j in range(3)],
            [Gather(self.net, self.full[3], rows, half, ORDER[2]), inner(0, 1024, 1), inner(1024, 1024, 2)],
            [
                Gather(self.net, wu, pl.ds(0, 32), half, ORDER[0]),
                Gather(self.net, wu, pl.ds(32, 16), half, ORDER[1]),
                Gather(self.net, wu, pl.ds(48, 16), half, ORDER[2]),
            ],
        )

    def store(self, src, dst):
        move = pltpu.make_async_copy(src, dst, self.local_sem.at[2 + len(self.stores)])
        move.start()
        self.stores.append(move)

    def both(self, src, dst):
        self.gets.append(self.net.copy(src, dst.at[self.c], self.net.ring("c", 0)))
        self.store(src, dst.at[self.c])

    def begin(self):
        greeted = self.net.greet()
        for j in range(4):
            self.mine[8 * j : 8 * j + 8, :] = self.own[j][...]
            self.mine[32 + 8 * j : 40 + 8 * j, :] = self.own[4][:, 1024 * j : 1024 * j + 1024]
        self.mine[64:96, :] = self.own[5][...]
        self.vectors.place()
        segment_bias(self.lengths, self.order, self.me["x"] * OWN - HALO, self.lo, self.bias)
        greeted()
        swap = self.net.copy(self.mine, self.peer, self.net.ring("c", 0))
        self.view.start()
        self.vectors.start()
        swap.wait_recv()
        place_own(self.me, self.mine, self.peer, self.full)

    def halo(self):
        self.view.halo()

    def cots_in(self):
        self.view.start_cots()

    def rows_done(self):
        self.view.done()
        self.both(self.window, self.x_out)

    def query(self):
        project(self.window.at[pl.ds(HALO, OWN)], self.full[0], self.q, self.vec.at[BQ : BQ + 1])

    def key(self):
        project(self.window, self.full[1], self.k)

    def value(self):
        project(self.window, self.full[2], self.v, self.vec.at[BV : BV + 1])

    def keep_heads(self):
        for j in range(3):
            self.store(self.full[j], self.weights_out[j])
        for src, dst in ((self.q, self.q_out), (self.k, self.k_out), (self.v, self.v_out)):
            self.store(src, dst)

    def attend(self, first, last):
        attention(self.q, self.k, self.v, self.bias, self.probs, self.context, first, last)

    def keep_probs(self):
        self.both(self.context, self.context_out)
        self.store(self.probs, self.probs_out)

    def mix(self):
        self.store(self.full[3], self.weights_out[3])
        self.store(self.full[4], self.weights_out[4])

        def body(t, carry):
            cols = columns(t * 512, 512)
            y = mm(self.context[...], tile(self.full[3], t * 512, 512)) + self.vec[BO : BO + 1, cols]
            self.total[:, cols] = y + self.window[pl.ds(HALO, OWN), cols].astype(F32)
            return carry

        lax.fori_loop(0, 2, body, 0, unroll=2)

    def norm_one(self):
        def body(t, carry):
            r = some_rows(t)
            n, inv = normalized(self.total[r, :])
            self.n1[r, :] = n
            self.inv1[r, :] = jnp.broadcast_to(inv, (ROWS, 128))
            y = n * self.vec[G1 : G1 + 1, :] + self.vec[S1 : S1 + 1, :]
            self.normed[r, :] = y
            self.low[r, :] = y.astype(BF)
            return carry

        lax.fori_loop(0, OWN // ROWS, body, 0)
        self.both(self.low, self.low_out)
        self.store(self.n1, self.n1_out)
        self.store(self.inv1, self.inv1_out)

    def feed_in(self, first, last):
        feed_in(self.low, self.full[4], self.inner, self.act, self.slope, first, last)
        if last == FF // 512:
            self.both(self.act, self.act_out)
            self.store(self.slope, self.slope_out)
            self.store(self.vec, self.vec_out)

    def feed_out(self):
        self.store(self.full[5], self.weights_out[5])

        def body(t, carry):
            cols = columns(t * 512, 512)
            y = mm(self.act[...], tile(self.full[5], t * 512, 512)) + self.vec[BU : BU + 1, cols]
            self.total[:, cols] = y + self.normed[:, cols]
            return carry

        lax.fori_loop(0, 2, body, 0, unroll=2)

    def cots_done(self):
        self.view.cots_done()

    def norm_two(self):
        def body(t, carry):
            r = some_rows(t)
            n, inv = normalized(self.total[r, :])
            gain = self.vec[G2 : G2 + 1, :]
            self.encoded[r, :] = (n * gain + self.vec[S2 : S2 + 1, :]).astype(BF)
            d = self.cots[r, :].astype(F32)
            self.normed[r, :] = norm_back(d * gain, n, inv)
            dn = jnp.sum((d * n).reshape(ROWS // 8, 8, D), axis=0)
            return carry[0] + dn, carry[1] + jnp.sum(d.reshape(ROWS // 8, 8, D), axis=0)

        zero = jnp.zeros((8, D), F32)
        gain_sum, shift_sum = lax.fori_loop(0, OWN // ROWS, body, (zero, zero))
        self.two[0:1, :] = jnp.sum(gain_sum, axis=0, keepdims=True)
        self.two[1:2, :] = jnp.sum(shift_sum, axis=0, keepdims=True)
        self.two[2:8, :] = jnp.zeros((6, D), F32)
        self.store(self.normed, self.d_out)
        self.store(self.encoded, self.encoded_out)
        self.store(self.two, self.two_out)

    def finish(self):
        for got in self.gets:
            got.wait_recv()
        for move in self.stores:
            move.wait()
        self.net.finish()


def forward_kernel(*refs):
    work = Forward(refs[:19], refs[19:40], refs[40:])
    a, b, u = work.lanes
    work.begin()
    each(a, Gather.p1)
    each(b, Gather.p1)
    each(u, Gather.p1)
    work.vectors.along_z()
    each(a, Gather.p2)
    each(b, Gather.p2_ring)
    each(u, Gather.p2_ring)
    work.vectors.along_y()
    each(a, Gather.p3)
    each(b, Gather.p2_mid)
    each(u, Gather.p2_mid)
    work.halo()
    work.vectors.along_x()
    each(a, Gather.p3_mid)
    each(b, Gather.p3)
    work.cots_in()
    each(a, Gather.p3_core)
    each(a, Gather.p3_end)
    work.vectors.done()
    each(a, Gather.done)
    each(b, Gather.p3_mid)
    each(u, Gather.p3)
    work.query()
    work.rows_done()
    work.key()
    work.value()
    work.attend(0, 2)
    each(b, Gather.p3_core)
    work.attend(2, 4)
    each(b, Gather.p3_end)
    work.attend(4, 6)
    each(u, Gather.p3_mid)
    work.attend(6, 8)
    work.keep_heads()
    each(u, Gather.p3_core)
    work.keep_probs()
    each(b, Gather.done)
    work.mix()
    work.norm_one()
    work.feed_in(0, 2)
    work.feed_in(2, 4)
    each(u, Gather.p3_end)
    work.feed_in(4, 6)
    work.feed_in(6, 8)
    each(u, Gather.done)
    work.feed_out()
    work.cots_done()
    work.norm_two()
    work.finish()


def forward_all(tokens, cotangent, lengths, order, own, small):
    any_space = pl.BlockSpec(memory_space=pl.ANY)
    vmem = pl.BlockSpec(memory_space=pltpu.VMEM)
    smem = pl.BlockSpec(memory_space=pltpu.SMEM)
    full = [(CHIPS + s, BF) for s in BLOCKS]
    kept = [
        ((2, WIN, D), BF),
        ((OWN, D), BF),
        ((WIN, D), BF),
        ((WIN, D), BF),
        ((2, OWN, FF), BF),
        ((2, OWN, D), BF),
        ((2, OWN, D), BF),
        ((2, OWN, FF), BF),
        ((OWN, FF), BF),
        ((OWN, D), F32),
        ((OWN, 128), F32),
        ((OWN, D), F32),
        ((OWN, D), BF),
        ((8, D), F32),
        ((8, D), F32),
    ]
    scratch = [((96, 1024), BF)] * 2 + full
    scratch += [((WIN, D), BF), ((OWN, D), BF), ((OWN, D), BF), ((WIN, D), BF), ((WIN, D), BF)]
    scratch += [((2, OWN, FF), BF), ((OWN, D), BF), ((OWN, D), BF), ((OWN, FF), BF), ((OWN, FF), BF)]
    scratch += [((2, SPAN, TOK), F32), ((OWN, D), F32), ((OWN, 128), F32), ((OWN, D), F32), ((OWN, D), F32)]
    scratch += [((OWN, D), BF), ((8, D), F32), ((1, FF), F32), ((8, D), F32), ((16, 128), F32)]
    scratch += [((16, 128), BF)] * 2 + [((4, 16, 128), BF)] * 2 + [((4, 2, 16, 128), BF)]
    return pl.pallas_call(
        forward_kernel,
        name="forward_all",
        out_shape=[jax.ShapeDtypeStruct(s, t) for s, t in full + kept],
        in_specs=[any_space] * 2 + [smem] * 2 + [vmem] * 15,
        out_specs=[any_space] * 21,
        scratch_shapes=[pltpu.VMEM(s, t) for s, t in scratch]
        + [
            pltpu.SemaphoreType.DMA((80,)),
            pltpu.SemaphoreType.DMA((80,)),
            pltpu.SemaphoreType.DMA((24,)),
        ],
        compiler_params=pltpu.CompilerParams(collective_id=1, has_side_effects=True, vmem_limit_bytes=62 << 20),
    )(tokens, cotangent, lengths, order, *own, *small)


def add_into(dst, srcs):
    lead = dst.shape[:-2]
    loop = lead[:-1] if len(lead) > 1 else lead
    total = math.prod(loop)

    def body(k, carry):
        index, rest = (), k
        for n in reversed(loop):
            index = (lax.rem(rest, n),) + index
            rest = lax.div(rest, n)
        value = dst[index].astype(F32)
        for s in srcs:
            value = value + s[index].astype(F32)
        dst[index] = value.astype(BF)
        return carry

    lax.fori_loop(0, total, body, 0)


class Reduce:
    def __init__(self, net, ref, rows, cols, order, bufs):
        self.net, self.ref, self.rows, self.cols = net, ref, rows, cols
        self.a, self.b, self.e = order
        self.wide, self.mid, self.low = bufs
        self.ringed = False

    def at(self, **over):
        place = {k: self.net.me[k] for k in AXES}
        place.update(over)
        return self.ref.at[chip_index(place) + (self.rows, self.cols)]

    def quarter(self, by, h):
        b = None if h is None else ("half", h)
        return self.at(**{self.a: self.net.moved(self.a, by)[self.a], self.b: b, self.e: None})

    def buf(self, k, h):
        b = None if h is None else ("half", h)
        return self.wide.at[(k,) + chip_index({self.b: b, self.e: None}, drop=(self.a,))]

    def send(self, batch, by, h, k, to):
        batch.send(self.quarter(by, h), self.buf(k, h), self.net.ring(self.a, to))

    def p1(self):
        self.near = Batch(self.net, self.buf(0, None))
        self.send(self.near, 2, 0, 0, 1)
        self.send(self.near, 2, 1, 0, 3)
        self.far = Batch(self.net, self.wide.at[pl.ds(1, 2)])
        self.send(self.far, 1, 1, 1, 1)
        self.send(self.far, 3, 0, 2, 3)

    def p1_mid(self):
        self.near.wait_recv()
        add_into(self.quarter(1, 0), [self.buf(0, 0)])
        self.send(self.far, 1, 0, 1, 1)
        add_into(self.quarter(3, 1), [self.buf(0, 1)])
        self.send(self.far, 3, 1, 2, 3)

    def p2(self):
        self.far.wait_recv()
        add_into(self.quarter(0, None), [self.buf(1, None), self.buf(2, None)])
        self.c = Batch(self.net, self.mid)
        for k, d in enumerate((1, 3, 2)):
            there = self.net.moved(self.b, d)[self.b]
            self.c.send(self.at(**{self.b: there, self.e: None}), self.mid.at[k], self.net.ring(self.b, d))

    def line(self, by, h):
        e = None if h is None else ("half", h)
        return self.at(**{self.b: self.net.moved(self.b, by)[self.b], self.e: e})

    def line_buf(self, k, h):
        e = None if h is None else ("half", h)
        return self.mid.at[(k,) + chip_index({self.e: e}, drop=(self.a, self.b))]

    def send_line(self, batch, by, h, k, to):
        batch.send(self.line(by, h), self.line_buf(k, h), self.net.ring(self.b, to))

    def p2_ring(self):
        self.far.wait_recv()
        add_into(self.quarter(0, None), [self.buf(1, None), self.buf(2, None)])
        self.near = Batch(self.net, self.line_buf(0, None))
        self.send_line(self.near, 2, 0, 0, 1)
        self.send_line(self.near, 2, 1, 0, 3)
        self.c = Batch(self.net, self.mid.at[pl.ds(1, 2)])
        self.send_line(self.c, 1, 1, 1, 1)
        self.send_line(self.c, 3, 0, 2, 3)

    def p2_mid(self):
        self.near.wait_recv()
        add_into(self.line(1, 0), [self.line_buf(0, 0)])
        self.send_line(self.c, 1, 0, 1, 1)
        add_into(self.line(3, 1), [self.line_buf(0, 1)])
        self.send_line(self.c, 3, 1, 2, 3)
        self.ringed = True

    def p3(self):
        self.c.wait_recv()
        add_into(self.at(**{self.e: None}), [self.mid.at[k] for k in range(1 if self.ringed else 0, 3)])
        self.c = Batch(self.net, self.low)
        for k, d in enumerate((1, 3, 2)):
            there = self.net.moved(self.e, d)[self.e]
            self.c.send(self.at(**{self.e: there}), self.low.at[k], self.net.ring(self.e, d))

    def result(self):
        self.c.wait_recv()
        value = self.at()[...].astype(F32)
        for k in range(3):
            value = value + self.low[k].astype(F32)
        return value


RECTS = (
    (5, (0, 16), (0, 512), 0),
    (5, (16, 16), (0, 512), 1),
    (5, (32, 32), (0, 512), 2),
    (4, (0, 16), (0, 768), 0),
    (4, (0, 16), (768, 512), 1),
    (4, (0, 16), (1280, 768), 2),
    (3, (0, 16), (0, 512), 1),
    (0, (0, 16), (0, 512), 0),
    (1, (0, 16), (0, 512), 1),
    (2, (0, 16), (0, 512), 2),
)
BIG_FIRST = tuple(tuple(reversed(o)) for o in ORDER)


def reduce_buffers():
    shapes = []
    for _, (_, rows), (_, width), order in RECTS:
        a, b, e = BIG_FIRST[order]
        shapes += [
            (3,) + chip_shape((a,)) + (rows, width),
            (3,) + chip_shape((a, b)) + (rows, width),
            (3, rows, width),
        ]
    return shapes


class VectorSum:
    def __init__(self, net, total, bufs):
        self.net, self.total = net, total
        self.sib, self.whole, self.vx, self.half, self.vy, self.one, self.vz = bufs

    def start(self):
        self.c = self.net.copy(self.total, self.sib, self.net.ring("c", 0))

    def around(self, axis, bufs, part):
        self.c = Batch(self.net, bufs)
        for k, d in enumerate((1, 3, 2)):
            self.c.send(part(self.net.moved(axis, d)[axis]), bufs.at[k], self.net.ring(axis, d))

    def along_x(self):
        self.c.wait_recv()
        self.whole[...] = self.total[...] + self.sib[...]
        self.around("x", self.vx, lambda x: self.whole.at[:, columns(256 * x, 256)])

    def along_y(self):
        self.c.wait_recv()
        mine = self.whole[:, columns(256 * self.net.me["x"], 256)]
        for k in range(3):
            mine = mine + self.vx[k]
        self.half[0], self.half[1] = mine[:, :128], mine[:, 128:]
        self.around("y", self.vy, lambda y: self.half.at[lax.rem(y, 2)])

    def along_z(self):
        self.c.wait_recv()
        mine = self.half[lax.rem(self.net.me["y"], 2)]
        for k in range(3):
            mine = mine + self.vy[k]
        self.one[...] = mine
        self.around("z", self.vz, lambda z: self.one)

    def done(self, out):
        self.c.wait_recv()
        t = (self.one[...] + self.vz[0]) + (self.vz[1] + self.vz[2])
        sh = lax.axis_index("shard")
        to = lax.broadcasted_iota(jnp.int32, (128, 128), 0)
        i = lax.broadcasted_iota(jnp.int32, (128, 128), 1)
        place = jnp.where(i < 64, 8 * sh + (i & 7), 32 * lax.rem(sh, 4) + i - 64)
        pick = jnp.where((place == to) & (i < 96), 1.0, 0.0).astype(BF)
        high = t.astype(BF)
        rest = t - high.astype(F32)
        mid = rest.astype(BF)
        last = (rest - mid.astype(F32)).astype(BF)
        got = (mm(high, pick) + mm(mid, pick)) + mm(last, pick)
        r = lax.broadcasted_iota(jnp.int32, (16, 128), 0)
        i = lax.broadcasted_iota(jnp.int32, (16, 128), 1)
        keep = ((i < 64) & (lax.shift_right_logical(i, 3) == r)) | ((i >= 64) & (r == 8 + lax.div(sh, 4)))
        out[...] = jnp.broadcast_to(jnp.sum(jnp.where(keep, got, 0.0), axis=0, keepdims=True), (8, 128))


def attention_back(q, k, v, probs, context, d_context, dq, dk, dv, first, last, start):
    def body(i, carry):
        h = lax.rem(i + start, HEADS // 2)
        cols = columns(h * 128, 128)
        dks, dvs = [], []
        for b in range(2):
            mine, near = pl.ds(b * TOK, TOK), pl.ds(b * TOK, SPAN)
            at = columns((2 * h + b) * OWN, OWN)
            p = jnp.concatenate([probs[0, :, at], probs[1, :, at]], axis=0)
            dc = d_context[mine, cols]
            dc2 = lane_split(dc)
            prod = (dc.astype(F32) * context[mine, cols].astype(F32)).T
            dr = []
            for s in range(2):
                own = slice(s * TOK, s * TOK + TOK)
                dsum = jnp.sum(prod[s * HEAD : s * HEAD + HEAD], axis=0, keepdims=True)
                dp = mm(v[near, cols], dc2[own], NT)
                dr.append((p[:, own].astype(F32) * ((dp - dsum) * 0.125)).astype(BF))
            dr = jnp.concatenate(dr, axis=1)
            dvs.append(mm(p, dc2))
            dks.append(mm(dr, lane_split(q[mine, cols])))
            g = mm(k[near, cols], dr, TN)
            g = jnp.concatenate([g[:HEAD, :TOK], g[HEAD:, TOK:]], axis=0)
            dq[mine, cols] = g.T.astype(BF)
        for d, o in ((dks, dk), (dvs, dv)):
            o[0:TOK, cols] = d[0][:TOK].astype(BF)
            o[TOK:SPAN, cols] = (d[0][TOK:] + d[1][: SPAN - TOK]).astype(BF)
            o[SPAN:WIN, cols] = d[1][SPAN - TOK :].astype(BF)
        return carry

    lax.fori_loop(first, last, body, 0, unroll=2)


def column_sum(x):
    n, width = x.shape
    return jnp.sum(jnp.sum(x.astype(F32).reshape(n // 8, 8, width), axis=0), axis=0, keepdims=True)


class Return:
    def __init__(self, net, window, encoded, back, out, token_grad, sems):
        self.net, self.window, self.encoded, self.back = net, window, encoded, back
        self.out, self.token_grad, self.sems = out, token_grad, sems
        self.swaps = []
        self.lo = lax.rem(net.me["y"], 2)

    def pair(self, src, dst, sem):
        mine, theirs = rows_at(TOK * self.lo, TOK), rows_at(TOK * (1 - self.lo), TOK)
        local = pltpu.make_async_copy(src.at[mine], dst.at[self.lo], sem)
        local.start()
        return local, self.net.copy(src.at[theirs], dst.at[self.lo], self.net.pair(1 - self.lo))

    def start_encoded(self):
        self.swaps.append(self.pair(self.encoded, self.out, self.sems.at[0]))

    def start(self):
        w, net = self.window, self.net
        self.c = Batch(net, self.back)
        self.c.send(w.at[pl.ds(0, HALO)], self.back.at[0], net.ring("x", 3))
        self.c.send(w.at[pl.ds(HALO + OWN, HALO)], self.back.at[1], net.ring("x", 1))

    def total(self):
        self.c.wait_recv()
        rest = OWN - HALO
        own = pl.ds(HALO, OWN)
        y = self.window[own, :].astype(F32)
        low = y[:rest] + self.back[1, :rest].astype(F32)
        mid = y[rest:HALO] + self.back[1, rest:].astype(F32) + self.back[0, : HALO - rest].astype(F32)
        high = y[HALO:] + self.back[0, HALO - rest :].astype(F32)
        self.window[own, :] = jnp.concatenate([low, mid, high], axis=0).astype(BF)
        self.swaps.append(self.pair(self.window.at[own], self.token_grad, self.sems.at[1]))

    def done(self):
        for local, moved in self.swaps:
            local.wait()
            moved.wait_recv()


class Stream:
    SLOTS = 4

    def __init__(self, full, ring, sems):
        wq, wk, wv, wo, wi, wu = full
        self.ring = ring
        self.moves = []
        for n in range(12):
            slot = ring.at[n % self.SLOTS]
            if n < 4:
                pairs = [(wu.at[n], slot)]
            elif n < 8:
                pairs = [
                    (wi.at[n - 4, :, :, :, :, pl.ds(1024 * j, 1024)], slot.at[:, :, :, pl.ds(16 * j, 16)])
                    for j in range(4)
                ]
            else:
                w = (wo, wk, wv, wq)[n - 8]
                pairs = [(w.at[x], slot.at[:, :, :, pl.ds(16 * x, 16)]) for x in range(4)]
            self.moves.append([pltpu.make_async_copy(s, d, sems.at[4 * (n % self.SLOTS) + j]) for j, (s, d) in enumerate(pairs)])

    def start(self, n):
        for move in self.moves[n]:
            move.start()

    def wait(self, n):
        for move in self.moves[n]:
            move.wait()

    def part(self, n, j):
        return self.ring[n % self.SLOTS, :, :, :, 16 * j : 16 * j + 16].reshape(256, 1024)


class Backward:
    def __init__(self, ins, outs, scratch):
        self.weights = ins[:6]
        (self.x_in, self.q_in, self.k_in, self.v_in, self.probs_in, self.context_in, self.low_in, self.act_in) = ins[6:14]
        (self.slope_in, self.n1_in, self.inv1_in, self.d_in, self.encoded, self.vec, self.two) = ins[14:]
        self.owned, (self.out, self.token_grad, self.small) = outs[:6], outs[6:]
        take = iter(scratch)
        nxt = lambda n: [next(take) for _ in range(n)]
        (self.ring,) = nxt(1)
        self.g = nxt(6)
        self.bufs = nxt(3 * len(RECTS))
        self.x, self.q, self.k, self.v, self.context, self.act, self.inner, self.n1, self.inv1, self.d = nxt(10)
        self.outer, self.outer_sib, self.inner_sib, self.branch, self.branch_sib, self.d_context = nxt(6)
        self.dq, self.dk, self.dv, self.dq_sib, self.dk_sib, self.dv_sib, self.dx, self.back = nxt(8)
        self.kept, self.low_t = nxt(2)
        self.total, *vector_bufs = nxt(8)
        self.finals, self.ends = nxt(6), nxt(6)
        send_sem, recv_sem, self.local_sem = nxt(3)
        self.net = Net(send_sem, recv_sem)
        self.c = self.net.me["c"]
        self.loads = 0
        self.swaps = []
        self.stream = Stream(self.weights, self.ring, self.local_sem.at[pl.ds(0, 16)])
        self.vectors = VectorSum(self.net, self.total, vector_bufs)
        self.back_rows = Return(
            self.net, self.dx, self.kept, self.back, self.out, self.token_grad, self.local_sem.at[pl.ds(16, 2)]
        )
        lanes = []
        for n, (w, (r0, rows), (base, width), order) in enumerate(RECTS):
            lanes.append(
                Reduce(
                    self.net,
                    self.g[w],
                    pl.ds(r0, rows),
                    pl.ds(base, width),
                    BIG_FIRST[order],
                    self.bufs[3 * n : 3 * n + 3],
                )
            )
        self.lanes = lanes

    def load(self, src, dst):
        move = pltpu.make_async_copy(src, dst, self.local_sem.at[18 + self.loads])
        self.loads += 1
        move.start()
        return move

    def half(self, which, width):
        return columns(which * width, width)

    def share(self, src, dst, width):
        return self.net.copy(src.at[:, self.half(1 - self.c, width)], dst, self.net.ring("c", 0))

    def begin(self):
        self.greeted = self.net.greet()
        at_d = self.load(self.d_in, self.d)
        self.at_act = self.load(self.act_in, self.act)
        self.total[...] = jnp.zeros((16, D), F32)
        self.total[G2 : G2 + 2, :] = self.two[0:2, :]
        at_d.wait()

        def body(t, carry):
            r = some_rows(t)
            low = self.d[r, :].astype(BF)
            self.outer[r, :] = low
            return carry + jnp.sum(low.astype(F32).reshape(ROWS // 8, 8, D), axis=0)

        s = lax.fori_loop(0, OWN // ROWS, body, jnp.zeros((8, D), F32), unroll=2)
        self.total[BU : BU + 1, :] = jnp.sum(s, axis=0, keepdims=True)

    def load_all(self):
        self.at_slope = self.load(self.slope_in, self.inner)
        for n in range(4):
            self.stream.start(n)
        self.at_low = [self.load(self.low_in.at[n], self.dx.at[pl.ds(OWN * n, OWN)]) for n in range(2)]
        self.at_n1 = [self.load(self.n1_in, self.n1), self.load(self.inv1_in, self.inv1)]
        self.at_kept = self.load(self.encoded, self.kept)
        self.at_rest = [
            self.load(self.context_in, self.context),
            self.load(self.x_in, self.x),
            self.load(self.q_in, self.q),
            self.load(self.k_in, self.k),
            self.load(self.v_in, self.v),
        ]

    def meet(self):
        self.greeted()
        self.got_outer = self.share(self.outer, self.outer_sib, 512)

    def d_inner(self):
        self.at_slope.wait()
        for n in range(4):
            self.stream.wait(n)

            cols = slice(1024 * n, 1024 * n + 1024)
            y = mm(self.outer[...], self.ring[n].reshape(1024, 1024), NT)
            y = (y * self.inner[:, cols].astype(F32)).astype(BF)
            self.inner[:, cols] = y
            s = column_sum(y)
            for dp in (2 * n, 2 * n + 1):
                for t in range(4):
                    at = 512 * (dp - 2 * n) + 128 * t
                    self.total[8 + t : 9 + t, 128 * dp : 128 * dp + 128] = s[:, at : at + 128]
            self.stream.start(n + 4)

    def share_inner(self):
        self.got_inner = self.share(self.inner, self.inner_sib, 2048)

    def grad_outer(self):
        self.at_act.wait()
        self.got_outer.wait_recv()
        c = self.c
        mine = self.outer.at[:, self.half(c, 512)]

        def body(t, carry):
            cols = columns(t * 1024, 1024)
            y = mm(self.act[c, :, cols], mine[...], TN) + mm(self.act[1 - c, :, cols], self.outer_sib[...], TN)
            self.g[5][t] = y.astype(BF).reshape(2, 2, 4, 64, 512)
            return carry

        lax.fori_loop(0, 4, body, 0, unroll=2)
        self.at_probs = self.load(self.probs_in, self.act)

    def d_normed(self):
        for n in range(4):
            self.stream.wait(4 + n)
            cols = slice(256 * n, 256 * n + 256)
            y = self.d[:, cols]
            for j in range(4):
                y = y + mm(self.inner[:, 1024 * j : 1024 * j + 1024], self.stream.part(4 + n, j), NT)
            self.d[:, cols] = y
            self.stream.start(8 + n)

    def turn_low(self):
        for move in self.at_low:
            move.wait()
        for j, which in enumerate((self.c, 1 - self.c)):
            rows = pl.ds(pl.multiple_of(OWN * which, OWN), OWN)
            for x in range(4):
                part = self.dx[rows, 256 * x : 256 * x + 256]
                self.low_t[256 * x : 256 * x + 256, OWN * j : OWN * j + OWN] = part.T

    def grad_inner(self):
        self.got_inner.wait_recv()
        c = self.c

        def body(t, carry):
            x, j = lax.div(t, 2), lax.rem(t, 2)
            rows, cols = pl.ds(pl.multiple_of(x * 256, 256), 256), columns(j * 1024, 1024)
            y = mm(self.low_t[rows, :OWN], self.inner[:, columns(c * 2048 + j * 1024, 1024)])
            y = y + mm(self.low_t[rows, OWN:], self.inner_sib[:, cols])
            self.g[4][x, :, :, :, :, cols] = y.astype(BF).reshape(2, 2, 4, 16, 1024)
            return carry

        lax.fori_loop(0, 8, body, 0, unroll=2)

    def norm_one(self):
        for move in self.at_n1:
            move.wait()

        def body(t, carry):
            r = some_rows(t)
            d, n = self.d[r, :], self.n1[r, :]
            da = norm_back(d * self.vec[G1 : G1 + 1, :], n, self.inv1[r, :1])
            low = da.astype(BF)
            self.d[r, :] = da
            self.branch[r, :] = low
            new = (d * n, d, low.astype(F32))
            return tuple(a + jnp.sum(b.reshape(ROWS // 8, 8, D), axis=0) for a, b in zip(carry, new))

        zero = jnp.zeros((8, D), F32)
        sums = lax.fori_loop(0, OWN // ROWS, body, (zero, zero, zero))
        for row, s in zip((G1, S1, BO), sums):
            self.total[row : row + 1, :] = jnp.sum(s, axis=0, keepdims=True)
        self.got_branch = self.share(self.branch, self.branch_sib, 512)

    def d_mixed(self):
        self.stream.wait(8)
        for x in range(4):
            self.d_context[:, 256 * x : 256 * x + 256] = mm(self.branch[...], self.stream.part(8, x), NT).astype(BF)

    def grad_rows(self, left, right, sib, out):
        mine = right.at[:, self.half(self.c, 512)]

        def body(x, carry):
            rows = columns(x * 256, 256)
            y = mm(left[0][:, rows], mine[...], TN) + mm(left[1][:, rows], sib[...], TN)
            out[x] = y.astype(BF).reshape(2, 2, 4, 16, 512)
            return carry

        lax.fori_loop(0, 4, body, 0, unroll=2)

    def pair(self, ref):
        return ref.at[self.c], ref.at[1 - self.c]

    def grad_output(self):
        self.got_branch.wait_recv()
        for move in self.at_rest:
            move.wait()
        self.grad_rows(self.pair(self.context), self.branch, self.branch_sib, self.g[3])

    def attend(self, first, last):
        if first == 0:
            self.at_probs.wait()
        attention_back(
            self.q,
            self.k,
            self.v,
            self.act,
            self.context.at[self.c],
            self.d_context,
            self.dq,
            self.dk,
            self.dv,
            first,
            last,
            HEADS // 4 * (1 - self.c),
        )

    def share_heads(self):
        self.got_heads = [
            self.share(self.dk, self.dk_sib, 512),
            self.share(self.dv, self.dv_sib, 512),
            self.share(self.dq, self.dq_sib, 512),
        ]

    def head_sums(self):
        self.total[BQ : BQ + 1, :] = column_sum(self.dq[...])
        self.total[BV : BV + 1, :] = column_sum(self.dv[...])
        self.vectors.start()

    def grad_key(self):
        self.got_heads[0].wait_recv()
        self.grad_rows(self.pair(self.x), self.dk, self.dk_sib, self.g[1])

    def grad_value(self):
        self.got_heads[1].wait_recv()
        self.grad_rows(self.pair(self.x), self.dv, self.dv_sib, self.g[2])

    def grad_query(self):
        self.got_heads[2].wait_recv()
        own = pl.ds(HALO, OWN)
        rows = (self.x.at[self.c, own], self.x.at[1 - self.c, own])
        self.grad_rows(rows, self.dq, self.dq_sib, self.g[0])

    def d_halo(self):
        for n in (9, 10):
            self.stream.wait(n)

        def sides(ref):
            return jnp.concatenate([ref[:HALO, :], ref[HALO + OWN :, :]], axis=0)

        for x in range(4):
            cols = slice(256 * x, 256 * x + 256)
            y = mm(sides(self.dk), self.stream.part(9, x), NT) + mm(sides(self.dv), self.stream.part(10, x), NT)
            self.dx[:HALO, cols] = y[:HALO].astype(BF)
            self.dx[HALO + OWN :, cols] = y[HALO:].astype(BF)
        self.back_rows.start()

    def d_own(self):
        self.stream.wait(11)
        own = slice(HALO, HALO + OWN)
        for x in range(4):
            cols = slice(256 * x, 256 * x + 256)
            y = mm(self.dk[own, :], self.stream.part(9, x), NT) + mm(self.dv[own, :], self.stream.part(10, x), NT)
            y = y + self.d[:, cols] + mm(self.dq[...], self.stream.part(11, x), NT)
            self.dx[own, cols] = y.astype(BF)

    def encoded_out(self):
        self.at_kept.wait()
        self.back_rows.start_encoded()

    def rows_back(self):
        self.back_rows.total()

    def final(self, *weights):
        c, net = self.c, self.net
        for w in weights:
            final, end = self.finals[w], self.ends[w]
            for lane, (of, (r0, rows), (base, width), _) in zip(self.lanes, RECTS):
                if of == w:
                    final[pl.ds(r0, rows), pl.ds(base, width)] = lane.result()
            n, width = final.shape[0] // 2, final.shape[1]
            kept = final.at[pl.ds(pl.multiple_of(n * c, 8), n)]
            given = final.at[pl.ds(pl.multiple_of(n * (1 - c), 8), n)]
            self.swaps.append((w, net.copy(given, end.at[:, columns(c * width, width)], net.ring("c", 0))))
            end[:, columns(c * width, width)] = kept[...]

    def finish(self):
        self.vectors.done(self.small)
        stores = []
        for w, swap in self.swaps:
            swap.wait_recv()
            stores.append(self.load(self.ends[w], self.owned[w]))
        for store in stores:
            store.wait()
        self.back_rows.done()
        self.net.finish()


def backward_kernel(*refs):
    work = Backward(refs[:21], refs[21:30], refs[30:])
    u0, u1, u2, i0, i1, i2, o, q, k, v = work.lanes
    work.begin()
    work.meet()
    work.load_all()
    work.grad_outer()
    u0.p1()
    u1.p1()
    u2.p1()
    work.d_inner()
    work.share_inner()
    work.encoded_out()
    work.d_normed()
    u0.p1_mid()
    u1.p1_mid()
    u2.p1_mid()
    work.norm_one()
    work.turn_low()
    work.d_mixed()
    work.grad_inner()
    i0.p1()
    i1.p1()
    i2.p1()
    work.grad_output()
    o.p1()
    work.attend(0, 2)
    work.attend(2, 4)
    i0.p1_mid()
    i1.p1_mid()
    i2.p1_mid()
    work.share_heads()
    work.attend(4, 6)
    o.p1_mid()
    u0.p2_ring()
    u1.p2_ring()
    u2.p2_ring()
    work.attend(6, 8)
    work.head_sums()
    work.d_halo()
    u0.p2_mid()
    u1.p2_mid()
    u2.p2_mid()
    work.grad_key()
    k.p1()
    work.grad_value()
    v.p1()
    work.grad_query()
    q.p1()
    work.d_own()
    work.vectors.along_x()
    i0.p2()
    i1.p2()
    i2.p2()
    k.p1_mid()
    v.p1_mid()
    q.p1_mid()
    u0.p3()
    u1.p3()
    u2.p3()
    work.vectors.along_y()
    o.p2()
    work.rows_back()
    i0.p3()
    i1.p3()
    i2.p3()
    work.vectors.along_z()
    k.p2()
    v.p2()
    q.p2()
    work.final(5)
    o.p3()
    work.final(4)
    k.p3()
    v.p3()
    q.p3()
    work.final(3, 1, 2, 0)
    work.finish()


def backward_all(kept):
    any_space = pl.BlockSpec(memory_space=pl.ANY)
    vmem = pl.BlockSpec(memory_space=pltpu.VMEM)
    owned = [(r // 2, n) for r, n in BLOCKS]
    scratch = [((4, 2, 2, 4, 64, 1024), BF)]
    scratch += [(CHIPS + (r, n // 2), BF) for r, n in BLOCKS]
    scratch += [(s, BF) for s in reduce_buffers()]
    scratch += [((2, WIN, D), BF), ((OWN, D), BF), ((WIN, D), BF), ((WIN, D), BF), ((2, OWN, D), BF)]
    scratch += [((2, OWN, FF), BF), ((OWN, FF), BF), ((OWN, D), F32), ((OWN, 128), F32), ((OWN, D), F32)]
    scratch += [((OWN, D), BF), ((OWN, 512), BF), ((OWN, 2048), BF), ((OWN, D), BF), ((OWN, 512), BF), ((OWN, D), BF)]
    scratch += [((OWN, D), BF), ((WIN, D), BF), ((WIN, D), BF), ((OWN, 512), BF), ((WIN, 512), BF), ((WIN, 512), BF)]
    scratch += [((WIN, D), BF), ((2, HALO, D), BF), ((OWN, D), BF), ((D, 2 * OWN), BF)]
    scratch += [((16, D), F32), ((16, D), F32), ((16, D), F32), ((3, 16, 256), F32), ((2, 16, 128), F32), ((3, 16, 128), F32)]
    scratch += [((16, 128), F32), ((3, 16, 128), F32)]
    scratch += [((r, n // 2), F32) for r, n in BLOCKS] + [(s, F32) for s in owned]
    return pl.pallas_call(
        backward_kernel,
        name="backward_all",
        out_shape=[jax.ShapeDtypeStruct(s, F32) for s in owned]
        + [jax.ShapeDtypeStruct((2, TOK, D), BF)] * 2
        + [jax.ShapeDtypeStruct((8, 128), F32)],
        in_specs=[any_space] * 19 + [vmem] * 2,
        out_specs=[any_space] * 8 + [vmem],
        scratch_shapes=[pltpu.VMEM(s, t) for s, t in scratch]
        + [
            pltpu.SemaphoreType.DMA((72,)),
            pltpu.SemaphoreType.DMA((72,)),
            pltpu.SemaphoreType.DMA((40,)),
        ],
        compiler_params=pltpu.CompilerParams(collective_id=2, has_side_effects=True, vmem_limit_bytes=63 << 20),
    )(*kept)


def keep_kernel(*refs):
    (sums, *ins), outs = refs[:9], refs[9:]
    for src, dst in zip(ins, outs):
        dst[...] = src[...]
    for j, dst in enumerate(outs[8:]):
        dst[...] = sums[0:1, 8 * j : 8 * j + dst.shape[1]]


def keep(sums, *arrays):
    shapes = [(a.shape, a.dtype) for a in arrays] + [((1, 8), F32)] * 8 + [((1, 32), F32)]
    return pl.pallas_call(
        keep_kernel,
        name="keep",
        out_shape=[jax.ShapeDtypeStruct(s, t) for s, t in shapes],
        in_specs=[pl.BlockSpec(memory_space=pltpu.VMEM)] * 9,
        out_specs=[pl.BlockSpec(memory_space=pltpu.VMEM)] * 17,
    )(sums, *arrays)


def local(
    tokens, cotangent, seq_lengths, block_offsets, deal_order, wq, wk, wv, wo, bq, bv, bo, g1, s1, wi, bi, wu, bu, g2, s2
):
    small = [v[None] for v in (bq, bv, bo, g1, s1, bu, g2, s2, bi)]
    kept = forward_all(
        tokens[:, 0], cotangent[:, 0], seq_lengths[:, 0], deal_order[:, 0], (wq, wk, wv, wo, wi, wu), small
    )
    *owned, out, token_grad, sums = backward_all(kept)
    results = keep(sums, *owned, out, token_grad)
    owned, (out, token_grad), vectors = results[:6], results[6:8], results[8:]
    sbq, sbv, sbo, sg1, ss1, sbu, sg2, ss2, sbi = [v[0] for v in vectors]
    return (
        out[:, None],
        token_grad[:, None],
        *owned[:4],
        sbq,
        sbv,
        sbo,
        sg1,
        ss1,
        owned[4],
        sbi,
        owned[5],
        sbu,
        sg2,
        ss2,
    )


def solution(mesh):
    rows = P(None, "shard", "dp", None)
    table = P(None, "shard", None)
    matrix, vector = P(("dp", "shard"), None), P(("dp", "shard"))
    in_specs = (rows, rows) + (table,) * 3 + (matrix,) * 4 + (vector,) * 5 + (matrix, vector, matrix) + (vector,) * 3
    out_specs = (rows, rows) + (matrix,) * 4 + (vector,) * 5 + (matrix, vector, matrix) + (vector,) * 3
    return jax.shard_map(local, mesh=mesh, in_specs=in_specs, out_specs=out_specs, check_vma=False)
```

```python
import math

import jax
import jax.numpy as jnp
from jax import lax
from jax.experimental import pallas as pl
from jax.experimental.pallas import tpu as pltpu
from jax.sharding import PartitionSpec as P

MESH = pl.DeviceIdType.MESH
BF = jnp.bfloat16
F32 = jnp.float32
D = 1024
FF = 4096
HEADS = 16
HEAD = 64
TOK = 128
OWN = 2 * TOK
HALO = 192
WIN = OWN + 2 * HALO
AXES = ("x", "y", "z")
ORDER = (("z", "y", "x"), ("x", "z", "y"), ("y", "x", "z"))
CHIPS = (4, 2, 2, 4)


def position():
    dp, sh = lax.axis_index("dp"), lax.axis_index("shard")
    return {
        "x": lax.div(dp, 2),
        "y": lax.div(sh, 8) * 2 + lax.rem(dp, 2),
        "z": lax.div(lax.rem(sh, 8), 2),
        "c": lax.rem(sh, 2),
    }


def device_at(at):
    return (
        at["x"] * 2 + lax.rem(at["y"], 2),
        lax.div(at["y"], 2) * 8 + at["z"] * 2 + at["c"],
    )


class Batch:
    def __init__(self, net, whole):
        self.net, self.whole = net, whole
        self.k = net.used
        net.used += 1
        net.batches.append(self)

    def send(self, src, dst, device):
        pltpu.make_async_remote_copy(
            src_ref=src,
            dst_ref=dst,
            send_sem=self.net.send_sem.at[self.k],
            recv_sem=self.net.recv_sem.at[self.k],
            device_id=device,
            device_id_type=MESH,
        ).start()

    def wait_recv(self):
        pltpu.make_async_copy(self.whole, self.whole, self.net.recv_sem.at[self.k]).wait()

    def wait_send(self):
        pltpu.make_async_copy(self.whole, self.whole, self.net.send_sem.at[self.k]).wait()


class Net:
    def __init__(self, send_sem, recv_sem):
        self.me = position()
        self.send_sem, self.recv_sem = send_sem, recv_sem
        self.used = 0
        self.batches = []

    def moved(self, axis, by):
        at = dict(self.me)
        if axis == "c":
            at["c"] = 1 - at["c"]
        else:
            at[axis] = lax.rem(at[axis] + by, 4)
        return at

    def ring(self, axis, by):
        return device_at(self.moved(axis, by))

    def pair(self, lo):
        at = dict(self.me)
        at["y"] = lax.div(at["y"], 2) * 2 + lo
        return device_at(at)

    def copy(self, src, dst, device):
        batch = Batch(self, dst)
        batch.send(src, dst, device)
        return batch

    def greet(self):
        bar = pltpu.get_barrier_semaphore()
        peers = [self.ring("c", 0)] + [self.ring(a, b) for a in AXES for b in (1, 2, 3)]
        for p in peers:
            pl.semaphore_signal(bar, inc=1, device_id=p, device_id_type=MESH)
        return lambda: pl.semaphore_wait(bar, len(peers))

    def finish(self):
        for batch in self.batches:
            batch.wait_send()
        assert self.used <= self.send_sem.shape[0], self.used


def chip_index(at, drop=()):
    out = []
    for axis in AXES:
        if axis in drop:
            continue
        v = at[axis]
        if axis == "y":
            if v is None:
                out += [slice(None), slice(None)]
            elif isinstance(v, tuple):
                out += [v[1], slice(None)]
            else:
                out += [lax.rem(v, 2), lax.div(v, 2)]
        elif v is None:
            out.append(slice(None))
        elif isinstance(v, tuple):
            out.append(pl.ds(2 * v[1], 2))
        else:
            out.append(v)
    return tuple(out)


def chip_shape(drop):
    shape = ()
    for axis in AXES:
        if axis not in drop:
            shape += (2, 2) if axis == "y" else (4,)
    return shape


def columns(base, width):
    return pl.ds(pl.multiple_of(base, 128), width)


class Gather:
    def __init__(self, net, ref, rows, cols, order):
        self.net, self.ref, self.rows, self.cols = net, ref, rows, cols
        self.a, self.b, self.e = order

    def at(self, **over):
        place = {k: self.net.me[k] for k in AXES}
        place.update(over)
        return self.ref.at[chip_index(place) + (self.rows, self.cols)]

    def send(self, batch, region, axis, by):
        batch.send(region, region, self.net.ring(axis, by))

    def blocks(self, *chips):
        return Batch(self.net, self.ref.at[chips + (self.rows, self.cols)])

    def p1(self):
        self.c = self.blocks(pl.ds(0, 3), 0, 0, 0)
        for d in (1, 3, 2):
            self.send(self.c, self.at(), self.a, d)

    def p2(self):
        self.c.wait_recv()
        self.c = self.blocks(pl.ds(0, 3), 0, 0, slice(None))
        for d in (1, 3, 2):
            self.send(self.c, self.at(**{self.a: None}), self.b, d)

    def p2_ring(self):
        self.c.wait_recv()
        self.c = self.blocks(pl.ds(0, 2), 0, 0, slice(None))
        for d in (1, 3):
            self.send(self.c, self.at(**{self.a: None}), self.b, d)

    def p2_mid(self):
        self.c.wait_recv()
        self.c = self.blocks(0, 0, 0, slice(None))
        for h, to in enumerate((1, 3)):
            b = self.net.moved(self.b, 4 - to)[self.b]
            self.send(self.c, self.at(**{self.a: ("half", h), self.b: b}), self.b, to)

    def part(self, h, by):
        e = self.net.moved(self.e, by)[self.e]
        return self.at(**{self.a: h if h is None else ("half", h), self.b: None, self.e: e})

    def quarter(self):
        return Batch(self.net, self.part(None, 0))

    def p3(self):
        self.c.wait_recv()
        self.near, self.far = self.quarter(), self.quarter()
        self.send(self.near, self.part(0, 0), self.e, 1)
        self.send(self.near, self.part(1, 0), self.e, 3)
        self.send(self.far, self.part(1, 0), self.e, 1)
        self.send(self.far, self.part(0, 0), self.e, 3)
        self.core = self.blocks(*(slice(None),) * 4)
        self.send(self.core, self.part(None, 0), "c", 0)

    def p3_mid(self):
        self.near.wait_recv()
        self.last = self.quarter()
        self.send(self.last, self.part(0, 3), self.e, 1)
        self.send(self.last, self.part(1, 1), self.e, 3)

    def p3_core(self):
        self.far.wait_recv()
        self.send(self.core, self.part(None, 3), "c", 0)
        self.send(self.core, self.part(None, 1), "c", 0)

    def p3_end(self):
        self.last.wait_recv()
        self.send(self.core, self.part(None, 2), "c", 0)

    def done(self):
        self.core.wait_recv()


def each(lanes, step):
    for lane in lanes:
        step(lane)


def rows_at(base, count):
    return pl.ds(pl.multiple_of(base, TOK // 2), count)


class Window:
    def __init__(self, net, tokens, cotangent, window, cots, local_sem):
        self.net, self.window, self.cots = net, window, cots
        self.tokens, self.cotangent, self.local_sem = tokens, cotangent, local_sem
        self.lo = lax.rem(net.me["y"], 2)

    def pair(self, src, dst, sem):
        local = pltpu.make_async_copy(src.at[self.lo], dst, sem)
        local.start()
        return local, self.net.copy(src.at[1 - self.lo], dst, self.net.pair(1 - self.lo))

    def start(self):
        mine = self.window.at[rows_at(HALO + TOK * self.lo, TOK)]
        self.rows = self.pair(self.tokens, mine, self.local_sem.at[0])

    def start_cots(self):
        mine = self.cots.at[rows_at(TOK * self.lo, TOK)]
        self.cot_rows = self.pair(self.cotangent, mine, self.local_sem.at[1])

    def halo(self):
        local, moved = self.rows
        local.wait()
        moved.wait_recv()
        w, net = self.window, self.net
        self.c = Batch(net, w.at[pl.ds(0, 2 * HALO)])
        self.c.send(w.at[pl.ds(OWN, HALO)], w.at[pl.ds(0, HALO)], net.ring("x", 1))
        self.c.send(w.at[pl.ds(HALO, HALO)], w.at[pl.ds(HALO + OWN, HALO)], net.ring("x", 3))

    def done(self):
        self.c.wait_recv()

    def cots_done(self):
        local, moved = self.cot_rows
        local.wait()
        moved.wait_recv()


def place_own(me, mine, peer, full):
    here = chip_index(me)
    c = me["c"]
    first = c == 0

    def both(a, b):
        return jnp.concatenate([jnp.where(first, a, b), jnp.where(first, b, a)], axis=0)

    half = columns(c * 512, 512)
    for j in range(4):
        r = slice(8 * j, 8 * j + 8)
        full[j][here + (slice(None), half)] = both(mine[r, half], peer[r, half])
    for t in range(2):
        r, s = slice(32 + 8 * t, 40 + 8 * t), slice(48 + 8 * t, 56 + 8 * t)
        a = jnp.where(first, mine[r, :], mine[s, :])
        b = jnp.where(first, peer[r, :], peer[s, :])
        full[4][here + (slice(None), columns(c * 2048 + 1024 * t, 1024))] = both(a, b)
    full[5][here + (slice(None), half)] = both(mine[64:96, half], peer[64:96, half])


BLOCKS = ((16, 1024),) * 4 + ((16, 4096), (64, 1024))


SPAN = TOK + 2 * HALO
NT = (((1,), (1,)), ((), ()))
TN = (((0,), (0,)), ((), ()))
NN = (((1,), (0,)), ((), ()))


def mm(a, b, dims=NN):
    return lax.dot_general(a, b, dims, preferred_element_type=F32)


def tile(w, n0, n):
    return w[:, :, :, :, :, columns(n0, n)].reshape(-1, n)


def project(rows, w, out, bias=None, n=1024):
    def body(t, carry):
        cols = columns(t * n, n)
        y = mm(rows[...], tile(w, t * n, n))
        if bias is not None:
            y = y + bias[:, cols]
        out[:, cols] = y.astype(BF)
        return carry

    lax.fori_loop(0, out.shape[1] // n, body, 0)


def lane_split(x):
    low = lax.broadcasted_iota(jnp.int32, x.shape, 1) < HEAD
    zero = jnp.zeros_like(x)
    return jnp.concatenate([jnp.where(low, x, zero), jnp.where(low, zero, x)], axis=0)


def lane_join(x):
    n = x.shape[0] // 2
    low = lax.broadcasted_iota(jnp.int32, (n, x.shape[1]), 1) < HEAD
    return jnp.where(low, x[:n], x[n:])


def attention(q, k, v, bias, probs, context, first, last):
    def body(h, carry):
        cols = columns(h * 128, 128)
        for b in range(2):
            mine, near = pl.ds(b * TOK, TOK), pl.ds(b * TOK, SPAN)
            some, two = k[near, cols], lane_split(q[mine, cols]) * jnp.asarray(0.125, BF)
            p = []
            for s in range(2):
                e = mm(some, two[s * TOK : s * TOK + TOK], NT) + bias[b]
                e = jnp.exp(e - jnp.max(e, axis=0, keepdims=True))
                p.append((e * (1.0 / jnp.sum(e, axis=0, keepdims=True))).astype(BF))
            p = jnp.concatenate(p, axis=1)
            at = columns((2 * h + b) * OWN, OWN)
            probs[0, :, at], probs[1, :, at] = p[:OWN], p[OWN:]
            y = mm(v[near, cols], p, TN)
            y = jnp.concatenate([y[:HEAD, :TOK], y[HEAD:, TOK:]], axis=0)
            context[mine, cols] = y.T.astype(BF)
        return carry

    lax.fori_loop(first, last, body, 0, unroll=2)


def normalized(a):
    centred = a - jnp.mean(a, axis=-1, keepdims=True)
    inv = lax.rsqrt(jnp.mean(centred * centred, axis=-1, keepdims=True) + 1e-05)
    return centred * inv, inv


def norm_back(dn, n, inv):
    return inv * (dn - jnp.mean(dn, axis=-1, keepdims=True) - n * jnp.mean(dn * n, axis=-1, keepdims=True))


def feed_in(low, wi, bi, act, slope, first, last, n=512):
    def body(t, carry):
        cols = columns(t * n, n)
        u = mm(low[...], tile(wi, t * n, n)) + bi[:, cols]
        phi = 0.5 + 0.5 * lax.erf(u * math.sqrt(0.5))
        act[:, cols] = (u * phi).astype(BF)
        slope[:, cols] = (phi + u * (jnp.exp(-0.5 * (u * u)) * (1.0 / math.sqrt(2 * math.pi)))).astype(BF)
        return carry

    lax.fori_loop(first, last, body, 0, unroll=2)


ROWS = 32


def some_rows(t):
    return pl.ds(pl.multiple_of(t * ROWS, ROWS), ROWS)


def segment_bias(lengths, order, start, lo, bias):
    ends, total = [], 0
    for k in range(16):
        total = total + lengths[lo, order[lo, k]]
        ends.append(total)

    def which(at):
        found = jnp.where(at < 0, -1, 0)
        for e in ends:
            found = found + (at >= e).astype(jnp.int32)
        return found

    keys = which(start + lax.broadcasted_iota(jnp.int32, (WIN, TOK), 0))
    queries = which(start + HALO + lax.broadcasted_iota(jnp.int32, (8, OWN), 1))[:1]
    for b in range(2):
        same = keys[b * TOK : b * TOK + SPAN] == queries[:, b * TOK : b * TOK + TOK]
        bias[b] = jnp.where(same, 0.0, -1e30)


class Vectors:
    def __init__(self, net, small, rows, tiles, vec, inner):
        self.net, self.small, self.rows = net, small, rows
        self.own, self.sib, self.tz, self.ty, self.tx = tiles
        self.vec, self.inner = vec, inner

    def around(self, axis, tiles, mine):
        self.c = Batch(self.net, tiles.at[pl.ds(0, 3)])
        for d in (1, 3, 2):
            self.c.send(tiles.at[mine], tiles.at[mine], self.net.ring(axis, d))

    def place(self):
        sh = lax.axis_index("shard")
        self.rows[...] = jnp.zeros((16, 128), F32)
        for j in range(9):
            n = self.small[j].shape[1]
            self.rows[j : j + 1, :n] = self.small[j][...].astype(F32)
        i = lax.broadcasted_iota(jnp.int32, (128, 128), 0)
        to = lax.broadcasted_iota(jnp.int32, (128, 128), 1)
        value = self.rows[...].astype(BF)
        eight = mm(value, jnp.where((to == 8 * sh + i) & (i < 8), 1.0, 0.0).astype(BF))
        many = mm(value, jnp.where((to == 32 * lax.rem(sh, 4) + i) & (i < 32), 1.0, 0.0).astype(BF))
        r = lax.broadcasted_iota(jnp.int32, (16, 128), 0)
        many = jnp.broadcast_to(many[8:9], (16, 128))
        tile = jnp.where(r < 8, eight, jnp.where(r == 8 + lax.div(sh, 4), many, 0.0))
        self.own[...] = tile.astype(BF)

    def start(self):
        self.c = self.net.copy(self.own, self.sib, self.net.ring("c", 0))

    def wait(self):
        self.c.wait_recv()

    def along_z(self):
        self.wait()
        z = self.net.me["z"]
        self.tz[z] = self.own[...] + self.sib[...]
        self.around("z", self.tz, z)

    def along_y(self):
        self.wait()
        y = self.net.me["y"]
        self.ty[y] = (self.tz[0] + self.tz[1]) + (self.tz[2] + self.tz[3])
        self.around("y", self.ty, y)

    def along_x(self):
        self.wait()
        x = self.net.me["x"]
        self.tx[x, 0] = self.ty[0] + self.ty[2]
        self.tx[x, 1] = self.ty[1] + self.ty[3]
        self.around("x", self.tx, x)

    def done(self):
        self.wait()
        for dp in range(8):
            got = self.tx[dp // 2, dp % 2].astype(F32)
            self.vec[:, 128 * dp : 128 * dp + 128] = got[:8]
            for t in range(4):
                at = 512 * dp + 128 * t
                self.inner[:, at : at + 128] = got[8 + t : 9 + t]


BQ, BV, BO, G1, S1, BU, G2, S2 = range(8)


class Forward:
    def __init__(self, ins, outs, scratch):
        self.tokens, self.cotangent, self.lengths, self.order = ins[:4]
        self.own, self.small = ins[4:10], ins[10:]
        self.weights_out = outs[:6]
        (self.x_out, self.q_out, self.k_out, self.v_out, self.probs_out, self.context_out, self.low_out) = outs[6:13]
        (self.act_out, self.slope_out, self.n1_out, self.inv1_out, self.d_out, self.encoded_out) = outs[13:19]
        self.vec_out, self.two_out = outs[19:]
        self.mine, self.peer = scratch[:2]
        self.full, scratch = scratch[2:8], scratch[8:]
        (self.window, self.cots, self.q, self.k, self.v, self.probs, self.context, self.low) = scratch[:8]
        (self.act, self.slope, self.bias, self.n1, self.inv1, self.normed, self.total, self.encoded) = scratch[8:16]
        self.vec, self.inner, self.two, self.placed = scratch[16:20]
        tiles, (send_sem, recv_sem, self.local_sem) = scratch[20:25], scratch[25:]
        self.net = Net(send_sem, recv_sem)
        self.me, self.c = self.net.me, self.net.me["c"]
        self.lo = lax.rem(self.me["y"], 2)
        self.stores, self.gets = [], []
        self.vectors = Vectors(self.net, self.small, self.placed, tiles, self.vec, self.inner)
        self.view = Window(self.net, self.tokens, self.cotangent, self.window, self.cots, self.local_sem)
        rows, half = slice(None), columns(self.c * 512, 512)
        wi, wu = self.full[4], self.full[5]

        def inner(base, width, order):
            return Gather(self.net, wi, rows, columns(self.c * 2048 + base, width), ORDER[order])

        self.lanes = (
            [Gather(self.net, self.full[j], rows, half, ORDER[j]) for j in range(3)],
            [Gather(self.net, self.full[3], rows, half, ORDER[2]), inner(0, 1024, 1), inner(1024, 1024, 2)],
            [
                Gather(self.net, wu, pl.ds(0, 32), half, ORDER[0]),
                Gather(self.net, wu, pl.ds(32, 16), half, ORDER[1]),
                Gather(self.net, wu, pl.ds(48, 16), half, ORDER[2]),
            ],
        )

    def store(self, src, dst):
        move = pltpu.make_async_copy(src, dst, self.local_sem.at[2 + len(self.stores)])
        move.start()
        self.stores.append(move)

    def both(self, src, dst):
        self.gets.append(self.net.copy(src, dst.at[self.c], self.net.ring("c", 0)))
        self.store(src, dst.at[self.c])

    def begin(self):
        greeted = self.net.greet()
        for j in range(4):
            self.mine[8 * j : 8 * j + 8, :] = self.own[j][...]
            self.mine[32 + 8 * j : 40 + 8 * j, :] = self.own[4][:, 1024 * j : 1024 * j + 1024]
        self.mine[64:96, :] = self.own[5][...]
        self.vectors.place()
        segment_bias(self.lengths, self.order, self.me["x"] * OWN - HALO, self.lo, self.bias)
        greeted()
        swap = self.net.copy(self.mine, self.peer, self.net.ring("c", 0))
        self.view.start()
        self.vectors.start()
        swap.wait_recv()
        place_own(self.me, self.mine, self.peer, self.full)

    def halo(self):
        self.view.halo()

    def cots_in(self):
        self.view.start_cots()

    def rows_done(self):
        self.view.done()
        self.both(self.window, self.x_out)

    def query(self):
        project(self.window.at[pl.ds(HALO, OWN)], self.full[0], self.q, self.vec.at[BQ : BQ + 1])

    def key(self):
        project(self.window, self.full[1], self.k)

    def value(self):
        project(self.window, self.full[2], self.v, self.vec.at[BV : BV + 1])

    def keep_heads(self):
        for j in range(3):
            self.store(self.full[j], self.weights_out[j])
        for src, dst in ((self.q, self.q_out), (self.k, self.k_out), (self.v, self.v_out)):
            self.store(src, dst)

    def attend(self, first, last):
        attention(self.q, self.k, self.v, self.bias, self.probs, self.context, first, last)

    def keep_probs(self):
        self.both(self.context, self.context_out)
        self.store(self.probs, self.probs_out)

    def mix(self):
        self.store(self.full[3], self.weights_out[3])
        self.store(self.full[4], self.weights_out[4])

        def body(t, carry):
            cols = columns(t * 512, 512)
            y = mm(self.context[...], tile(self.full[3], t * 512, 512)) + self.vec[BO : BO + 1, cols]
            self.total[:, cols] = y + self.window[pl.ds(HALO, OWN), cols].astype(F32)
            return carry

        lax.fori_loop(0, 2, body, 0, unroll=2)

    def norm_one(self):
        def body(t, carry):
            r = some_rows(t)
            n, inv = normalized(self.total[r, :])
            self.n1[r, :] = n
            self.inv1[r, :] = jnp.broadcast_to(inv, (ROWS, 128))
            y = n * self.vec[G1 : G1 + 1, :] + self.vec[S1 : S1 + 1, :]
            self.normed[r, :] = y
            self.low[r, :] = y.astype(BF)
            return carry

        lax.fori_loop(0, OWN // ROWS, body, 0, unroll=2)
        self.both(self.low, self.low_out)
        self.store(self.n1, self.n1_out)
        self.store(self.inv1, self.inv1_out)

    def feed_in(self, first, last):
        feed_in(self.low, self.full[4], self.inner, self.act, self.slope, first, last)
        if last == FF // 512:
            self.both(self.act, self.act_out)
            self.store(self.slope, self.slope_out)
            self.store(self.vec, self.vec_out)

    def feed_out(self):
        self.store(self.full[5], self.weights_out[5])

        def body(t, carry):
            cols = columns(t * 512, 512)
            y = mm(self.act[...], tile(self.full[5], t * 512, 512)) + self.vec[BU : BU + 1, cols]
            self.total[:, cols] = y + self.normed[:, cols]
            return carry

        lax.fori_loop(0, 2, body, 0, unroll=2)

    def cots_done(self):
        self.view.cots_done()

    def norm_two(self):
        def body(t, carry):
            r = some_rows(t)
            n, inv = normalized(self.total[r, :])
            gain = self.vec[G2 : G2 + 1, :]
            self.encoded[r, :] = (n * gain + self.vec[S2 : S2 + 1, :]).astype(BF)
            d = self.cots[r, :].astype(F32)
            self.normed[r, :] = norm_back(d * gain, n, inv)
            dn = jnp.sum((d * n).reshape(ROWS // 8, 8, D), axis=0)
            return carry[0] + dn, carry[1] + jnp.sum(d.reshape(ROWS // 8, 8, D), axis=0)

        zero = jnp.zeros((8, D), F32)
        gain_sum, shift_sum = lax.fori_loop(0, OWN // ROWS, body, (zero, zero), unroll=2)
        self.two[0:1, :] = jnp.sum(gain_sum, axis=0, keepdims=True)
        self.two[1:2, :] = jnp.sum(shift_sum, axis=0, keepdims=True)
        self.two[2:8, :] = jnp.zeros((6, D), F32)
        self.store(self.normed, self.d_out)
        self.store(self.encoded, self.encoded_out)
        self.store(self.two, self.two_out)

    def finish(self):
        for got in self.gets:
            got.wait_recv()
        for move in self.stores:
            move.wait()
        self.net.finish()


def forward_kernel(*refs):
    work = Forward(refs[:19], refs[19:40], refs[40:])
    a, b, u = work.lanes
    work.begin()
    each(a, Gather.p1)
    each(b, Gather.p1)
    each(u, Gather.p1)
    work.vectors.along_z()
    each(a, Gather.p2)
    each(b, Gather.p2_ring)
    each(u, Gather.p2_ring)
    work.vectors.along_y()
    each(a, Gather.p3)
    each(b, Gather.p2_mid)
    each(u, Gather.p2_mid)
    work.halo()
    work.vectors.along_x()
    each(a, Gather.p3_mid)
    each(b, Gather.p3)
    work.cots_in()
    each(a, Gather.p3_core)
    each(a, Gather.p3_end)
    work.vectors.done()
    each(a, Gather.done)
    each(b, Gather.p3_mid)
    each(u, Gather.p3)
    work.query()
    work.rows_done()
    work.key()
    work.value()
    work.attend(0, 2)
    each(b, Gather.p3_core)
    work.attend(2, 4)
    each(b, Gather.p3_end)
    work.attend(4, 6)
    each(u, Gather.p3_mid)
    work.attend(6, 8)
    work.keep_heads()
    each(u, Gather.p3_core)
    work.keep_probs()
    each(b, Gather.done)
    work.mix()
    work.norm_one()
    work.feed_in(0, 2)
    work.feed_in(2, 4)
    each(u, Gather.p3_end)
    work.feed_in(4, 6)
    work.feed_in(6, 8)
    each(u, Gather.done)
    work.feed_out()
    work.cots_done()
    work.norm_two()
    work.finish()


def forward_all(tokens, cotangent, lengths, order, own, small):
    any_space = pl.BlockSpec(memory_space=pl.ANY)
    vmem = pl.BlockSpec(memory_space=pltpu.VMEM)
    smem = pl.BlockSpec(memory_space=pltpu.SMEM)
    full = [(CHIPS + s, BF) for s in BLOCKS]
    kept = [
        ((2, WIN, D), BF),
        ((OWN, D), BF),
        ((WIN, D), BF),
        ((WIN, D), BF),
        ((2, OWN, FF), BF),
        ((2, OWN, D), BF),
        ((2, OWN, D), BF),
        ((2, OWN, FF), BF),
        ((OWN, FF), BF),
        ((OWN, D), F32),
        ((OWN, 128), F32),
        ((OWN, D), F32),
        ((OWN, D), BF),
        ((8, D), F32),
        ((8, D), F32),
    ]
    scratch = [((96, 1024), BF)] * 2 + full
    scratch += [((WIN, D), BF), ((OWN, D), BF), ((OWN, D), BF), ((WIN, D), BF), ((WIN, D), BF)]
    scratch += [((2, OWN, FF), BF), ((OWN, D), BF), ((OWN, D), BF), ((OWN, FF), BF), ((OWN, FF), BF)]
    scratch += [((2, SPAN, TOK), F32), ((OWN, D), F32), ((OWN, 128), F32), ((OWN, D), F32), ((OWN, D), F32)]
    scratch += [((OWN, D), BF), ((8, D), F32), ((1, FF), F32), ((8, D), F32), ((16, 128), F32)]
    scratch += [((16, 128), BF)] * 2 + [((4, 16, 128), BF)] * 2 + [((4, 2, 16, 128), BF)]
    return pl.pallas_call(
        forward_kernel,
        name="forward_all",
        out_shape=[jax.ShapeDtypeStruct(s, t) for s, t in full + kept],
        in_specs=[any_space] * 2 + [smem] * 2 + [vmem] * 15,
        out_specs=[any_space] * 21,
        scratch_shapes=[pltpu.VMEM(s, t) for s, t in scratch]
        + [
            pltpu.SemaphoreType.DMA((72,)),
            pltpu.SemaphoreType.DMA((72,)),
            pltpu.SemaphoreType.DMA((24,)),
        ],
        compiler_params=pltpu.CompilerParams(collective_id=1, has_side_effects=True, vmem_limit_bytes=62 << 20),
    )(tokens, cotangent, lengths, order, *own, *small)


def add_into(dst, srcs):
    lead = dst.shape[:-2]
    loop = lead[:-1] if len(lead) > 1 else lead
    total = math.prod(loop)

    def body(k, carry):
        index, rest = (), k
        for n in reversed(loop):
            index = (lax.rem(rest, n),) + index
            rest = lax.div(rest, n)
        value = dst[index].astype(F32)
        for s in srcs:
            value = value + s[index].astype(F32)
        dst[index] = value.astype(BF)
        return carry

    lax.fori_loop(0, total, body, 0)


class Reduce:
    def __init__(self, net, ref, rows, cols, order, bufs):
        self.net, self.ref, self.rows, self.cols = net, ref, rows, cols
        self.a, self.b, self.e = order
        self.wide, self.mid, self.low = bufs
        self.ringed = False

    def at(self, **over):
        place = {k: self.net.me[k] for k in AXES}
        place.update(over)
        return self.ref.at[chip_index(place) + (self.rows, self.cols)]

    def quarter(self, by, h):
        b = None if h is None else ("half", h)
        return self.at(**{self.a: self.net.moved(self.a, by)[self.a], self.b: b, self.e: None})

    def buf(self, k, h):
        b = None if h is None else ("half", h)
        return self.wide.at[(k,) + chip_index({self.b: b, self.e: None}, drop=(self.a,))]

    def send(self, batch, by, h, k, to):
        batch.send(self.quarter(by, h), self.buf(k, h), self.net.ring(self.a, to))

    def p1(self):
        self.near = Batch(self.net, self.buf(0, None))
        self.send(self.near, 2, 0, 0, 1)
        self.send(self.near, 2, 1, 0, 3)
        self.far = Batch(self.net, self.wide.at[pl.ds(1, 2)])
        self.send(self.far, 1, 1, 1, 1)
        self.send(self.far, 3, 0, 2, 3)

    def p1_mid(self):
        self.near.wait_recv()
        add_into(self.quarter(1, 0), [self.buf(0, 0)])
        self.send(self.far, 1, 0, 1, 1)
        add_into(self.quarter(3, 1), [self.buf(0, 1)])
        self.send(self.far, 3, 1, 2, 3)

    def p2(self):
        self.far.wait_recv()
        add_into(self.quarter(0, None), [self.buf(1, None), self.buf(2, None)])
        self.c = Batch(self.net, self.mid)
        for k, d in enumerate((1, 3, 2)):
            there = self.net.moved(self.b, d)[self.b]
            self.c.send(self.at(**{self.b: there, self.e: None}), self.mid.at[k], self.net.ring(self.b, d))

    def line(self, by, h):
        e = None if h is None else ("half", h)
        return self.at(**{self.b: self.net.moved(self.b, by)[self.b], self.e: e})

    def line_buf(self, k, h):
        e = None if h is None else ("half", h)
        return self.mid.at[(k,) + chip_index({self.e: e}, drop=(self.a, self.b))]

    def send_line(self, batch, by, h, k, to):
        batch.send(self.line(by, h), self.line_buf(k, h), self.net.ring(self.b, to))

    def p2_ring(self):
        self.far.wait_recv()
        add_into(self.quarter(0, None), [self.buf(1, None), self.buf(2, None)])
        self.near = Batch(self.net, self.line_buf(0, None))
        self.send_line(self.near, 2, 0, 0, 1)
        self.send_line(self.near, 2, 1, 0, 3)
        self.c = Batch(self.net, self.mid.at[pl.ds(1, 2)])
        self.send_line(self.c, 1, 1, 1, 1)
        self.send_line(self.c, 3, 0, 2, 3)

    def p2_mid(self):
        self.near.wait_recv()
        add_into(self.line(1, 0), [self.line_buf(0, 0)])
        self.send_line(self.c, 1, 0, 1, 1)
        add_into(self.line(3, 1), [self.line_buf(0, 1)])
        self.send_line(self.c, 3, 1, 2, 3)
        self.ringed = True

    def p3(self):
        self.c.wait_recv()
        add_into(self.at(**{self.e: None}), [self.mid.at[k] for k in range(1 if self.ringed else 0, 3)])
        self.c = Batch(self.net, self.low)
        for k, d in enumerate((1, 3, 2)):
            there = self.net.moved(self.e, d)[self.e]
            self.c.send(self.at(**{self.e: there}), self.low.at[k], self.net.ring(self.e, d))

    def result(self):
        self.c.wait_recv()
        value = self.at()[...].astype(F32)
        for k in range(3):
            value = value + self.low[k].astype(F32)
        return value


RECTS = (
    (5, (0, 16), (0, 512), 0),
    (5, (16, 16), (0, 512), 1),
    (5, (32, 32), (0, 512), 2),
    (4, (0, 16), (0, 768), 0),
    (4, (0, 16), (768, 512), 1),
    (4, (0, 16), (1280, 768), 2),
    (3, (0, 16), (0, 512), 1),
    (0, (0, 16), (0, 512), 0),
    (1, (0, 16), (0, 512), 1),
    (2, (0, 16), (0, 512), 2),
)
BIG_FIRST = tuple(tuple(reversed(o)) for o in ORDER)


def reduce_buffers():
    shapes = []
    for _, (_, rows), (_, width), order in RECTS:
        a, b, e = BIG_FIRST[order]
        shapes += [
            (3,) + chip_shape((a,)) + (rows, width),
            (3,) + chip_shape((a, b)) + (rows, width),
            (3, rows, width),
        ]
    return shapes


class VectorSum:
    def __init__(self, net, total, bufs):
        self.net, self.total = net, total
        self.sib, self.whole, self.vx, self.half, self.vy, self.one, self.vz = bufs

    def start(self):
        self.c = self.net.copy(self.total, self.sib, self.net.ring("c", 0))

    def around(self, axis, bufs, part):
        self.c = Batch(self.net, bufs)
        for k, d in enumerate((1, 3, 2)):
            self.c.send(part(self.net.moved(axis, d)[axis]), bufs.at[k], self.net.ring(axis, d))

    def along_x(self):
        self.c.wait_recv()
        self.whole[...] = self.total[...] + self.sib[...]
        self.around("x", self.vx, lambda x: self.whole.at[:, columns(256 * x, 256)])

    def along_y(self):
        self.c.wait_recv()
        mine = self.whole[:, columns(256 * self.net.me["x"], 256)]
        for k in range(3):
            mine = mine + self.vx[k]
        self.half[0], self.half[1] = mine[:, :128], mine[:, 128:]
        self.around("y", self.vy, lambda y: self.half.at[lax.rem(y, 2)])

    def along_z(self):
        self.c.wait_recv()
        mine = self.half[lax.rem(self.net.me["y"], 2)]
        for k in range(3):
            mine = mine + self.vy[k]
        self.one[...] = mine
        self.around("z", self.vz, lambda z: self.one)

    def done(self, out):
        self.c.wait_recv()
        t = (self.one[...] + self.vz[0]) + (self.vz[1] + self.vz[2])
        sh = lax.axis_index("shard")
        to = lax.broadcasted_iota(jnp.int32, (128, 128), 0)
        i = lax.broadcasted_iota(jnp.int32, (128, 128), 1)
        place = jnp.where(i < 64, 8 * sh + (i & 7), 32 * lax.rem(sh, 4) + i - 64)
        pick = jnp.where((place == to) & (i < 96), 1.0, 0.0).astype(BF)
        high = t.astype(BF)
        rest = t - high.astype(F32)
        mid = rest.astype(BF)
        last = (rest - mid.astype(F32)).astype(BF)
        got = (mm(high, pick) + mm(mid, pick)) + mm(last, pick)
        r = lax.broadcasted_iota(jnp.int32, (16, 128), 0)
        i = lax.broadcasted_iota(jnp.int32, (16, 128), 1)
        keep = ((i < 64) & (lax.shift_right_logical(i, 3) == r)) | ((i >= 64) & (r == 8 + lax.div(sh, 4)))
        out[...] = jnp.broadcast_to(jnp.sum(jnp.where(keep, got, 0.0), axis=0, keepdims=True), (8, 128))


def attention_back(q, k, v, probs, context, d_context, dq, dk, dv, first, last, start):
    def body(i, carry):
        h = lax.rem(i + start, HEADS // 2)
        cols = columns(h * 128, 128)
        dks, dvs = [], []
        for b in range(2):
            mine, near = pl.ds(b * TOK, TOK), pl.ds(b * TOK, SPAN)
            at = columns((2 * h + b) * OWN, OWN)
            p = jnp.concatenate([probs[0, :, at], probs[1, :, at]], axis=0)
            dc = d_context[mine, cols]
            dc2 = lane_split(dc)
            prod = (dc.astype(F32) * context[mine, cols].astype(F32)).T
            dr = []
            for s in range(2):
                own = slice(s * TOK, s * TOK + TOK)
                dsum = jnp.sum(prod[s * HEAD : s * HEAD + HEAD], axis=0, keepdims=True)
                dp = mm(v[near, cols], dc2[own], NT)
                dr.append((p[:, own].astype(F32) * ((dp - dsum) * 0.125)).astype(BF))
            dr = jnp.concatenate(dr, axis=1)
            dvs.append(mm(p, dc2))
            dks.append(mm(dr, lane_split(q[mine, cols])))
            g = mm(k[near, cols], dr, TN)
            g = jnp.concatenate([g[:HEAD, :TOK], g[HEAD:, TOK:]], axis=0)
            dq[mine, cols] = g.T.astype(BF)
        for d, o in ((dks, dk), (dvs, dv)):
            o[0:TOK, cols] = d[0][:TOK].astype(BF)
            o[TOK:SPAN, cols] = (d[0][TOK:] + d[1][: SPAN - TOK]).astype(BF)
            o[SPAN:WIN, cols] = d[1][SPAN - TOK :].astype(BF)
        return carry

    lax.fori_loop(first, last, body, 0, unroll=2)


def column_sum(x):
    n, width = x.shape
    return jnp.sum(jnp.sum(x.astype(F32).reshape(n // 8, 8, width), axis=0), axis=0, keepdims=True)


class Return:
    def __init__(self, net, window, encoded, back, out, token_grad, sems):
        self.net, self.window, self.encoded, self.back = net, window, encoded, back
        self.out, self.token_grad, self.sems = out, token_grad, sems
        self.swaps = []
        self.lo = lax.rem(net.me["y"], 2)

    def pair(self, src, dst, sem):
        mine, theirs = rows_at(TOK * self.lo, TOK), rows_at(TOK * (1 - self.lo), TOK)
        local = pltpu.make_async_copy(src.at[mine], dst.at[self.lo], sem)
        local.start()
        return local, self.net.copy(src.at[theirs], dst.at[self.lo], self.net.pair(1 - self.lo))

    def start_encoded(self):
        self.swaps.append(self.pair(self.encoded, self.out, self.sems.at[0]))

    def start(self):
        w, net = self.window, self.net
        self.c = Batch(net, self.back)
        self.c.send(w.at[pl.ds(0, HALO)], self.back.at[0], net.ring("x", 3))
        self.c.send(w.at[pl.ds(HALO + OWN, HALO)], self.back.at[1], net.ring("x", 1))

    def total(self):
        self.c.wait_recv()
        rest = OWN - HALO
        own = pl.ds(HALO, OWN)
        y = self.window[own, :].astype(F32)
        low = y[:rest] + self.back[1, :rest].astype(F32)
        mid = y[rest:HALO] + self.back[1, rest:].astype(F32) + self.back[0, : HALO - rest].astype(F32)
        high = y[HALO:] + self.back[0, HALO - rest :].astype(F32)
        self.window[own, :] = jnp.concatenate([low, mid, high], axis=0).astype(BF)
        self.swaps.append(self.pair(self.window.at[own], self.token_grad, self.sems.at[1]))

    def done(self):
        for local, moved in self.swaps:
            local.wait()
            moved.wait_recv()


class Stream:
    SLOTS = 4

    def __init__(self, full, ring, sems):
        wq, wk, wv, wo, wi, wu = full
        self.ring = ring
        self.moves = []
        for n in range(12):
            slot = ring.at[n % self.SLOTS]
            if n < 4:
                pairs = [(wu.at[n], slot)]
            elif n < 8:
                pairs = [
                    (wi.at[n - 4, :, :, :, :, pl.ds(1024 * j, 1024)], slot.at[:, :, :, pl.ds(16 * j, 16)])
                    for j in range(4)
                ]
            else:
                w = (wo, wk, wv, wq)[n - 8]
                pairs = [(w.at[x], slot.at[:, :, :, pl.ds(16 * x, 16)]) for x in range(4)]
            self.moves.append([pltpu.make_async_copy(s, d, sems.at[4 * (n % self.SLOTS) + j]) for j, (s, d) in enumerate(pairs)])

    def start(self, n):
        for move in self.moves[n]:
            move.start()

    def wait(self, n):
        for move in self.moves[n]:
            move.wait()

    def part(self, n, j):
        return self.ring[n % self.SLOTS, :, :, :, 16 * j : 16 * j + 16].reshape(256, 1024)


class Backward:
    def __init__(self, ins, outs, scratch):
        self.weights = ins[:6]
        (self.x_in, self.q_in, self.k_in, self.v_in, self.probs_in, self.context_in, self.low_in, self.act_in) = ins[6:14]
        (self.slope_in, self.n1_in, self.inv1_in, self.d_in, self.encoded, self.vec, self.two) = ins[14:]
        self.owned, (self.out, self.token_grad, self.small) = outs[:6], outs[6:]
        take = iter(scratch)
        nxt = lambda n: [next(take) for _ in range(n)]
        (self.ring,) = nxt(1)
        self.g = nxt(6)
        self.bufs = nxt(3 * len(RECTS))
        self.x, self.q, self.k, self.v, self.context, self.act, self.inner, self.n1, self.inv1, self.d = nxt(10)
        self.outer, self.outer_sib, self.inner_sib, self.branch, self.branch_sib, self.d_context = nxt(6)
        self.dq, self.dk, self.dv, self.dq_sib, self.dk_sib, self.dv_sib, self.dx, self.back = nxt(8)
        self.kept, self.low_t = nxt(2)
        self.total, *vector_bufs = nxt(8)
        self.finals, self.ends = nxt(6), nxt(6)
        send_sem, recv_sem, self.local_sem = nxt(3)
        self.net = Net(send_sem, recv_sem)
        self.c = self.net.me["c"]
        self.loads = 0
        self.swaps = []
        self.stream = Stream(self.weights, self.ring, self.local_sem.at[pl.ds(0, 16)])
        self.vectors = VectorSum(self.net, self.total, vector_bufs)
        self.back_rows = Return(
            self.net, self.dx, self.kept, self.back, self.out, self.token_grad, self.local_sem.at[pl.ds(16, 2)]
        )
        lanes = []
        for n, (w, (r0, rows), (base, width), order) in enumerate(RECTS):
            lanes.append(
                Reduce(
                    self.net,
                    self.g[w],
                    pl.ds(r0, rows),
                    pl.ds(base, width),
                    BIG_FIRST[order],
                    self.bufs[3 * n : 3 * n + 3],
                )
            )
        self.lanes = lanes

    def load(self, src, dst):
        move = pltpu.make_async_copy(src, dst, self.local_sem.at[18 + self.loads])
        self.loads += 1
        move.start()
        return move

    def half(self, which, width):
        return columns(which * width, width)

    def share(self, src, dst, width):
        return self.net.copy(src.at[:, self.half(1 - self.c, width)], dst, self.net.ring("c", 0))

    def begin(self):
        self.greeted = self.net.greet()
        at_d = self.load(self.d_in, self.d)
        self.at_act = self.load(self.act_in, self.act)
        self.total[...] = jnp.zeros((16, D), F32)
        self.total[G2 : G2 + 2, :] = self.two[0:2, :]
        at_d.wait()

        def body(t, carry):
            r = some_rows(t)
            low = self.d[r, :].astype(BF)
            self.outer[r, :] = low
            return carry + jnp.sum(low.astype(F32).reshape(ROWS // 8, 8, D), axis=0)

        s = lax.fori_loop(0, OWN // ROWS, body, jnp.zeros((8, D), F32), unroll=2)
        self.total[BU : BU + 1, :] = jnp.sum(s, axis=0, keepdims=True)

    def load_all(self):
        self.at_slope = self.load(self.slope_in, self.inner)
        for n in range(4):
            self.stream.start(n)
        self.at_low = [self.load(self.low_in.at[n], self.dx.at[pl.ds(OWN * n, OWN)]) for n in range(2)]
        self.at_n1 = [self.load(self.n1_in, self.n1), self.load(self.inv1_in, self.inv1)]
        self.at_kept = self.load(self.encoded, self.kept)
        self.at_rest = [
            self.load(self.context_in, self.context),
            self.load(self.x_in, self.x),
            self.load(self.q_in, self.q),
            self.load(self.k_in, self.k),
            self.load(self.v_in, self.v),
        ]

    def meet(self):
        self.greeted()
        self.got_outer = self.share(self.outer, self.outer_sib, 512)

    def d_inner(self):
        self.at_slope.wait()
        for n in range(4):
            self.stream.wait(n)

            cols = slice(1024 * n, 1024 * n + 1024)
            y = mm(self.outer[...], self.ring[n].reshape(1024, 1024), NT)
            y = (y * self.inner[:, cols].astype(F32)).astype(BF)
            self.inner[:, cols] = y
            s = column_sum(y)
            for dp in (2 * n, 2 * n + 1):
                for t in range(4):
                    at = 512 * (dp - 2 * n) + 128 * t
                    self.total[8 + t : 9 + t, 128 * dp : 128 * dp + 128] = s[:, at : at + 128]
            self.stream.start(n + 4)

    def share_inner(self):
        self.got_inner = self.share(self.inner, self.inner_sib, 2048)

    def grad_outer(self):
        self.at_act.wait()
        self.got_outer.wait_recv()
        c = self.c
        mine = self.outer.at[:, self.half(c, 512)]

        def body(t, carry):
            cols = columns(t * 1024, 1024)
            y = mm(self.act[c, :, cols], mine[...], TN) + mm(self.act[1 - c, :, cols], self.outer_sib[...], TN)
            self.g[5][t] = y.astype(BF).reshape(2, 2, 4, 64, 512)
            return carry

        lax.fori_loop(0, 4, body, 0, unroll=2)
        self.at_probs = self.load(self.probs_in, self.act)

    def d_normed(self):
        for n in range(4):
            self.stream.wait(4 + n)
            cols = slice(256 * n, 256 * n + 256)
            y = self.d[:, cols]
            for j in range(4):
                y = y + mm(self.inner[:, 1024 * j : 1024 * j + 1024], self.stream.part(4 + n, j), NT)
            self.d[:, cols] = y
            self.stream.start(8 + n)

    def turn_low(self):
        for move in self.at_low:
            move.wait()
        for j, which in enumerate((self.c, 1 - self.c)):
            rows = pl.ds(pl.multiple_of(OWN * which, OWN), OWN)
            for x in range(4):
                part = self.dx[rows, 256 * x : 256 * x + 256]
                self.low_t[256 * x : 256 * x + 256, OWN * j : OWN * j + OWN] = part.T

    def grad_inner(self):
        self.got_inner.wait_recv()
        c = self.c

        def body(t, carry):
            x, j = lax.div(t, 2), lax.rem(t, 2)
            rows, cols = pl.ds(pl.multiple_of(x * 256, 256), 256), columns(j * 1024, 1024)
            y = mm(self.low_t[rows, :OWN], self.inner[:, columns(c * 2048 + j * 1024, 1024)])
            y = y + mm(self.low_t[rows, OWN:], self.inner_sib[:, cols])
            self.g[4][x, :, :, :, :, cols] = y.astype(BF).reshape(2, 2, 4, 16, 1024)
            return carry

        lax.fori_loop(0, 8, body, 0, unroll=2)

    def norm_one(self):
        for move in self.at_n1:
            move.wait()

        def body(t, carry):
            r = some_rows(t)
            d, n = self.d[r, :], self.n1[r, :]
            da = norm_back(d * self.vec[G1 : G1 + 1, :], n, self.inv1[r, :1])
            low = da.astype(BF)
            self.d[r, :] = da
            self.branch[r, :] = low
            new = (d * n, d, low.astype(F32))
            return tuple(a + jnp.sum(b.reshape(ROWS // 8, 8, D), axis=0) for a, b in zip(carry, new))

        zero = jnp.zeros((8, D), F32)
        sums = lax.fori_loop(0, OWN // ROWS, body, (zero, zero, zero), unroll=2)
        for row, s in zip((G1, S1, BO), sums):
            self.total[row : row + 1, :] = jnp.sum(s, axis=0, keepdims=True)
        self.got_branch = self.share(self.branch, self.branch_sib, 512)

    def d_mixed(self):
        self.stream.wait(8)
        for x in range(4):
            self.d_context[:, 256 * x : 256 * x + 256] = mm(self.branch[...], self.stream.part(8, x), NT).astype(BF)

    def grad_rows(self, left, right, sib, out):
        mine = right.at[:, self.half(self.c, 512)]

        def body(x, carry):
            rows = columns(x * 256, 256)
            y = mm(left[0][:, rows], mine[...], TN) + mm(left[1][:, rows], sib[...], TN)
            out[x] = y.astype(BF).reshape(2, 2, 4, 16, 512)
            return carry

        lax.fori_loop(0, 4, body, 0, unroll=2)

    def pair(self, ref):
        return ref.at[self.c], ref.at[1 - self.c]

    def grad_output(self):
        self.got_branch.wait_recv()
        for move in self.at_rest:
            move.wait()
        self.grad_rows(self.pair(self.context), self.branch, self.branch_sib, self.g[3])

    def attend(self, first, last):
        if first == 0:
            self.at_probs.wait()
        attention_back(
            self.q,
            self.k,
            self.v,
            self.act,
            self.context.at[self.c],
            self.d_context,
            self.dq,
            self.dk,
            self.dv,
            first,
            last,
            HEADS // 4 * (1 - self.c),
        )

    def share_heads(self):
        self.got_heads = [
            self.share(self.dk, self.dk_sib, 512),
            self.share(self.dv, self.dv_sib, 512),
            self.share(self.dq, self.dq_sib, 512),
        ]

    def head_sums(self):
        self.total[BQ : BQ + 1, :] = column_sum(self.dq[...])
        self.total[BV : BV + 1, :] = column_sum(self.dv[...])
        self.vectors.start()

    def grad_key(self):
        self.got_heads[0].wait_recv()
        self.grad_rows(self.pair(self.x), self.dk, self.dk_sib, self.g[1])

    def grad_value(self):
        self.got_heads[1].wait_recv()
        self.grad_rows(self.pair(self.x), self.dv, self.dv_sib, self.g[2])

    def grad_query(self):
        self.got_heads[2].wait_recv()
        own = pl.ds(HALO, OWN)
        rows = (self.x.at[self.c, own], self.x.at[1 - self.c, own])
        self.grad_rows(rows, self.dq, self.dq_sib, self.g[0])

    def d_halo(self):
        for n in (9, 10):
            self.stream.wait(n)

        def sides(ref):
            return jnp.concatenate([ref[:HALO, :], ref[HALO + OWN :, :]], axis=0)

        for x in range(4):
            cols = slice(256 * x, 256 * x + 256)
            y = mm(sides(self.dk), self.stream.part(9, x), NT) + mm(sides(self.dv), self.stream.part(10, x), NT)
            self.dx[:HALO, cols] = y[:HALO].astype(BF)
            self.dx[HALO + OWN :, cols] = y[HALO:].astype(BF)
        self.back_rows.start()

    def d_own(self):
        self.stream.wait(11)
        own = slice(HALO, HALO + OWN)
        for x in range(4):
            cols = slice(256 * x, 256 * x + 256)
            y = mm(self.dk[own, :], self.stream.part(9, x), NT) + mm(self.dv[own, :], self.stream.part(10, x), NT)
            y = y + self.d[:, cols] + mm(self.dq[...], self.stream.part(11, x), NT)
            self.dx[own, cols] = y.astype(BF)

    def encoded_out(self):
        self.at_kept.wait()
        self.back_rows.start_encoded()

    def rows_back(self):
        self.back_rows.total()

    def final(self, *weights):
        c, net = self.c, self.net
        for w in weights:
            final, end = self.finals[w], self.ends[w]
            for lane, (of, (r0, rows), (base, width), _) in zip(self.lanes, RECTS):
                if of == w:
                    final[pl.ds(r0, rows), pl.ds(base, width)] = lane.result()
            n, width = final.shape[0] // 2, final.shape[1]
            kept = final.at[pl.ds(pl.multiple_of(n * c, 8), n)]
            given = final.at[pl.ds(pl.multiple_of(n * (1 - c), 8), n)]
            self.swaps.append((w, net.copy(given, end.at[:, columns(c * width, width)], net.ring("c", 0))))
            end[:, columns(c * width, width)] = kept[...]

    def finish(self):
        self.vectors.done(self.small)
        stores = []
        for w, swap in self.swaps:
            swap.wait_recv()
            stores.append(self.load(self.ends[w], self.owned[w]))
        for store in stores:
            store.wait()
        self.back_rows.done()
        self.net.finish()


def backward_kernel(*refs):
    work = Backward(refs[:21], refs[21:30], refs[30:])
    u0, u1, u2, i0, i1, i2, o, q, k, v = work.lanes
    work.begin()
    work.meet()
    work.load_all()
    work.grad_outer()
    u0.p1()
    u1.p1()
    u2.p1()
    work.d_inner()
    work.share_inner()
    work.encoded_out()
    work.d_normed()
    u0.p1_mid()
    u1.p1_mid()
    u2.p1_mid()
    work.norm_one()
    work.turn_low()
    work.d_mixed()
    work.grad_inner()
    i0.p1()
    i1.p1()
    i2.p1()
    work.grad_output()
    o.p1()
    work.attend(0, 2)
    work.attend(2, 4)
    i0.p1_mid()
    i1.p1_mid()
    i2.p1_mid()
    work.share_heads()
    work.attend(4, 6)
    o.p1_mid()
    u0.p2_ring()
    u1.p2_ring()
    u2.p2_ring()
    work.attend(6, 8)
    work.head_sums()
    work.d_halo()
    u0.p2_mid()
    u1.p2_mid()
    u2.p2_mid()
    work.grad_key()
    k.p1()
    work.grad_value()
    v.p1()
    work.grad_query()
    q.p1()
    work.d_own()
    work.vectors.along_x()
    i0.p2()
    i1.p2()
    i2.p2()
    k.p1_mid()
    v.p1_mid()
    q.p1_mid()
    u0.p3()
    u1.p3()
    u2.p3()
    work.vectors.along_y()
    o.p2()
    work.rows_back()
    i0.p3()
    i1.p3()
    i2.p3()
    work.vectors.along_z()
    k.p2()
    v.p2()
    q.p2()
    work.final(5)
    o.p3()
    work.final(4)
    k.p3()
    v.p3()
    q.p3()
    work.final(3, 1, 2, 0)
    work.finish()


def backward_all(kept):
    any_space = pl.BlockSpec(memory_space=pl.ANY)
    vmem = pl.BlockSpec(memory_space=pltpu.VMEM)
    owned = [(r // 2, n) for r, n in BLOCKS]
    scratch = [((4, 2, 2, 4, 64, 1024), BF)]
    scratch += [(CHIPS + (r, n // 2), BF) for r, n in BLOCKS]
    scratch += [(s, BF) for s in reduce_buffers()]
    scratch += [((2, WIN, D), BF), ((OWN, D), BF), ((WIN, D), BF), ((WIN, D), BF), ((2, OWN, D), BF)]
    scratch += [((2, OWN, FF), BF), ((OWN, FF), BF), ((OWN, D), F32), ((OWN, 128), F32), ((OWN, D), F32)]
    scratch += [((OWN, D), BF), ((OWN, 512), BF), ((OWN, 2048), BF), ((OWN, D), BF), ((OWN, 512), BF), ((OWN, D), BF)]
    scratch += [((OWN, D), BF), ((WIN, D), BF), ((WIN, D), BF), ((OWN, 512), BF), ((WIN, 512), BF), ((WIN, 512), BF)]
    scratch += [((WIN, D), BF), ((2, HALO, D), BF), ((OWN, D), BF), ((D, 2 * OWN), BF)]
    scratch += [((16, D), F32), ((16, D), F32), ((16, D), F32), ((3, 16, 256), F32), ((2, 16, 128), F32), ((3, 16, 128), F32)]
    scratch += [((16, 128), F32), ((3, 16, 128), F32)]
    scratch += [((r, n // 2), F32) for r, n in BLOCKS] + [(s, F32) for s in owned]
    return pl.pallas_call(
        backward_kernel,
        name="backward_all",
        out_shape=[jax.ShapeDtypeStruct(s, F32) for s in owned]
        + [jax.ShapeDtypeStruct((2, TOK, D), BF)] * 2
        + [jax.ShapeDtypeStruct((8, 128), F32)],
        in_specs=[any_space] * 19 + [vmem] * 2,
        out_specs=[any_space] * 8 + [vmem],
        scratch_shapes=[pltpu.VMEM(s, t) for s, t in scratch]
        + [
            pltpu.SemaphoreType.DMA((62,)),
            pltpu.SemaphoreType.DMA((62,)),
            pltpu.SemaphoreType.DMA((40,)),
        ],
        compiler_params=pltpu.CompilerParams(collective_id=2, has_side_effects=True, vmem_limit_bytes=63 << 20),
    )(*kept)


def keep_kernel(*refs):
    (sums, *ins), outs = refs[:9], refs[9:]
    for src, dst in zip(ins, outs):
        dst[...] = src[...]
    for j, dst in enumerate(outs[8:]):
        dst[...] = sums[0:1, 8 * j : 8 * j + dst.shape[1]]


def keep(sums, *arrays):
    shapes = [(a.shape, a.dtype) for a in arrays] + [((1, 8), F32)] * 8 + [((1, 32), F32)]
    return pl.pallas_call(
        keep_kernel,
        name="keep",
        out_shape=[jax.ShapeDtypeStruct(s, t) for s, t in shapes],
        in_specs=[pl.BlockSpec(memory_space=pltpu.VMEM)] * 9,
        out_specs=[pl.BlockSpec(memory_space=pltpu.VMEM)] * 17,
    )(sums, *arrays)


def local(
    tokens, cotangent, seq_lengths, block_offsets, deal_order, wq, wk, wv, wo, bq, bv, bo, g1, s1, wi, bi, wu, bu, g2, s2
):
    small = [v[None] for v in (bq, bv, bo, g1, s1, bu, g2, s2, bi)]
    kept = forward_all(
        tokens[:, 0], cotangent[:, 0], seq_lengths[:, 0], deal_order[:, 0], (wq, wk, wv, wo, wi, wu), small
    )
    *owned, out, token_grad, sums = backward_all(kept)
    results = keep(sums, *owned, out, token_grad)
    owned, (out, token_grad), vectors = results[:6], results[6:8], results[8:]
    sbq, sbv, sbo, sg1, ss1, sbu, sg2, ss2, sbi = [v[0] for v in vectors]
    return (
        out[:, None],
        token_grad[:, None],
        *owned[:4],
        sbq,
        sbv,
        sbo,
        sg1,
        ss1,
        owned[4],
        sbi,
        owned[5],
        sbu,
        sg2,
        ss2,
    )


def solution(mesh):
    rows = P(None, "shard", "dp", None)
    table = P(None, "shard", None)
    matrix, vector = P(("dp", "shard"), None), P(("dp", "shard"))
    in_specs = (rows, rows) + (table,) * 3 + (matrix,) * 4 + (vector,) * 5 + (matrix, vector, matrix) + (vector,) * 3
    out_specs = (rows, rows) + (matrix,) * 4 + (vector,) * 5 + (matrix, vector, matrix) + (vector,) * 3
    return jax.shard_map(local, mesh=mesh, in_specs=in_specs, out_specs=out_specs, check_vma=False)
```
